32 devices in a mesh: seq: 8 (over y, x, core), rec: 4 (over z).
Axes of the slice: x: 2, y: 2, z: 4, core: 2. Of those that a mesh axis runs over, the one named last changes fastest.
Arguments:
- features: bfloat16 [16, 8192, 80], P('rec', 'seq'), may hold values from -16 to 16, as said below
- time_keep: int32 [16, 8192], P('rec', 'seq'), may hold values 0 or 1
- freq_keep: int32 [16, 80], P('rec'), may hold values 0 or 1
- block_flags: int32 [16, 8], P('rec'), may hold values from 0 to 1, as said below
- decays: float32 [16, 8, 2048], P('rec', None, 'seq'), may hold values from 0.5 to 1, as said below
- w_sub: bfloat16 [512, 320], replicated, may hold values from -0.3125 to 0.3125
- ln1_gain: float32 [512], replicated, may hold values from 0.25 to 1.75
- ffn1_in: bfloat16 [512, 2048], replicated, may hold values from -0.25 to 0.25
- ffn1_out: bfloat16 [2048, 512], replicated, may hold values from -0.125 to 0.125
- ln2_gain: float32 [512], replicated, may hold values from 0.25 to 1.75
- ssm_in: bfloat16 [512, 1536], replicated, may hold values from -0.25 to 0.25
- ssm_out: bfloat16 [512, 512], replicated, may hold values from -0.25 to 0.25
- ln3_gain: float32 [512], replicated, may hold values from 0.25 to 1.75
- conv_in: bfloat16 [512, 1024], replicated, may hold values from -0.25 to 0.25
- conv_depth: float32 [512, 15], replicated, may hold values from -1.5 to 1.5
- bn_gain: float32 [512], replicated, may hold values from 0.25 to 1.75
- bn_shift: float32 [512], replicated, may hold values from -3 to 3
- conv_out: bfloat16 [512, 512], replicated, may hold values from -0.25 to 0.25
- ln4_gain: float32 [512], replicated, may hold values from 0.25 to 1.75
- ffn2_in: bfloat16 [512, 2048], replicated, may hold values from -0.25 to 0.25
- ffn2_out: bfloat16 [2048, 512], replicated, may hold values from -0.125 to 0.125
- ln5_gain: float32 [512], replicated, may hold values from 0.25 to 1.75
- out_grad: bfloat16 [16, 2048, 512], P('rec', 'seq'), may hold values from -6 to 6
Outputs:
- output: bfloat16 [16, 2048, 512], P('rec', 'seq')
- features_grad: float32 [16, 8192, 80], P('rec', 'seq')
- w_sub_grad: float32 [512, 320], P('seq')
- ln1_gain_grad: float32 [512], P('seq')
- ffn1_in_grad: float32 [512, 2048], P('seq')
- ffn1_out_grad: float32 [2048, 512], P('seq')
- ln2_gain_grad: float32 [512], P('seq')
- ssm_in_grad: float32 [512, 1536], P('seq')
- ssm_out_grad: float32 [512, 512], P('seq')
- ln3_gain_grad: float32 [512], P('seq')
- conv_in_grad: float32 [512, 1024], P('seq')
- conv_depth_grad: float32 [512, 15], P('seq')
- bn_gain_grad: float32 [512], P('seq')
- bn_shift_grad: float32 [512], P('seq')
- conv_out_grad: float32 [512, 512], P('seq')
- ln4_gain_grad: float32 [512], P('seq')
- ffn2_in_grad: float32 [512, 2048], P('seq')
- ffn2_out_grad: float32 [2048, 512], P('seq')
- ln5_gain_grad: float32 [512], P('seq')
The draws below stay inside these ranges and needn't reach their ends.
Inputs may be any that keep to these rules, and one draw needn't show every extreme that they name: `features`: entries are the input frames with a ramp along time; all finite. decays[r, h, t] is the factor by which head h of row r keeps its state at frame t; strictly below 1. block_flags[r, 0] is 1 in every row; after block 0 a 1 stands only at blocks whose number is a multiple of 4; in every draw some row has no 1 after block 0.
All inputs are finite; a program needn't handle non-finite values. No bound on the sum of `time_keep` or of `freq_keep` on one device may be relied on, other than what follows from the above.
Results may differ from the reference program's by a relative error of at most 0.012.
Values sent between devices are 32-bit elements; how exact they have to be, the bound alone decides.
No kernel may reach another device: no remote copies, remote signals or barrier semaphores. Data moves between devices by JAX's collectives and lax.ppermute only.
A program may use at most 256 MiB of HBM per device.

```python
import jax
import jax.numpy as jnp
from jax import lax

D = 512
FF = 2048
HEADS = 8
STATE = 32
MELS = 80
SUB = 4
KERNEL = 15
T_DEV = 256
HEADP = 64
PROJ = 1536
FRAMES_PER_LINE = 2048
UTTERANCE_COUNT = 16
FRAMES = 8192
N_SEQ = 8


def draw_features(key, part):
    noise_key, pattern_key = jax.random.split(jax.random.fold_in(key, 11))
    ramp_line = 2.5 * jnp.arange(FRAMES, dtype=jnp.float32) / FRAMES
    noise_part = jax.random.normal(noise_key, (UTTERANCE_COUNT, FRAMES, MELS), jnp.float32)
    pattern = jax.random.normal(pattern_key, (UTTERANCE_COUNT, 1, MELS), jnp.float32)
    attention_contents = jnp.clip(noise_part + ramp_line[None, :, None] * pattern, -16.0, 16.0)
    return attention_contents.astype(jnp.bfloat16)


def draw_decays(key, part):
    generator_seeds = jax.random.split(jax.random.fold_in(key, 23), 7)
    head_order = jax.random.permutation(generator_seeds[0], HEADS)
    slow_heads = head_order < HEADS // 2
    slow_rate = jnp.exp(jax.random.uniform(generator_seeds[1], (UTTERANCE_COUNT, HEADS, 1), jnp.float32, -2.3, -0.2)) / FRAMES_PER_LINE
    fast_rate = jnp.exp(jax.random.uniform(generator_seeds[2], (UTTERANCE_COUNT, HEADS, 1), jnp.float32, -3.912, -3.401))
    base_rate = jnp.where(slow_heads[None, :, None], slow_rate, fast_rate)
    block_total = FRAMES_PER_LINE // T_DEV
    block_factor = jnp.exp(jax.random.uniform(generator_seeds[3], (UTTERANCE_COUNT, HEADS, block_total, 1), jnp.float32, -0.35, 0.35))
    block_factor = (block_factor * jnp.ones((1, 1, 1, T_DEV), jnp.float32)).reshape(UTTERANCE_COUNT, HEADS, FRAMES_PER_LINE)
    frame_factor = jax.random.uniform(generator_seeds[4], (UTTERANCE_COUNT, HEADS, FRAMES_PER_LINE), jnp.float32, 0.5, 1.5)
    omission_probability = base_rate * block_factor * frame_factor
    perturbation_draw = jax.random.uniform(generator_seeds[5], (UTTERANCE_COUNT, 1, FRAMES_PER_LINE), jnp.float32) < 2.0 / FRAMES_PER_LINE
    omitted_fraction = jax.random.uniform(generator_seeds[6], (UTTERANCE_COUNT, 1, FRAMES_PER_LINE), jnp.float32, 0.6, 0.85)
    return jnp.where(perturbation_draw, omitted_fraction, 1.0) * jnp.exp(-omission_probability)


def draw_block_flags(key, part):
    bits_key, row_key = jax.random.split(jax.random.fold_in(key, 37))
    block_total = FRAMES_PER_LINE // T_DEV
    bits = jax.random.randint(bits_key, (UTTERANCE_COUNT, block_total), 0, 2)
    position = jnp.arange(block_total)[None, :]
    starts = jnp.where(position % 4 == 0, bits, 0)
    whole_row = jax.random.randint(row_key, (), 0, UTTERANCE_COUNT)
    row_ids = jnp.arange(UTTERANCE_COUNT)[:, None]
    starts = jnp.where(row_ids == whole_row, 0, starts)
    return jnp.where(position == 0, 1, starts).astype(jnp.int32)


def place_ends(entries, stream_key, low, top_value):
    spot = [jax.random.randint(jax.random.fold_in(stream_key, axis), (), 0, length) for axis, length in enumerate(entries.shape)]
    main_axis = entries.shape.index(max(entries.shape))
    next_to = spot[:main_axis] + [(spot[main_axis] + 1) % entries.shape[main_axis]] + spot[main_axis + 1:]
    return entries.at[tuple(spot)].set(low).at[tuple(next_to)].set(top_value)


def block_scale(own_key, dims, shards, low, largest):
    gain = 1.0
    for axis_at, shards_of in shards:
        steps = jax.random.uniform(jax.random.fold_in(jax.random.fold_in(own_key, 6), axis_at), (shards_of,), jnp.float32, low / len(shards), largest / len(shards))
        gain = gain * jnp.repeat(jnp.exp(steps), dims[axis_at] // shards_of).reshape((-1,) + (1,) * (len(dims) - 1 - axis_at))
    return gain


def bell_draw(stream_key, shape, width, bound, cuts=(), kind=jnp.bfloat16):
    loudness = block_scale(stream_key, shape, cuts, -0.22, 0.18) if cuts else 1.0
    drawn = jax.random.normal(stream_key, shape, jnp.float32) * width * loudness
    return jnp.minimum(jnp.maximum(drawn, -bound), bound).astype(kind)


def setup_inputs(seed: int = 0) -> dict:
    key_list = jax.random.split(jax.random.key(seed), 24)
    features = draw_features(jax.random.fold_in(key_list[23], 71), 0)
    time_keep = place_ends((jax.random.randint(key_list[1], (UTTERANCE_COUNT, FRAMES), 0, 6) < 5).astype(jnp.int32), jax.random.fold_in(key_list[1], 1), 0, 1)
    freq_keep = place_ends((jax.random.randint(key_list[2], (UTTERANCE_COUNT, MELS), 0, 8) < 7).astype(jnp.int32), jax.random.fold_in(key_list[2], 1), 0, 1)
    block_flags = draw_block_flags(jax.random.fold_in(key_list[23], 71), 0)
    decays = draw_decays(jax.random.fold_in(key_list[23], 71), 0)
    w_sub = bell_draw(key_list[5], (D, SUB * MELS), (SUB * MELS) ** -0.5, 0.3125)
    ln1_gain = jnp.clip(1.0 + 0.15 * jax.random.normal(key_list[6], (D,), jnp.float32), 0.25, 1.75)
    ffn1_in = bell_draw(key_list[7], (D, FF), D ** -0.5, 0.25)
    ffn1_out = bell_draw(key_list[8], (FF, D), FF ** -0.5, 0.125)
    ln2_gain = jnp.clip(1.0 + 0.15 * jax.random.normal(key_list[9], (D,), jnp.float32), 0.25, 1.75)
    ssm_in = bell_draw(key_list[10], (D, PROJ), D ** -0.5, 0.25)
    ssm_out = bell_draw(key_list[11], (D, D), D ** -0.5, 0.25)
    ln3_gain = jnp.clip(1.0 + 0.15 * jax.random.normal(key_list[12], (D,), jnp.float32), 0.25, 1.75)
    conv_in = bell_draw(key_list[13], (D, 2 * D), D ** -0.5, 0.25)
    conv_depth = bell_draw(key_list[14], (D, KERNEL), KERNEL ** -0.5, 1.5, (), jnp.float32)
    bn_gain = jnp.clip(1.0 + 0.15 * jax.random.normal(key_list[15], (D,), jnp.float32), 0.25, 1.75)
    bn_shift = bell_draw(key_list[16], (D,), 0.5, 3.0, (), jnp.float32)
    conv_out = bell_draw(key_list[17], (D, D), D ** -0.5, 0.25)
    ln4_gain = jnp.clip(1.0 + 0.15 * jax.random.normal(key_list[18], (D,), jnp.float32), 0.25, 1.75)
    ffn2_in = bell_draw(key_list[19], (D, FF), D ** -0.5, 0.25)
    ffn2_out = bell_draw(key_list[20], (FF, D), FF ** -0.5, 0.125)
    ln5_gain = jnp.clip(1.0 + 0.15 * jax.random.normal(key_list[21], (D,), jnp.float32), 0.25, 1.75)
    out_grad = bell_draw(key_list[22], (UTTERANCE_COUNT, FRAMES_PER_LINE, D), 1.0, 6.0, ((0, 4), (1, 8)))
    return {"features": features, "time_keep": time_keep, "freq_keep": freq_keep, "block_flags": block_flags, "decays": decays, "w_sub": w_sub, "ln1_gain": ln1_gain, "ffn1_in": ffn1_in, "ffn1_out": ffn1_out, "ln2_gain": ln2_gain, "ssm_in": ssm_in, "ssm_out": ssm_out, "ln3_gain": ln3_gain, "conv_in": conv_in, "conv_depth": conv_depth, "bn_gain": bn_gain, "bn_shift": bn_shift, "conv_out": conv_out, "ln4_gain": ln4_gain, "ffn2_in": ffn2_in, "ffn2_out": ffn2_out, "ln5_gain": ln5_gain, "out_grad": out_grad}


@jax.custom_vjp
def low(v):
    return lax.optimization_barrier(v.astype(jnp.bfloat16)).astype(jnp.float32)

@jax.custom_vjp
def low_back(v):
    return v

def low_keep(v):
    return (low(v), None)

def low_pass(kept, grad):
    return (grad,)

def back_keep(v):
    return (v, None)

def back_low(kept, grad):
    return (low(grad),)
low.defvjp(low_keep, low_pass)
low_back.defvjp(back_keep, back_low)
norm_eps = 1e-05
batch_eps = 1e-05

def product(matrix_a, matrix_b):
    return jnp.dot(matrix_a, matrix_b, precision=lax.Precision.HIGHEST, preferred_element_type=jnp.float32)

def contract(formula, tensor_a, tensor_b):
    return jnp.einsum(formula, tensor_a, tensor_b, precision=lax.Precision.HIGHEST)

def layer_norm(signal, norm_gain):
    centred = signal - lax.optimization_barrier(jnp.mean(signal, axis=-1, keepdims=True))
    spread = lax.optimization_barrier(jnp.mean(centred * centred, axis=-1, keepdims=True))
    return centred * lax.rsqrt(spread + norm_eps) * norm_gain

def feed_forward(signal, norm_gain, weight_in, weight_out):
    standardized_input = low(layer_norm(signal, norm_gain))
    hidden = low_back(product(standardized_input, weight_in))
    active = low(jax.nn.silu(hidden))
    return low_back(product(active, weight_out))

def block_step(carried, pieces):
    attention_contents, keys_in, read_vecs, log_decay, keep_flag = pieces
    start_state = carried * keep_flag
    cumulative = jnp.cumsum(log_decay, axis=1)
    length = log_decay.shape[1]
    causal = jnp.arange(length)[:, None] >= jnp.arange(length)[None, :]
    spread = cumulative[:, :, None] - cumulative[:, None, :]
    weights = jnp.where(causal, jnp.exp(jnp.where(causal, spread, 0.0)), 0.0)
    scores = contract('htn,hsn->hts', read_vecs, keys_in) * weights
    mixed_out = contract('hts,hsp->htp', scores, attention_contents)
    mixed_out = mixed_out + contract('htn,hnp->htp', read_vecs * jnp.exp(cumulative)[:, :, None], start_state)
    tail_weight = jnp.exp(cumulative[:, -1:] - cumulative)
    end_state = jnp.exp(cumulative[:, -1])[:, None, None] * start_state
    end_state = end_state + contract('hsn,hsp->hnp', keys_in * tail_weight[:, :, None], attention_contents)
    return (end_state, mixed_out)

def state_space(signal, norm_gain, weight_in, weight_out, decay_row, block_keep):
    standardized_input = low(layer_norm(signal, norm_gain))
    projected = low_back(product(standardized_input, weight_in))
    width_bc = HEADS * STATE
    attention_contents = projected[:, :D].reshape(FRAMES_PER_LINE, HEADS, HEADP).transpose(1, 0, 2)
    gate_in = projected[:, D:2 * D]
    keys_in = projected[:, 2 * D:2 * D + width_bc].reshape(FRAMES_PER_LINE, HEADS, STATE).transpose(1, 0, 2)
    read_vecs = projected[:, 2 * D + width_bc:].reshape(FRAMES_PER_LINE, HEADS, STATE).transpose(1, 0, 2)
    log_decay = jnp.log(decay_row)
    keys_in = keys_in * jnp.sqrt(-2.0 * log_decay)[:, :, None]

    def by_block(tensor):
        shaped = tensor.reshape((HEADS, N_SEQ, T_DEV) + tensor.shape[2:])
        return jnp.moveaxis(shaped, 1, 0)
    initial = jnp.zeros((HEADS, STATE, HEADP), jnp.float32)
    final_state, outputs = lax.scan(jax.checkpoint(block_step), initial, (by_block(attention_contents), by_block(keys_in), by_block(read_vecs), by_block(log_decay), block_keep))
    mixed_out = jnp.moveaxis(outputs, 0, 1).reshape(HEADS, FRAMES_PER_LINE, HEADP).transpose(1, 0, 2).reshape(FRAMES_PER_LINE, D)
    gated = low(mixed_out * STATE ** (-0.5) * jax.nn.silu(gate_in))
    return low_back(product(gated, weight_out))

def depthwise(signal, depth_weight, segment):
    half_span = KERNEL // 2
    padded = jnp.pad(signal, ((half_span, half_span), (0, 0)))
    segment_pad = jnp.pad(segment, (half_span, half_span), constant_values=-1)
    running = jnp.zeros_like(signal)
    for offset in range(KERNEL):
        same_rec = (segment_pad[offset:offset + FRAMES_PER_LINE] == segment)[:, None]
        running = running + jnp.where(same_rec, padded[offset:offset + FRAMES_PER_LINE], 0.0) * depth_weight[:, offset]
    return running

def reference(features, time_keep, freq_keep, block_flags, decays, w_sub, ln1_gain, ffn1_in, ffn1_out, ln2_gain, ssm_in, ssm_out, ln3_gain, conv_in, conv_depth, bn_gain, bn_shift, conv_out, ln4_gain, ffn2_in, ffn2_out, ln5_gain, out_grad):
    keep_mask = (time_keep[:, :, None] * freq_keep[:, None, :]).astype(jnp.float32)
    segment_ids = jnp.repeat(jnp.cumsum(block_flags, axis=1).astype(jnp.int32), T_DEV, axis=1).astype(jnp.int32)
    block_keep = (1 - block_flags).astype(jnp.float32)
    params = (w_sub.astype(jnp.float32), ln1_gain, ffn1_in.astype(jnp.float32), ffn1_out.astype(jnp.float32), ln2_gain, ssm_in.astype(jnp.float32), ssm_out.astype(jnp.float32), ln3_gain, conv_in.astype(jnp.float32), conv_depth, bn_gain, bn_shift, conv_out.astype(jnp.float32), ln4_gain, ffn2_in.astype(jnp.float32), ffn2_out.astype(jnp.float32), ln5_gain)

    def forward(features_f, params_f):
        sub_w, gain_one, one_in, one_out, gain_two, mix_in, mix_out, gain_three, lift_w, depth_w, batch_gain, batch_shift, drop_w, gain_four, two_in, two_out, gain_five = params_f

        def front(row_data):
            feature_row, keep_row, segment_row, decay_row, keep_blocks = row_data
            masked = (feature_row * keep_row).reshape(FRAMES_PER_LINE, SUB * MELS)
            layer_in = low_back(product(masked, sub_w.T))
            after_ffn = layer_in + 0.5 * feed_forward(layer_in, gain_one, one_in, one_out)
            after_ssm = after_ffn + state_space(after_ffn, gain_two, mix_in, mix_out, decay_row, keep_blocks)
            standardized_input = low(layer_norm(after_ssm, gain_three))
            lifted = low_back(product(standardized_input, lift_w))
            glu_out = lifted[:, :D] * jax.nn.sigmoid(lifted[:, D:])
            return (after_ssm, depthwise(glu_out, depth_w, segment_row))
        ssm_all, depth_all = lax.map(jax.checkpoint(front), (features_f, keep_mask, segment_ids, decays, block_keep))
        batch_mean = lax.optimization_barrier(jnp.mean(depth_all, axis=(0, 1)))
        batch_square = lax.optimization_barrier(jnp.mean(depth_all * depth_all, axis=(0, 1)))
        batch_inv = lax.rsqrt(batch_square - batch_mean * batch_mean + batch_eps)

        def back(row_data):
            after_ssm, depth_row = row_data
            batch_out = (depth_row - batch_mean) * batch_inv * batch_gain + batch_shift
            active = low(jax.nn.silu(batch_out))
            after_conv = after_ssm + low_back(product(active, drop_w))
            after_late = after_conv + 0.5 * feed_forward(after_conv, gain_four, two_in, two_out)
            return layer_norm(after_late, gain_five)
        return lax.map(jax.checkpoint(back), (ssm_all, depth_all))
    result, pullback = jax.vjp(forward, features.astype(jnp.float32), params)
    features_grad, grads = pullback(out_grad.astype(jnp.float32))
    g_sub, g_ln1, g_ffn1_in, g_ffn1_out, g_ln2, g_ssm_in, g_ssm_out, g_ln3, g_conv_in, g_depth, g_bn_gain, g_bn_shift, g_conv_out, g_ln4, g_ffn2_in, g_ffn2_out, g_ln5 = grads
    return (result.astype(jnp.bfloat16), features_grad, g_sub, g_ln1, g_ffn1_in, g_ffn1_out, g_ln2, g_ssm_in, g_ssm_out, g_ln3, g_conv_in, g_depth, g_bn_gain, g_bn_shift, g_conv_out, g_ln4, g_ffn2_in, g_ffn2_out, g_ln5)
```

```python
import jax
import jax.numpy as jnp
from jax import lax
from jax.sharding import PartitionSpec as P

D = 512
HEADS = 8
STATE = 32
SUB = 4
KERNEL = 15
HEADP = 64


norm_eps = 1e-05
batch_eps = 1e-05
highest = lax.Precision.HIGHEST


def flip_pairs(count, mask):
    return [(i, i ^ mask) for i in range(count)]


def entering(decay, state, backward):
    count, mine = lax.axis_size("seq"), lax.axis_index("seq")
    before_decay, before_state = jnp.ones_like(decay), jnp.zeros_like(state)
    mask = 1
    while mask < count:
        pairs = flip_pairs(count, mask)
        other_decay = lax.ppermute(decay, "seq", pairs)
        other_state = lax.ppermute(state, "seq", pairs)
        second = ((mine & mask) != 0) != backward
        wide, other_wide = decay[:, :, None, None], other_decay[:, :, None, None]
        before_state = jnp.where(
            second, before_decay[:, :, None, None] * other_state + before_state, before_state
        )
        before_decay = jnp.where(second, before_decay * other_decay, before_decay)
        state = jnp.where(
            second, wide * other_state + state, other_wide * state + other_state
        )
        decay = decay * other_decay
        mask *= 2
    return before_state


def sum_over_all(value):
    count = lax.axis_size("seq") * lax.axis_size("rec")
    copies = jnp.broadcast_to(value[None], (count,) + value.shape)
    return jnp.sum(lax.all_to_all(copies, ("rec", "seq"), 0, 0), axis=0)


def halve(value, axis, bit, dim):
    place = lax.axis_index(axis)
    mine = (place >> bit) & 1
    sent = lax.dynamic_index_in_dim(value, 1 - mine, dim, keepdims=False)
    kept = lax.dynamic_index_in_dim(value, mine, dim, keepdims=False)
    return kept + lax.ppermute(sent, axis, flip_pairs(lax.axis_size(axis), 1 << bit))


def scatter_rows(value, parts):
    count = lax.axis_size("seq")
    bits = count.bit_length() - 1
    rows, columns = value.shape
    split = value.reshape((2,) * bits + (rows // count, columns))
    split = halve(split, "seq", 0, bits - 1)
    pieces = []
    half = (bits - 1) // 2
    orders = (
        list(range(1, bits)),
        list(range(1 + half, bits)) + list(range(1, 1 + half)),
    )
    start = 0
    for part, order in zip(parts, orders):
        piece = lax.slice_in_dim(split, start, start + part, axis=split.ndim - 1)
        left = list(range(bits - 1, 0, -1))
        for bit in order:
            piece = halve(piece, "seq", bit, left.index(bit))
            left.remove(bit)
        pieces.append(piece)
        start += part
    return jnp.concatenate(pieces, axis=1)


def sum_over_rec(value):
    count = lax.axis_size("rec")
    bits = count.bit_length() - 1
    rows, columns = value.shape
    piece = value.reshape(rows, count, columns // count).transpose(1, 0, 2)
    piece = piece.reshape((2,) * bits + (rows, columns // count))
    place = lax.axis_index("rec")
    for bit in range(bits):
        piece = halve(piece, "rec", bit, 0)
    piece = piece[None]
    for bit in reversed(range(bits)):
        other = lax.ppermute(piece, "rec", flip_pairs(count, 1 << bit))
        mine = (place >> bit) & 1
        low = jnp.where(mine == 0, piece, other)
        high = jnp.where(mine == 0, other, piece)
        piece = jnp.stack([low, high])
        piece = piece.reshape((-1,) + piece.shape[2:])
    order = [sum(((i >> k) & 1) << (bits - 1 - k) for k in range(bits)) for i in range(count)]
    piece = piece.reshape((2,) * bits + (rows, columns // count))
    piece = piece.reshape(count, rows, columns // count)
    piece = piece.transpose(1, 0, 2)
    return piece.reshape(rows, columns)


def extended(cells, sides, width):
    for axis, dim in sides:
        count = lax.axis_size(axis)
        ends = count - 1
        head = lax.slice_in_dim(cells, 0, width, axis=dim)
        tail = lax.slice_in_dim(cells, cells.shape[dim] - width, cells.shape[dim], axis=dim)
        cells = jnp.concatenate(
            [
                lax.ppermute(tail, axis, [(i, (i + 1) % count) for i in range(ends)]),
                cells,
                lax.ppermute(head, axis, [((i + 1) % count, i) for i in range(ends)]),
            ],
            axis=dim,
        )
    return cells


def plain_dot(matrix_a, matrix_b):
    return jnp.dot(matrix_a, matrix_b, preferred_element_type=jnp.float32)


def dot_transposed(matrix_a, matrix_b):
    return lax.dot_general(
        matrix_a, matrix_b, (((1,), (1,)), ((), ())), preferred_element_type=jnp.float32
    )


def dot_outer(matrix_a, matrix_b):
    return lax.dot_general(
        matrix_a, matrix_b, (((0,), (0,)), ((), ())), preferred_element_type=jnp.float32
    )


def contract(formula, tensor_a, tensor_b):
    return jnp.einsum(
        formula,
        tensor_a.astype(jnp.bfloat16),
        tensor_b.astype(jnp.bfloat16),
        preferred_element_type=jnp.float32,
    )


def norm_forward(signal, norm_gain):
    centred = signal - jnp.mean(signal, axis=-1, keepdims=True)
    inv_scale = lax.rsqrt(jnp.mean(centred * centred, axis=-1, keepdims=True) + norm_eps)
    unit_part = centred * inv_scale
    return (unit_part * norm_gain, (unit_part, inv_scale))


def norm_backward(incoming, saved_norm, norm_gain):
    unit_part, inv_scale = saved_norm
    scaled = incoming * norm_gain
    inner_part = (
        scaled
        - jnp.mean(scaled, axis=-1, keepdims=True)
        - unit_part * jnp.mean(scaled * unit_part, axis=-1, keepdims=True)
    )
    return (inner_part * inv_scale, jnp.sum(incoming * unit_part, axis=0))


def silu_slope(signal):
    sigmoid = jax.nn.sigmoid(signal)
    return sigmoid * (1.0 + signal * (1.0 - sigmoid))


def ffn_forward(signal, norm_gain, weight_in, weight_out):
    standardized_input, saved_norm = norm_forward(signal, norm_gain)
    lowered = standardized_input.astype(jnp.bfloat16)
    hidden = plain_dot(lowered, weight_in)
    active = jax.nn.silu(hidden).astype(jnp.bfloat16)
    return (signal + 0.5 * plain_dot(active, weight_out), (saved_norm, lowered, hidden, active))


def ffn_backward(incoming, saved_set, norm_gain, weight_in, weight_out):
    saved_norm, lowered, hidden, active = saved_set
    out_low = (0.5 * incoming).astype(jnp.bfloat16)
    out_weight_grad = dot_outer(active, out_low)
    hidden_low = (dot_transposed(out_low, weight_out) * silu_slope(hidden)).astype(jnp.bfloat16)
    in_weight_grad = dot_outer(lowered, hidden_low)
    back_part, gain_grad = norm_backward(
        dot_transposed(hidden_low, weight_in), saved_norm, norm_gain
    )
    return (incoming + back_part, gain_grad, in_weight_grad, out_weight_grad)


def depth_apply(padded, depth_weight, step_count, flipped):
    running = jnp.zeros(padded.shape[:1] + (step_count,) + padded.shape[2:], jnp.float32)
    for offset in range(KERNEL):
        first_row = KERNEL - 1 - offset if flipped else offset
        running = (
            running + padded[:, first_row : first_row + step_count, :] * depth_weight[:, offset]
        )
    return running


def local(
    features,
    time_keep,
    freq_keep,
    block_flags,
    decays,
    w_sub,
    ln1_gain,
    ffn1_in,
    ffn1_out,
    ln2_gain,
    ssm_in,
    ssm_out,
    ln3_gain,
    conv_in,
    conv_depth,
    bn_gain,
    bn_shift,
    conv_out,
    ln4_gain,
    ffn2_in,
    ffn2_out,
    ln5_gain,
    out_grad,
):
    row_count, frame_count, mel_count = features.shape
    step_count = frame_count // SUB
    token_count = row_count * step_count
    block_count = lax.axis_size("seq")
    seq_place = lax.axis_index("seq")
    device_count = block_count * lax.axis_size("rec")
    frame_total = float(token_count * device_count)
    here_start = lax.dynamic_index_in_dim(block_flags, seq_place, 1, keepdims=False)
    next_start = lax.dynamic_index_in_dim(
        block_flags, jnp.minimum(seq_place + 1, block_count - 1), 1, keepdims=False
    )
    keep_here = (1 - here_start).astype(jnp.float32)
    keep_next = jnp.where(seq_place + 1 < block_count, 1 - next_start, 0).astype(jnp.float32)
    keep_mask = time_keep[:, :, None] * freq_keep[:, None, :]
    masked = features * keep_mask.astype(jnp.bfloat16)
    flat_in = masked.reshape(token_count, SUB * mel_count)
    layer_in = dot_transposed(flat_in, w_sub)
    after_ffn, ffn1_saved = ffn_forward(layer_in, ln1_gain, ffn1_in, ffn1_out)
    normed_ssm, ssm_norm = norm_forward(after_ffn, ln2_gain)
    lowered_ssm = normed_ssm.astype(jnp.bfloat16)
    projected = plain_dot(lowered_ssm, ssm_in)
    width_bc = HEADS * STATE

    def by_head(column_block, head_width):
        return column_block.reshape(row_count, step_count, HEADS, head_width).transpose(0, 2, 1, 3)

    def by_token(head_block):
        return head_block.transpose(0, 2, 1, 3).reshape(token_count, -1)

    attention_contents = by_head(projected[:, :D], HEADP)
    gate_in = projected[:, D : 2 * D]
    read_vecs = by_head(projected[:, 2 * D + width_bc :], STATE)
    log_decay = jnp.log(decays)
    input_scale = jnp.sqrt(-2.0 * log_decay)
    keys_in = by_head(projected[:, 2 * D : 2 * D + width_bc], STATE) * input_scale[..., None]
    causal = jnp.arange(step_count)[:, None] >= jnp.arange(step_count)[None, :]
    cumulative = jnp.einsum(
        "rhs,ts->rht", log_decay, causal.astype(jnp.float32), precision=highest
    )
    weights = jnp.where(
        causal,
        jnp.exp(jnp.where(causal, cumulative[..., :, None] - cumulative[..., None, :], 0.0)),
        0.0,
    )
    head_weight = jnp.exp(cumulative)
    tail_weight = jnp.exp(cumulative[..., -1:] - cumulative)
    block_decay = keep_here[:, None] * jnp.exp(cumulative[..., -1])
    local_end = contract("rhsn,rhsp->rhnp", keys_in * tail_weight[..., None], attention_contents)
    start_state = entering(block_decay, local_end, False) * keep_here[:, None, None, None]
    scores = contract("rhtn,rhsn->rhts", read_vecs, keys_in) * weights
    reads_start = read_vecs * head_weight[..., None]
    mixed_out = contract("rhts,rhsp->rhtp", scores, attention_contents) + contract(
        "rhtn,rhnp->rhtp", reads_start, start_state
    )
    mixed_flat = by_token(mixed_out) * STATE ** (-0.5)
    gate_sig = jax.nn.sigmoid(gate_in)
    gated = (mixed_flat * gate_in * gate_sig).astype(jnp.bfloat16)
    after_ssm = after_ffn + plain_dot(gated, ssm_out)
    normed_conv, conv_norm = norm_forward(after_ssm, ln3_gain)
    lowered_conv = normed_conv.astype(jnp.bfloat16)
    lifted = plain_dot(lowered_conv, conv_in)
    lift_sig = jax.nn.sigmoid(lifted[:, D:])
    glu_out = (lifted[:, :D] * lift_sig).reshape(row_count, step_count, D)
    half_span = KERNEL // 2
    rim_pos = jnp.arange(step_count + 2 * half_span)[None, :]
    rim_keep = jnp.where(
        rim_pos < half_span,
        keep_here[:, None],
        jnp.where(rim_pos >= step_count + half_span, keep_next[:, None], 1.0),
    )[:, :, None]
    padded = extended(glu_out, (("seq", 1),), half_span) * rim_keep
    depth_out = depth_apply(padded, conv_depth, step_count, False)
    batch_statistic_sums = sum_over_all(
        jnp.stack([jnp.sum(depth_out, axis=(0, 1)), jnp.sum(depth_out * depth_out, axis=(0, 1))])
    )
    batch_mean = batch_statistic_sums[0] / frame_total
    batch_inv = lax.rsqrt(
        batch_statistic_sums[1] / frame_total - batch_mean * batch_mean + batch_eps
    )
    batch_unit = (depth_out - batch_mean) * batch_inv
    batch_out = (batch_unit * bn_gain + bn_shift).reshape(token_count, D)
    active_conv = jax.nn.silu(batch_out).astype(jnp.bfloat16)
    after_conv = after_ssm + plain_dot(active_conv, conv_out)
    after_late, ffn2_saved = ffn_forward(after_conv, ln4_gain, ffn2_in, ffn2_out)
    result, final_norm = norm_forward(after_late, ln5_gain)
    late_grad, ln5_grad = norm_backward(
        out_grad.reshape(token_count, D).astype(jnp.float32), final_norm, ln5_gain
    )
    conv_grad, ln4_grad, ffn2_in_grad, ffn2_out_grad = ffn_backward(
        late_grad, ffn2_saved, ln4_gain, ffn2_in, ffn2_out
    )
    conv_low = conv_grad.astype(jnp.bfloat16)
    conv_out_grad = dot_outer(active_conv, conv_low)
    batch_grad = (dot_transposed(conv_low, conv_out) * silu_slope(batch_out)).reshape(
        row_count, step_count, D
    )
    back_stats = sum_over_all(
        jnp.stack([jnp.sum(batch_grad * batch_unit, axis=(0, 1)), jnp.sum(batch_grad, axis=(0, 1))])
    )
    depth_grad = (
        bn_gain
        * batch_inv
        * (batch_grad - (back_stats[1] + batch_unit * back_stats[0]) / frame_total)
    )
    conv_depth_grad = jnp.stack(
        [
            jnp.sum(depth_grad * padded[:, offset : offset + step_count, :], axis=(0, 1))
            for offset in range(KERNEL)
        ],
        axis=1,
    )
    grad_padded = extended(depth_grad, (("seq", 1),), half_span) * rim_keep
    glu_grad = depth_apply(grad_padded, conv_depth, step_count, True).reshape(token_count, D)
    lifted_low = jnp.concatenate(
        [glu_grad * lift_sig, glu_grad * lifted[:, :D] * lift_sig * (1.0 - lift_sig)], axis=1
    ).astype(jnp.bfloat16)
    conv_in_grad = dot_outer(lowered_conv, lifted_low)
    conv_back, ln3_grad = norm_backward(dot_transposed(lifted_low, conv_in), conv_norm, ln3_gain)
    ssm_grad = conv_grad + conv_back
    ssm_low = ssm_grad.astype(jnp.bfloat16)
    ssm_out_grad = dot_outer(gated, ssm_low)
    gated_grad = dot_transposed(ssm_low, ssm_out)
    mixed_grad = by_head(gated_grad * gate_in * gate_sig * STATE ** (-0.5), HEADP)
    gate_grad = gated_grad * mixed_flat * silu_slope(gate_in)
    pulled = contract("rhtn,rhtp->rhnp", reads_start, mixed_grad)
    end_grad = entering(block_decay, keep_here[:, None, None, None] * pulled, True)
    paired = contract("rhtp,rhsp->rhts", mixed_grad, attention_contents) * weights
    reads_grad = contract("rhts,rhsn->rhtn", paired, keys_in) + head_weight[..., None] * contract(
        "rhtp,rhnp->rhtn", mixed_grad, start_state
    )
    values_grad = contract("rhts,rhtp->rhsp", scores, mixed_grad) + tail_weight[
        ..., None
    ] * contract("rhsn,rhnp->rhsp", keys_in, end_grad)
    keys_grad = (
        contract("rhts,rhtn->rhsn", paired, read_vecs)
        + tail_weight[..., None] * contract("rhsp,rhnp->rhsn", attention_contents, end_grad)
    ) * input_scale[..., None]
    proj_low = jnp.concatenate(
        [by_token(values_grad), gate_grad, by_token(keys_grad), by_token(reads_grad)], axis=1
    ).astype(jnp.bfloat16)
    ssm_in_grad = dot_outer(lowered_ssm, proj_low)
    ssm_back, ln2_grad = norm_backward(dot_transposed(proj_low, ssm_in), ssm_norm, ln2_gain)
    front_grad = ssm_grad + ssm_back
    entry_grad, ln1_grad, ffn1_in_grad, ffn1_out_grad = ffn_backward(
        front_grad, ffn1_saved, ln1_gain, ffn1_in, ffn1_out
    )
    entry_low = entry_grad.astype(jnp.bfloat16)
    w_sub_grad = dot_outer(entry_low, flat_in)
    features_grad = plain_dot(entry_low, w_sub).reshape(
        row_count, frame_count, mel_count
    ) * keep_mask.astype(jnp.float32)
    share_rows = D // block_count
    offset_start = seq_place * share_rows
    bn_gain_grad = lax.dynamic_slice_in_dim(back_stats[0], offset_start, share_rows)
    bn_shift_grad = lax.dynamic_slice_in_dim(back_stats[1], offset_start, share_rows)
    def by_share(grad):
        wide = grad.reshape(block_count, -1, share_rows, grad.shape[1])
        return wide.transpose(0, 2, 1, 3).reshape(D, -1)

    def from_share(block, columns):
        wide = block.reshape(share_rows, -1, columns)
        return wide.transpose(1, 0, 2).reshape(-1, columns)

    small = jnp.concatenate(
        [
            jnp.stack([ln1_grad, ln2_grad, ln3_grad, ln4_grad, ln5_grad], axis=1),
            conv_depth_grad,
            jnp.zeros((D, 44), jnp.float32),
        ],
        axis=1,
    )
    group_a = lax.psum_scatter(
        jnp.concatenate([ffn2_in_grad, by_share(ffn2_out_grad), conv_out_grad], axis=1),
        "seq",
        scatter_dimension=0,
        tiled=True,
    )
    group_b = lax.psum_scatter(
        jnp.concatenate([conv_in_grad, ssm_out_grad, ssm_in_grad], axis=1),
        "seq",
        scatter_dimension=0,
        tiled=True,
    )
    group_c = scatter_rows(
        jnp.concatenate([by_share(ffn1_out_grad), ffn1_in_grad, w_sub_grad, small], axis=1),
        (2048, 2432),
    )
    late = sum_over_rec(jnp.concatenate([group_a, group_b], axis=1))
    last = sum_over_rec(group_c)
    gains = last[:, 4416:]
    return (
        result.reshape(row_count, step_count, D).astype(jnp.bfloat16),
        features_grad,
        last[:, 4096:4416],
        gains[:, 0],
        last[:, 2048:4096],
        from_share(last[:, :2048], D),
        gains[:, 1],
        late[:, 6144:7680],
        late[:, 5632:6144],
        gains[:, 2],
        late[:, 4608:5632],
        gains[:, 5 : 5 + KERNEL],
        bn_gain_grad,
        bn_shift_grad,
        late[:, 4096:4608],
        gains[:, 3],
        late[:, :2048],
        from_share(late[:, 2048:4096], D),
        gains[:, 4],
    )


def solution(mesh):
    return jax.shard_map(
        local,
        mesh=mesh,
        in_specs=(
            P("rec", "seq", None),
            P("rec", "seq"),
            P("rec", None),
            P("rec", None),
            P("rec", None, "seq"),
            P(),
            P(),
            P(),
            P(),
            P(),
            P(),
            P(),
            P(),
            P(),
            P(),
            P(),
            P(),
            P(),
            P(),
            P(),
            P(),
            P(),
            P("rec", "seq", None),
        ),
        out_specs=(
            P("rec", "seq", None),
            P("rec", "seq", None),
            P("seq", None),
            P("seq"),
            P("seq", None),
            P("seq", None),
            P("seq"),
            P("seq", None),
            P("seq", None),
            P("seq"),
            P("seq", None),
            P("seq", None),
            P("seq"),
            P("seq"),
            P("seq", None),
            P("seq"),
            P("seq", None),
            P("seq", None),
            P("seq"),
        ),
        check_vma=False,
    )
```

```python
import jax
import jax.numpy as jnp
from jax import lax
from jax.experimental import pallas as pl
from jax.experimental.pallas import tpu as pltpu
from jax.sharding import PartitionSpec as P

D = 512
FF = 2048
HEADS = 8
STATE = 32
SUB = 4
KERNEL = 15
HEADP = 64
PROJ = 1536
WIDE = 512
EPS = 1e-05
F32 = jnp.float32
BF16 = jnp.bfloat16
LIMIT = 56
READ_SCALE = STATE ** (-0.5)


def dot(a, b):
    return lax.dot_general(a, b, (((1,), (0,)), ((), ())), preferred_element_type=F32)


def dot_t(a, b):
    return lax.dot_general(a, b, (((1,), (1,)), ((), ())), preferred_element_type=F32)


def t_dot(a, b):
    return lax.dot_general(a, b, (((0,), (0,)), ((), ())), preferred_element_type=F32)


def sigmoid(x):
    return 0.5 * jnp.tanh(0.5 * x) + 0.5


def mean(x):
    return jnp.mean(x, axis=-1, keepdims=True)


def norm(x, gain):
    centred = x - mean(x)
    scale = lax.rsqrt(mean(centred * centred) + EPS)
    return (centred * scale * gain).astype(BF16), scale


def norm_back(grad, normed, scale, gain):
    wide = normed.astype(F32)
    inverse = 1.0 / gain
    both = grad * wide
    inner = grad * gain
    back = scale * (inner - mean(inner) - wide * inverse * mean(both))
    return back, jnp.sum(both, axis=0, keepdims=True) * inverse


def split_two(x):
    high = x.astype(BF16)
    return high, (x - high.astype(F32)).astype(BF16)


def split_three(x):
    high, rest = split_two(x)
    return high, rest, (x - high.astype(F32) - rest.astype(F32)).astype(BF16)


def iota(shape, dim):
    return lax.broadcasted_iota(jnp.int32, shape, dim)


def lane_mask(columns, width, index):
    lane = iota((16, columns), 1)
    inside = (lane >= width * index) & (lane < width * (index + 1))
    return jnp.where(inside, 1.0, 0.0).astype(BF16)[:1]


def pack_state(full):
    lane = iota((STATE, 128), 1)
    return [
        jnp.where(
            lane < HEADP,
            full[64 * a : 64 * a + 32, 128 * a : 128 * a + 128],
            full[64 * a + 32 : 64 * a + 64, 128 * a : 128 * a + 128],
        )
        for a in range(4)
    ]


def unpack_state(ref, full):
    lane = iota((STATE, 128), 1)
    full[...] = jnp.zeros_like(full)
    for a in range(4):
        pair = ref[0, a, :STATE, :]
        full[64 * a : 64 * a + 32, 128 * a : 128 * a + 128] = jnp.where(
            lane < HEADP, pair, 0.0
        ).astype(BF16)
        full[64 * a + 32 : 64 * a + 64, 128 * a : 128 * a + 128] = jnp.where(
            lane < HEADP, 0.0, pair
        ).astype(BF16)


def accumulate(ref, value):
    first = pl.program_id(0) == 0

    @pl.when(first)
    def _():
        ref[...] = value

    @pl.when(jnp.logical_not(first))
    def _():
        ref[...] += value


def front_kernel(
    feat, tk, fk, dec, dec_t, keep, w_sub, g1, w1, w2, g2, w_in,
    flat, x1, a1, r1, s1, d1, a2, r2, u, g, bs, c, ce, bt, se, ee, te, cum, cum_t, state,
    frames,
):
    steps = x1.shape[1]
    frames[...] = feat[0].astype(F32)
    parts = [
        frames[pl.ds(j, steps, stride=SUB), :] * (tk[0][:, j : j + 1] * fk[0]) for j in range(SUB)
    ]
    parts.append(jnp.zeros((steps, WIDE - SUB * parts[0].shape[1]), F32))
    stacked = jnp.concatenate(parts, axis=1).astype(BF16)
    flat[0] = stacked
    x0 = dot(stacked, w_sub[...])
    low, scale = norm(x0, g1[...])
    a1[0] = low
    r1[0] = scale
    total = jnp.zeros((steps, D), F32)
    for at in range(0, FF, D):
        hidden = dot(low, w1[:, at : at + D])
        gate = sigmoid(hidden)
        active = hidden * gate
        d1[0, :, at : at + D] = (gate * (1.0 + hidden - active)).astype(BF16)
        active = active.astype(BF16)
        s1[0, :, at : at + D] = active
        total += dot(active, w2[at : at + D, :])
    after = x0 + 0.5 * total
    x1[0] = after
    low, scale = norm(after, g2[...])
    a2[0] = low
    r2[0] = scale
    u_low = dot(low, w_in[:, :D]).astype(BF16)
    u[0] = u_low
    g[0] = dot(low, w_in[:, D : 2 * D]).astype(BF16)
    keys = dot(low, w_in[:, 2 * D : 2 * D + 256])
    reads = dot(low, w_in[:, 2 * D + 256 :])
    log_decay = jnp.log(dec_t[0])
    lower = jnp.where(iota((steps, steps), 0) >= iota((steps, steps), 1), 1.0, 0.0).astype(BF16)
    running = sum(dot(lower, part) for part in split_three(log_decay))
    running_t = sum(dot_t(part, lower) for part in split_three(jnp.log(dec[0])))
    cum[0] = running
    cum_t[0] = running_t
    spread = jnp.where(iota((HEADS, 256), 1) // STATE == iota((HEADS, 256), 0), 1.0, 0.0).astype(BF16)

    def over_columns(value):
        return sum(dot(part, spread) for part in split_two(value))

    scale_wide = over_columns(jnp.sqrt(-2.0 * log_decay))
    head = jnp.exp(running)
    head_wide = over_columns(head)
    tail_wide = over_columns(jnp.exp(running[steps - 1 :, :] - running))
    se[0] = scale_wide.astype(BF16)
    ee[0] = head_wide.astype(BF16)
    te[0] = tail_wide.astype(BF16)
    keys = keys * scale_wide
    bs[0] = keys.astype(BF16)
    c[0] = reads.astype(BF16)
    ce[0] = (reads * head_wide).astype(BF16)
    tailed = (keys * tail_wide).astype(BF16)
    bt[0] = tailed
    spread_values = jnp.where(iota((HEADS, D), 1) // HEADP == iota((HEADS, D), 0), 1.0, 0.0).astype(BF16)
    block = sum(dot(part, spread_values) for part in split_three(head[steps - 8 :, :]))
    block = block[7:8, :] * keep[0, pl.program_id(0)]
    for a, pair in enumerate(pack_state(t_dot(tailed, u_low))):
        state[0, a, :STATE, :] = pair
        state[0, a, STATE:, :] = jnp.broadcast_to(block[:, 128 * a : 128 * a + 128], (8, 128))


def mix_kernel(u, bs, c, cum, cum_t, mixed, pairs, decay_pairs):
    steps = u.shape[1]
    causal = iota((steps, steps), 0) >= iota((steps, steps), 1)
    keys = bs[0]
    reads = c[0]
    for q in range(2):
        values = u[0, :, 256 * q : 256 * q + 256]
        total = jnp.zeros((steps, 256), F32)
        for b in range(4):
            h = 4 * q + b
            weights = jnp.exp(
                jnp.where(causal, cum[0, :, h : h + 1] - cum_t[0, h : h + 1, :], -1e30)
            )
            scores = (dot_t(reads * lane_mask(256, STATE, h), keys) * weights).astype(BF16)
            decay_pairs[0, h] = weights.astype(BF16)
            pairs[0, h] = scores
            total += dot(scores, values * lane_mask(256, HEADP, b))
        mixed[0, :, 256 * q : 256 * q + 256] = total


def lift_kernel(
    mixed, ce, start, g, x1, w_out, g3, w_conv,
    z, gs, yd, x2, a3, r3, v, sq, cq, top, bottom,
    full,
):
    steps = x1.shape[1]
    unpack_state(start, full)
    y = (mixed[0] + dot(ce[0], full[...])) * READ_SCALE
    gate = g[0].astype(F32)
    sig = sigmoid(gate)
    active = gate * sig
    gs[0] = (active * READ_SCALE).astype(BF16)
    yd[0] = (y * sig * (1.0 + gate - active)).astype(BF16)
    gated = (y * active).astype(BF16)
    z[0] = gated
    after = x1[0] + dot(gated, w_out[...])
    x2[0] = after
    low, scale = norm(after, g3[...])
    a3[0] = low
    r3[0] = scale
    first = dot(low, w_conv[:, :D])
    sig = sigmoid(dot(low, w_conv[:, D:]))
    out = first * sig
    v[0] = out
    sq[0] = sig.astype(BF16)
    cq[0] = (out * (1.0 - sig)).astype(BF16)
    top[0] = out[:8, :]
    bottom[0] = out[steps - 8 :, :]


def fill_padded(padded, body, before, after, keep):
    steps = body.shape[1]
    row = pl.program_id(0)
    for i in range(D // 128):
        columns = slice(128 * i, 128 * i + 128)
        padded[i, :8, :] = before[0, :, columns] * keep[0, row]
        padded[i, 8 : 8 + steps, :] = body[0, :, columns]
        padded[i, 8 + steps :, :] = after[0, :, columns] * keep[1, row]


def depth_kernel(v, before, after, keep, taps, dc, sums, padded):
    steps = v.shape[1]
    fill_padded(padded, v, before, after, keep)
    total, square = [], []
    for at in range(0, D, 128):
        running = jnp.zeros((steps, 128), F32)
        for k in range(KERNEL):
            running += padded[at // 128, k + 1 : k + 1 + steps, :] * taps[k : k + 1, at : at + 128]
        dc[0, :, at : at + 128] = running
        total.append(jnp.sum(running, axis=0, keepdims=True))
        square.append(jnp.sum(running * running, axis=0, keepdims=True))
    accumulate(sums, jnp.concatenate([jnp.concatenate(total, axis=1), jnp.concatenate(square, axis=1)], axis=0))


def batch_stats(stats, count):
    middle = stats[0:1, :] / count
    return middle, lax.rsqrt(stats[1:2, :] / count - middle * middle + EPS)


def late_kernel(count):
    def kernel(
        dc, x2, og, stats, bn_gain, bn_shift, w_conv, g4, w3, w4, g5,
        out, e, a4, s4, gf, gh, ge, gx3, gbn, sums, ln4, ln5,
        slope,
    ):
        middle, inv = batch_stats(stats, count)
        unit = (dc[0] - middle) * inv
        batch = unit * bn_gain[...] + bn_shift[...]
        sig = sigmoid(batch)
        active = batch * sig
        conv_slope = sig * (1.0 + batch - active)
        active = active.astype(BF16)
        e[0] = active
        x3 = x2[0] + dot(active, w_conv[...])
        low, scale4 = norm(x3, g4[...])
        a4[0] = low
        total = jnp.zeros_like(x3)
        for at in range(0, FF, D):
            hidden = dot(low, w3[:, at : at + D])
            gate = sigmoid(hidden)
            active = hidden * gate
            slope[:, at : at + D] = (gate * (1.0 + hidden - active)).astype(BF16)
            active = active.astype(BF16)
            s4[0, :, at : at + D] = active
            total += dot(active, w4[at : at + D, :])
        x4 = x3 + 0.5 * total
        centred = x4 - mean(x4)
        scale = lax.rsqrt(mean(centred * centred) + EPS)
        unit5 = centred * scale
        out[0] = (unit5 * g5[...]).astype(BF16)
        grad = og[0].astype(F32)
        both = grad * unit5
        inner = grad * g5[...]
        accumulate(ln5, jnp.sum(both, axis=0, keepdims=True))
        gx4 = scale * (inner - mean(inner) - unit5 * mean(inner * unit5))
        gf_low = (0.5 * gx4).astype(BF16)
        gf[0] = gf_low
        back = jnp.zeros_like(x3)
        for at in range(0, FF, D):
            hidden = (dot_t(gf_low, w4[at : at + D, :]) * slope[:, at : at + D].astype(F32)).astype(BF16)
            gh[0, :, at : at + D] = hidden
            back += dot_t(hidden, w3[:, at : at + D])
        back, gain4 = norm_back(back, low, scale4, g4[...])
        accumulate(ln4, gain4)
        grad3 = gx4 + back
        gx3[0] = grad3
        ge_low = grad3.astype(BF16)
        ge[0] = ge_low
        batch_grad = dot_t(ge_low, w_conv[...]) * conv_slope
        gbn[0] = batch_grad
        accumulate(
            sums,
            jnp.concatenate(
                [
                    jnp.sum(batch_grad * unit, axis=0, keepdims=True),
                    jnp.sum(batch_grad, axis=0, keepdims=True),
                ],
                axis=0,
            ),
        )

    return kernel


def batch_back(gbn, dc, stats, back, bn_gain, count):
    middle, inv = batch_stats(stats, count)
    unit = (dc - middle) * inv
    return bn_gain * inv * (gbn - (back[1:2, :] + unit * back[0:1, :]) / count)


def depth_grad_kernel(count):
    def kernel(gbn, dc, stats, back, bn_gain, v, before, after, keep, _, gd, taps_grad, padded):
        steps = v.shape[1]
        fill_padded(padded, v, before, after, keep)
        grad = batch_back(gbn[0], dc[0], stats, back, bn_gain[...], count)
        gd[0] = grad
        columns = []
        for at in range(0, D, 128):
            piece = gd[0, :, at : at + 128]
            rows = [
                jnp.sum(padded[at // 128, k + 1 : k + 1 + steps, :] * piece, axis=0, keepdims=True)
                for k in range(KERNEL)
            ]
            columns.append(jnp.concatenate(rows + [jnp.zeros((1, 128), F32)], axis=0))
        accumulate(taps_grad, jnp.concatenate(columns, axis=1))

    return kernel


def conv_back_kernel(
    gd, before, after, keep, taps, sq, cq, w_conv, a3, r3, g3, gx3, w_out, gs, yd, ce, block,
    gq, gx2, gz, gy, gg, pulled, ln3,
    padded,
):
    steps = gd.shape[1]
    fill_padded(padded, gd, before, after, keep)
    for at in range(0, D, 128):
        running = jnp.zeros((steps, 128), F32)
        for k in range(KERNEL):
            running += padded[at // 128, 15 - k : 15 - k + steps, :] * taps[k : k + 1, at : at + 128]
        gq[0, :, at : at + 128] = (running * sq[0, :, at : at + 128].astype(F32)).astype(BF16)
        gq[0, :, D + at : D + at + 128] = (running * cq[0, :, at : at + 128].astype(F32)).astype(BF16)
    back, gain = norm_back(dot_t(gq[0], w_conv[...]), a3[0], r3[0], g3[...])
    accumulate(ln3, gain)
    grad = gx3[0] + back
    gx2[0] = grad
    low = grad.astype(BF16)
    gz[0] = low
    inner = dot_t(low, w_out[...])
    gg[0] = (inner * yd[0].astype(F32)).astype(BF16)
    read_grad = (inner * gs[0].astype(F32)).astype(BF16)
    gy[0] = read_grad
    row = pl.program_id(0)
    for a, pair in enumerate(pack_state(t_dot(ce[0], read_grad))):
        pulled[0, a, :STATE, :] = pair * keep[0, row]
        pulled[0, a, STATE:, :] = block[0, a, STATE:, :]


def mix_back_kernel(u, bs, c, ee, gy, start, pairs, decay_pairs, _, gu, gb, gc, full):
    steps = u.shape[1]
    unpack_state(start, full)
    reads_grad = dot_t(gy[0], full[...]) * ee[0].astype(F32)
    keys_grad = jnp.zeros((steps, 256), F32)
    keys = bs[0]
    reads = c[0]
    for q in range(2):
        values = u[0, :, 256 * q : 256 * q + 256]
        grads = gy[0, :, 256 * q : 256 * q + 256]
        total = jnp.zeros((steps, 256), F32)
        for b in range(4):
            h = 4 * q + b
            masked = grads * lane_mask(256, HEADP, b)
            scores = (dot_t(masked, values) * decay_pairs[0, h].astype(F32)).astype(BF16)
            mask = lane_mask(256, STATE, h)
            reads_grad += dot(scores, keys * mask)
            keys_grad += t_dot(scores, reads * mask)
            total += t_dot(pairs[0, h], masked)
        gu[0, :, 256 * q : 256 * q + 256] = total
    gc[0] = reads_grad.astype(BF16)
    gb[0] = keys_grad


def mix_end_kernel(
    end, u, bt, te, se, gu, gb, gc, gg, w_in, a2, r2, g2, gx2, _,
    gp, gx1, gf, ln2,
    full,
):
    unpack_state(end, full)
    gp[0, :, :D] = (gu[0] + dot(bt[0], full[...])).astype(BF16)
    gp[0, :, D : 2 * D] = gg[0]
    keys_grad = gb[0] + te[0].astype(F32) * dot_t(u[0], full[...])
    gp[0, :, 2 * D : 2 * D + 256] = (keys_grad * se[0].astype(F32)).astype(BF16)
    gp[0, :, 2 * D + 256 :] = gc[0]
    back, gain = norm_back(dot_t(gp[0], w_in[...]), a2[0], r2[0], g2[...])
    accumulate(ln2, gain)
    grad = gx2[0] + back
    gx1[0] = grad
    gf[0] = (0.5 * grad).astype(BF16)


def front_back_kernel(
    gx1, gf, w2, d1, w1, a1, r1, g1, w_sub, tk, fk, _,
    gh, gxr, fg, ln1,
):
    steps = gx1.shape[1]
    low = gf[0]
    back = jnp.zeros((steps, D), F32)
    for at in range(0, FF, D):
        hidden = (dot_t(low, w2[at : at + D, :]) * d1[0, :, at : at + D].astype(F32)).astype(BF16)
        gh[0, :, at : at + D] = hidden
        back += dot_t(hidden, w1[:, at : at + D])
    back, gain = norm_back(back, a1[0], r1[0], g1[...])
    accumulate(ln1, gain)
    low = (gx1[0] + back).astype(BF16)
    gxr[0] = low
    frames = dot(low, w_sub[...])
    mels = fk.shape[2]
    for j in range(SUB):
        fg[0, pl.ds(j, steps, stride=SUB), :] = frames[:, mels * j : mels * (j + 1)] * (
            tk[0][:, j : j + 1] * fk[0]
        )


def by_share_store(out, at, share, start, block):
    for piece in range(block.shape[0] // share):
        row = start + share * piece
        place = row // (4 * share) * share
        k = row % (4 * share) // share
        out[place : place + share, at + D * k : at + D * (k + 1)] = block[
            share * piece : share * (piece + 1), :
        ]


def late_weights_kernel(share):
    def kernel(a4, e, s4, gh, ge, gf, out):
        left = a4[...].T
        for at in range(0, FF, D):
            out[:, at : at + D] = dot(left, gh[:, at : at + D])
        for at in range(0, 1024, 256):
            by_share_store(out, FF, share, at, dot(s4[:, at : at + 256].T, gf[...]))
        out[:, 2 * FF :] = dot(e[...].T, ge[...])

    return kernel


def turned(place, share, core, block):
    rows = block.T
    half = rows.shape[0] // 2
    for s in range(rows.shape[0] // share):
        side = core if s % 2 == 0 else 1 - core
        at = pl.multiple_of(side * half + s // 2 * share, 16)
        place[pl.ds(at, share), :] = rows[s * share : (s + 1) * share, :]


def turned_by_share(place, share, core, block):
    for at in range(0, block.shape[1], 256):
        rows = block[:, at : at + 256].T
        for piece in range(256 // share):
            row = at + share * piece
            s, k = row // (4 * share), row % (4 * share) // share
            side = core if s % 2 == 0 else 1 - core
            to = pl.multiple_of(side * (D // 2) + D * k + s // 2 * share, 16)
            place[pl.ds(to, share), :] = rows[share * piece : share * (piece + 1), :]


def weights_kernel(pairs, share, waits):
    has_small = pairs[-1] == (1, 0)

    def kernel(core_ref, *refs):
        count = len(pairs)
        lefts, rights = refs[:count], refs[count : 2 * count]
        extra = refs[2 * count] if has_small else None
        kept, sent = refs[2 * count + has_small + waits :][:2]
        places = refs[2 * count + has_small + waits + 2 :]
        step = pl.program_id(0)
        core = core_ref[0]
        start = 0
        for (wide, long), left, right, place in zip(pairs, lefts, rights, places):
            steps = max(wide, long)

            @pl.when(step == start)
            def _(left=left, place=place, wide=wide):
                if wide == 1:
                    turned(place, share, core, left[...])
                else:
                    turned_by_share(place, share, core, left)

            @pl.when((step >= start) & (step < start + steps))
            def _(right=right, place=place, wide=wide, start=start):
                if wide == 1:
                    rows = place[...]
                else:
                    rows = place[pl.ds(pl.multiple_of((step - start) * D, D), D), :]
                block = dot(rows, right[...])
                kept[...] = block[: D // 2, :]
                sent[...] = block[D // 2 :, :]

            start += steps
        if has_small:

            @pl.when(step == start - 1)
            def _():
                for s in range(D // share // 2):
                    for out, side in ((kept, core), (sent, 1 - core)):
                        at = pl.multiple_of((2 * s + side) * share, 8)
                        out[s * share : (s + 1) * share, :] += extra[pl.ds(at, share), :]

    return kernel


def weight_sums(pairs, share, core, small=None, after=()):
    tokens = pairs[0][0].shape[0]
    sizes = [(l.shape[1] // D, r.shape[1] // D) for l, r in pairs]
    if small is not None:
        sizes[-1] = (1, 0)
    lefts, rights, start = [], [], 0
    for (left, right), (wide, long) in zip(pairs, sizes):
        steps = max(wide, long)
        lefts.append((left, "all"))
        if wide == 1 and long > 1:
            index = lambda j, start=start, last=steps - 1: (0, jnp.clip(j - start, 0, last))
            rights.append((right, pl.BlockSpec((tokens, D), index)))
        else:
            rights.append((right, "all"))
        start += steps
    columns = start * D
    extra = [] if small is None else [(small, "all")]
    half = ((D // 2, columns), F32, pl.BlockSpec((D // 2, D), lambda j: (0, j)))
    return call(
        weights_kernel(sizes, share, len(after)),
        (start,),
        [(core, scalars())] + lefts + rights + extra + [(a, anywhere()) for a in after],
        [half, half],
        [pltpu.VMEM((D * wide, tokens), BF16) for wide, _ in sizes],
        2 * tokens * D * columns,
        "weights",
    )


def row_spec(shape):
    rest = len(shape) - 1
    return pl.BlockSpec((1,) + tuple(shape[1:]), lambda r: (r,) + (0,) * rest)


def whole_spec(shape):
    return pl.BlockSpec(tuple(shape), lambda r: (0,) * len(shape))


def held_spec(shape):
    return pl.BlockSpec(tuple(shape), lambda r: (0,) * len(shape), pipeline_mode=pl.Buffered(1))


def scalars():
    return pl.BlockSpec(memory_space=pltpu.SMEM)


def anywhere():
    return pl.BlockSpec(memory_space=pl.ANY)


TIMES = {'front': 19, 'mix': 6, 'lift': 8, 'depth': 6, 'late': 22, 'late_weights': 10, 'depth_grad': 7, 'conv_back': 11, 'mix_back': 11, 'mix_end': 8, 'front_back': 13, 'weights': 9}


def call(kernel, grid, ins, outs, scratch=(), flops=0, name=None, room=LIMIT):
    def made(kind, shape):
        if kind == "row":
            return row_spec(shape)
        return whole_spec(shape) if kind == "all" else kind

    moved = sum(a.size * a.dtype.itemsize for a, _ in ins)
    return pl.pallas_call(
        kernel,
        grid=grid,
        in_specs=[held_spec(a.shape) if kind == "all" else made(kind, a.shape) for a, kind in ins],
        out_specs=[made(kind, shape) for shape, _, kind in outs],
        out_shape=[jax.ShapeDtypeStruct(shape, kind) for shape, kind, _ in outs],
        scratch_shapes=list(scratch),
        compiler_params=pltpu.CompilerParams(
            dimension_semantics=("arbitrary",), vmem_limit_bytes=room * 2**20
        ),
        cost_estimate=pl.CostEstimate(
            flops=int(TIMES[name] * 1.15e9), bytes_accessed=0, transcendentals=0
        ),
        name=name,
    )(*[a for a, _ in ins])


def flip_pairs(count, mask):
    return [(i, i ^ mask) for i in range(count)]


def entering(value, backward):
    count, mine = lax.axis_size("seq"), lax.axis_index("seq")

    def link(earlier, later):
        decay = later[:, :, STATE : STATE + 1, :]
        state = decay * earlier[:, :, :STATE, :] + later[:, :, :STATE, :]
        return jnp.concatenate([state, decay * earlier[:, :, STATE:, :]], axis=2)

    shape = value.shape[:2] + (STATE, value.shape[3])
    before = jnp.concatenate(
        [jnp.zeros(shape, F32), jnp.ones(value.shape[:2] + (8, value.shape[3]), F32)], axis=2
    )
    mask = 1
    while mask < count:
        other = lax.ppermute(value, "seq", flip_pairs(count, mask))
        second = ((mine & mask) != 0) != backward
        before = jnp.where(second, link(other, before), before)
        value = jnp.where(second, link(other, value), link(value, other))
        mask *= 2
    return before


def halos(top, bottom):
    count = lax.axis_size("seq")
    ends = range(count - 1)
    return (
        lax.ppermute(bottom, "seq", [(i, i + 1) for i in ends]),
        lax.ppermute(top, "seq", [(i + 1, i) for i in ends]),
    )


def sum_over_all(value):
    count = lax.axis_size("seq") * lax.axis_size("rec")
    copies = jnp.broadcast_to(value[None], (count,) + value.shape)
    return jnp.sum(lax.all_to_all(copies, ("rec", "seq"), 0, 0), axis=0)


def scatter_sum(value):
    return lax.psum_scatter(value, "seq", scatter_dimension=0, tiled=True)


def in_vmem(kernel, scalars_in, ins, outs, after, name):
    vmem = pl.BlockSpec(memory_space=pltpu.VMEM)
    return pl.pallas_call(
        kernel,
        in_specs=[scalars()] + [vmem] * len(ins) + [anywhere()] * len(after),
        out_specs=[vmem] * len(outs),
        out_shape=[jax.ShapeDtypeStruct(shape, F32) for shape in outs],
        compiler_params=pltpu.CompilerParams(vmem_limit_bytes=32 * 2**20),
        cost_estimate=pl.CostEstimate(
            flops=0, bytes_accessed=0, transcendentals=0
        ),
        name=name,
    )(scalars_in, *ins, *after)


def part_rows(ref, group, chunk, side, columns):
    if chunk % 8:
        low = ref[2 * group * chunk : (2 * group + 1) * chunk, columns]
        high = ref[(2 * group + 1) * chunk : (2 * group + 2) * chunk, columns]
        return jnp.where(side == 0, low, high)
    return ref[pl.ds(pl.multiple_of((2 * group + side) * chunk, 8), chunk), columns]


def add_and_split(bits, groups, after):
    arrays, outs, plan = [], [], []

    def known(array):
        for i, other in enumerate(arrays):
            if other is array:
                return i
        arrays.append(array)
        return len(arrays) - 1

    for items, chunk, bit in groups:
        rows = items[0][0].shape[0]
        placed, at = [], 0
        for kept, received, first, columns in items:
            placed.append(
                (known(kept), None if received is None else known(received), first, columns, at)
            )
            at += columns
        plan.append((placed, rows, chunk, bit, len(outs)))
        outs += [(rows // 2, at)] * 2
    count = len(arrays) + len(after)

    def kernel(bit_ref, *refs):
        for placed, rows, chunk, bit, out in plan:
            mine = bit_ref[bit]
            for kept, received, first, columns, at in placed:
                for target, side in ((refs[count + out], mine), (refs[count + out + 1], 1 - mine)):
                    for group in range(rows // chunk // 2):
                        value = part_rows(refs[kept], group, chunk, side, slice(first, first + columns))
                        if received is not None:
                            value = value + part_rows(
                                refs[received], group, chunk, side, slice(first, first + columns)
                            )
                        target[group * chunk : (group + 1) * chunk, at : at + columns] = value

    made = in_vmem(kernel, bits, arrays, outs, after, "add_and_split")
    return [(made[i], made[i + 1]) for i in range(0, len(made), 2)]


def add_pair(bits, kept, received, after):
    def kernel(_, a, b, *rest):
        rest[-1][...] = a[...] + b[...]

    return in_vmem(kernel, bits, [kept, received], [kept.shape], after, "add_pair")[0]


def join(bits, mine, other, bit, after, pieces=None):
    rows, columns = mine.shape
    outs = [(2 * rows, columns)]
    if pieces is not None:
        outs = [(8 * rows, D) if spread else (2 * rows, wide) for _, wide, spread in pieces]
    cuts = [(0, columns, False)] if pieces is None else pieces

    def kernel(bit_ref, mine_ref, other_ref, *rest):
        first = bit_ref[bit] == 0
        targets = rest[len(after) :]
        for target, (at, wide, spread) in zip(targets, cuts):
            for k in range(4 if spread else 1):
                width = D if spread else wide
                left = mine_ref[:, at + D * k : at + D * k + width]
                right = other_ref[:, at + D * k : at + D * k + width]
                start = 2 * rows * k
                target[start : start + rows, :] = jnp.where(first, left, right)
                target[start + rows : start + 2 * rows, :] = jnp.where(first, right, left)

    made = in_vmem(kernel, bits, [mine, other], outs, after, "join")
    return made[0] if pieces is None else made


class Sum:
    def __init__(self, bits, pieces):
        self.bits = bits
        self.pieces = pieces
        self.seq = lax.axis_size("seq")
        self.rec = lax.axis_size("rec")
        self.chip_bits = self.seq.bit_length() - 2
        self.rec_bits = self.rec.bit_length() - 1
        self.parts = []
        self.left = []
        self.steps = []
        self.done = None

    def swap(self, value, axis, bit):
        return lax.ppermute(value, axis, flip_pairs(lax.axis_size(axis), 1 << bit))

    def begin(self, kept, sent, first):
        columns = kept.shape[1]
        received = self.swap(sent, "seq", 0)
        self.parts = [[(kept, received, 0, first)], [(kept, received, first, columns - first)]]
        turn = 1 + self.chip_bits // 2
        orders = (
            list(range(1, self.chip_bits + 1)),
            list(range(turn, self.chip_bits + 1)) + list(range(1, turn)),
        )
        self.left = [list(range(self.chip_bits, 0, -1)) for _ in orders]
        self.steps += [("chips", now) for now in zip(*orders)]
        self.finish_steps()

    def finish_steps(self):
        self.steps += [("rec", bit) for bit in range(self.rec_bits)] + [("turn", self.rec_bits - 1)]
        self.steps += [("join", bit) for bit in reversed(range(self.rec_bits))]

    def advance(self, after):
        kind, now = self.steps.pop(0)
        if kind == "chips":
            groups = []
            for items, bit, left in zip(self.parts, now, self.left):
                rows = items[0][0].shape[0]
                chunk = rows >> (left.index(bit) + 1)
                left.remove(bit)
                groups.append((items, chunk, bit))
            made = add_and_split(self.bits, groups, after)
            self.parts = [
                [(kept, self.swap(sent, "seq", bit), 0, kept.shape[1])]
                for (kept, sent), bit in zip(made, now)
            ]
            return made[0][0]
        if kind == "rec":
            items = [item for part in self.parts for item in part]
            groups = [(items, items[0][0].shape[0] // 2, self.chip_bits + 1 + now)]
            [(kept, sent)] = add_and_split(self.bits, groups, after)
            self.parts = [[(kept, self.swap(sent, "rec", now), 0, kept.shape[1])]]
            return kept
        if kind == "turn":
            [[(kept, received, _, _)]] = self.parts
            self.mine = add_pair(self.bits, kept, received, after)
            self.other = self.swap(self.mine, "rec", now)
            return self.mine
        bit = self.chip_bits + 1 + now
        if now == 0:
            self.done = join(self.bits, self.mine, self.other, bit, after, self.pieces)
            return self.done[0]
        self.mine = join(self.bits, self.mine, self.other, bit, after)
        self.other = self.swap(self.mine, "rec", now - 1)
        return self.mine


def local(
    features, time_keep, freq_keep, block_flags, decays, w_sub, ln1_gain, ffn1_in, ffn1_out, ln2_gain,
    ssm_in, ssm_out, ln3_gain, conv_in, conv_depth, bn_gain, bn_shift, conv_out, ln4_gain, ffn2_in,
    ffn2_out, ln5_gain, out_grad,
):
    rows, frame_count, mels = features.shape
    steps = frame_count // SUB
    tokens = rows * steps
    blocks = lax.axis_size("seq")
    place = lax.axis_index("seq")
    count = float(tokens * blocks * lax.axis_size("rec"))
    share = D // blocks
    here = lax.dynamic_index_in_dim(block_flags, place, 1, keepdims=False)
    after = lax.dynamic_index_in_dim(
        block_flags, jnp.minimum(place + 1, blocks - 1), 1, keepdims=False
    )
    keep_here = (1 - here).astype(F32)
    keep_next = jnp.where(place + 1 < blocks, 1 - after, 0).astype(F32)
    keep = (jnp.stack([keep_here, keep_next]), scalars())
    tk = (time_keep.reshape(rows, steps, SUB).astype(F32), "row")
    fk = (freq_keep[:, None, :].astype(F32), "row")
    sub_wide = jnp.pad(w_sub, ((0, 0), (0, WIDE - SUB * mels)))
    g1, g2, g3, g4, g5, bg, bb = (
        (gain.reshape(1, D), "all")
        for gain in (ln1_gain, ln2_gain, ln3_gain, ln4_gain, ln5_gain, bn_gain, bn_shift)
    )
    taps = (jnp.pad(conv_depth.T, ((0, 1), (0, 0))), "all")

    def rows_of(width, kind=F32):
        return ((rows, steps, width), kind, "row")

    per_state = ((rows, 4, STATE + 8, 128), F32, "row")
    edge = ((rows, 8, D), F32, "row")
    line = ((1, D), F32, "all")
    two_lines = ((2, D), F32, "all")
    padded = pltpu.VMEM((D // 128, steps + 16, 128), F32)
    full = pltpu.VMEM((256, D), BF16)

    def row(value):
        return (value, "row")

    def every(value):
        return (value, "all")

    (flat, x1, a1, r1, s1, d1, a2, r2, u, g, bs, c, ce, bt, se, ee, te, cum, cum_t, state) = call(
        front_kernel,
        (rows,),
        [
            row(features), tk, fk, row(decays), row(decays.transpose(0, 2, 1)), keep,
            every(sub_wide.T), g1, every(ffn1_in), every(ffn1_out), g2, every(ssm_in),
        ],
        [
            rows_of(WIDE, BF16), rows_of(D), rows_of(D, BF16), rows_of(1), rows_of(FF, BF16),
            rows_of(FF, BF16), rows_of(D, BF16), rows_of(1), rows_of(D, BF16), rows_of(D, BF16),
            rows_of(256, BF16), rows_of(256, BF16), rows_of(256, BF16), rows_of(256, BF16),
            rows_of(256, BF16), rows_of(256, BF16), rows_of(256, BF16), rows_of(HEADS),
            ((rows, HEADS, steps), F32, "row"), per_state,
        ],
        [pltpu.VMEM((frame_count, mels), F32)],
        2 * tokens * D * (WIDE + 2 * FF + PROJ),
        "front",
    )
    before = entering(state, False)
    start = before * keep_here[:, None, None, None]
    pair_shape = ((rows, HEADS, steps, steps), BF16, "row")
    mixed, pairs, decay_pairs = call(
        mix_kernel,
        (rows,),
        [row(u), row(bs), row(c), row(cum), row(cum_t)],
        [rows_of(D), pair_shape, pair_shape],
        (),
        2 * tokens * 256 * 256 * 16,
        "mix",
    )
    z, gs, yd, x2, a3, r3, v, sq, cq, top, bottom = call(
        lift_kernel,
        (rows,),
        [row(mixed), row(ce), row(start), row(g), row(x1), every(ssm_out), g3, every(conv_in)],
        [
            rows_of(D, BF16), rows_of(D, BF16), rows_of(D, BF16), rows_of(D), rows_of(D, BF16),
            rows_of(1), rows_of(D), rows_of(D, BF16), rows_of(D, BF16), edge, edge,
        ],
        [full],
        2 * tokens * D * 4 * D,
        "lift",
    )
    v_before, v_after = halos(top, bottom)
    dc, sums = call(
        depth_kernel,
        (rows,),
        [row(v), row(v_before), row(v_after), keep, taps],
        [rows_of(D), two_lines],
        [padded],
        2 * tokens * D * 64,
        "depth",
    )
    stats = sum_over_all(sums)
    out, e, a4, s4, gf4, gh4, ge, gx3, gbn, back_sums, ln4, ln5 = call(
        late_kernel(count),
        (rows,),
        [
            row(dc), row(x2), row(out_grad), every(stats), bg, bb, every(conv_out), g4,
            every(ffn2_in), every(ffn2_out), g5,
        ],
        [
            rows_of(D, BF16), rows_of(D, BF16), rows_of(D, BF16), rows_of(FF, BF16), rows_of(D, BF16),
            rows_of(FF, BF16), rows_of(D, BF16), rows_of(D), rows_of(D), two_lines, line, line,
        ],
        [pltpu.VMEM((steps, FF), BF16)],
        2 * tokens * D * (4 * FF + 2 * D),
        "late",
    )
    back = sum_over_all(back_sums)

    def flatten(value):
        return value.reshape(tokens, value.shape[-1])

    def column_block(value, width):
        return (flatten(value), pl.BlockSpec((tokens, width), lambda i: (0, i)))

    def row_block(columns):
        return ((D, columns), F32, pl.BlockSpec((256, columns), lambda i: (i, 0)))

    (late_grads,) = call(
        late_weights_kernel(share),
        (2,),
        [
            column_block(a4, 256), column_block(e, 256), column_block(s4, 1024),
            every(flatten(gh4)), every(flatten(ge)), every(flatten(gf4)),
        ],
        [row_block(2 * FF + D)],
        (),
        2 * tokens * D * (2 * FF + D),
        "late_weights",
    )
    group_a = scatter_sum(late_grads)

    def edge_grad(at):
        return batch_back(
            lax.slice_in_dim(gbn, at, at + 8, axis=1),
            lax.slice_in_dim(dc, at, at + 8, axis=1),
            stats, back, bn_gain, count,
        )

    gd_before, gd_after = halos(edge_grad(0), edge_grad(steps - 8))
    gd, taps_grad = call(
        depth_grad_kernel(count),
        (rows,),
        [
            row(gbn), row(dc), every(stats), every(back), bg, row(v), row(v_before), row(v_after), keep,
            (late_grads, anywhere()),
        ],
        [rows_of(D), ((16, D), F32, "all")],
        [padded],
        2 * tokens * D * 64,
        "depth_grad",
    )
    gq, gx2, gz, gy, gg, pulled, ln3 = call(
        conv_back_kernel,
        (rows,),
        [
            row(gd), row(gd_before), row(gd_after), keep, taps, row(sq), row(cq), every(conv_in),
            row(a3), row(r3), g3, row(gx3), every(ssm_out), row(gs), row(yd), row(ce), row(state),
        ],
        [
            rows_of(2 * D, BF16), rows_of(D), rows_of(D, BF16), rows_of(D, BF16), rows_of(D, BF16),
            per_state, line,
        ],
        [padded],
        2 * tokens * D * 4 * D,
        "conv_back",
    )
    end = entering(pulled, True)
    core = (place % 2).reshape(1)
    kept, sent = weight_sums([(flatten(a3), flatten(gq)), (flatten(z), flatten(gz))], share, core)
    bits = jnp.stack(
        [(place >> k) & 1 for k in range(blocks.bit_length() - 1)]
        + [(lax.axis_index("rec") >> k) & 1 for k in range(lax.axis_size("rec").bit_length() - 1)]
    )
    early = Sum(
        bits,
        [
            (0, FF, False), (FF, FF, True), (2 * FF, D, False), (2 * FF + D, 2 * D, False),
            (2 * FF + 3 * D, D, False),
        ],
    )
    early.begin(kept, sent, D)
    gu, gb, gc = call(
        mix_back_kernel,
        (rows,),
        [
            row(u), row(bs), row(c), row(ee), row(gy), row(start), row(pairs), row(decay_pairs),
            (sent, anywhere()),
        ],
        [rows_of(D), rows_of(256), rows_of(256, BF16)],
        [full],
        2 * tokens * 256 * 256 * 32,
        "mix_back",
    )
    token = early.advance([gu])
    gp, gx1, gf1, ln2 = call(
        mix_end_kernel,
        (rows,),
        [
            row(end), row(u), row(bt), row(te), row(se), row(gu), row(gb), row(gc), row(gg),
            every(ssm_in), row(a2), row(r2), g2, row(gx2), (token, anywhere()),
        ],
        [rows_of(PROJ, BF16), rows_of(D), rows_of(D, BF16), line],
        [full],
        2 * tokens * D * PROJ,
        "mix_end",
    )
    token = early.advance([gf1])
    kept, sent = weight_sums(
        [(flatten(a2), flatten(gp)), (flatten(s1), flatten(gf1))], share, core, None, [token]
    )
    middle = Sum(bits, [(0, PROJ, False), (PROJ, FF, True)])
    middle.begin(kept, sent, PROJ)
    gh1, gxr, features_grad, ln1 = call(
        front_back_kernel,
        (rows,),
        [
            row(gx1), row(gf1), every(ffn1_out), row(d1), every(ffn1_in), row(a1), row(r1), g1,
            every(sub_wide), tk, fk, (sent, anywhere()),
        ],
        [rows_of(FF, BF16), rows_of(D, BF16), ((rows, frame_count, mels), F32, "row"), line],
        (),
        2 * tokens * D * (WIDE + 2 * FF),
        "front_back",
    )
    small = jnp.concatenate(
        [ln1, ln2, ln3, ln4, ln5, taps_grad[:KERNEL], jnp.zeros((WIDE - SUB * mels - 20, D), F32)],
        axis=0,
    )
    small = jnp.pad(small.T, ((0, 0), (SUB * mels, 0)))
    token = middle.advance([ln1])
    while early.steps[0][0] == "chips":
        token = early.advance([token])
    early.parts = [[(group_a, None, 0, group_a.shape[1])]] + early.parts
    token = early.advance([token])
    last = Sum(bits, [(0, FF, False), (FF, SUB * mels, False), (FF + SUB * mels, 24, False)])
    kept, sent = weight_sums(
        [(flatten(a1), flatten(gh1)), (flatten(gxr), flatten(flat))], share, core, small, [token]
    )
    last.begin(kept, sent, 2 * D)
    order = [early, middle, last, early, middle, last, middle, last, early, middle, last, early, middle, last]
    order += [middle, last]
    token = sent
    while any(group.steps for group in (early, middle, last)):
        group = order.pop(0) if order else next(g for g in (early, middle, last) if g.steps)
        if group.steps:
            token = group.advance([token])
    ffn2_in_grad, ffn2_out_grad, conv_out_grad, conv_in_grad, ssm_out_grad = early.done
    ssm_in_grad, ffn1_out_grad = middle.done
    ffn1_in_grad, w_sub_grad, gains = last.done

    start_row = place * share
    return (
        out,
        features_grad,
        w_sub_grad,
        gains[:, 0],
        ffn1_in_grad,
        ffn1_out_grad,
        gains[:, 1],
        ssm_in_grad,
        ssm_out_grad,
        gains[:, 2],
        conv_in_grad,
        gains[:, 5 : 5 + KERNEL],
        lax.dynamic_slice_in_dim(back[0], start_row, share),
        lax.dynamic_slice_in_dim(back[1], start_row, share),
        conv_out_grad,
        gains[:, 3],
        ffn2_in_grad,
        ffn2_out_grad,
        gains[:, 4],
    )


def solution(mesh):
    block = P("rec", "seq", None)
    rows_of_seq, line = P("seq", None), P("seq")
    return jax.shard_map(
        local,
        mesh=mesh,
        in_specs=(block, P("rec", "seq"), P("rec", None), P("rec", None), P("rec", None, "seq"))
        + (P(),) * 17
        + (block,),
        out_specs=(
            block, block, rows_of_seq, line, rows_of_seq, rows_of_seq, line, rows_of_seq, rows_of_seq,
            line, rows_of_seq, rows_of_seq, line, line, rows_of_seq, line, rows_of_seq, rows_of_seq, line,
        ),
        check_vma=False,
    )
```

```python
import jax
import jax.numpy as jnp
from jax import lax
from jax.experimental import pallas as pl
from jax.experimental.pallas import tpu as pltpu
from jax.sharding import PartitionSpec as P

D = 512
FF = 2048
HEADS = 8
STATE = 32
SUB = 4
KERNEL = 15
HEADP = 64
PROJ = 1536
WIDE = 512
EPS = 1e-05
F32 = jnp.float32
BF16 = jnp.bfloat16
LIMIT = 32
READ_SCALE = STATE ** (-0.5)


def dot(a, b):
    return lax.dot_general(a, b, (((1,), (0,)), ((), ())), preferred_element_type=F32)


def dot_t(a, b):
    return lax.dot_general(a, b, (((1,), (1,)), ((), ())), preferred_element_type=F32)


def t_dot(a, b):
    return lax.dot_general(a, b, (((0,), (0,)), ((), ())), preferred_element_type=F32)


def sigmoid(x):
    return 0.5 * jnp.tanh(0.5 * x) + 0.5


def mean(x):
    return jnp.mean(x, axis=-1, keepdims=True)


def norm(x, gain):
    centred = x - mean(x)
    scale = lax.rsqrt(mean(centred * centred) + EPS)
    return (centred * scale * gain).astype(BF16), scale


def norm_back(grad, normed, scale, gain):
    wide = normed.astype(F32)
    inverse = 1.0 / gain
    both = grad * wide
    inner = grad * gain
    back = scale * (inner - mean(inner) - wide * inverse * mean(both))
    return back, jnp.sum(both, axis=0, keepdims=True) * inverse


def split_two(x):
    high = x.astype(BF16)
    return high, (x - high.astype(F32)).astype(BF16)


def split_three(x):
    high, rest = split_two(x)
    return high, rest, (x - high.astype(F32) - rest.astype(F32)).astype(BF16)


def iota(shape, dim):
    return lax.broadcasted_iota(jnp.int32, shape, dim)


def lane_mask(columns, width, index):
    lane = iota((16, columns), 1)
    inside = (lane >= width * index) & (lane < width * (index + 1))
    return jnp.where(inside, 1.0, 0.0).astype(BF16)[:1]


def pack_state(full):
    lane = iota((STATE, 128), 1)
    return [
        jnp.where(
            lane < HEADP,
            full[64 * a : 64 * a + 32, 128 * a : 128 * a + 128],
            full[64 * a + 32 : 64 * a + 64, 128 * a : 128 * a + 128],
        )
        for a in range(4)
    ]


def unpack_state(ref, full):
    lane = iota((STATE, 128), 1)
    full[...] = jnp.zeros_like(full)
    for a in range(4):
        pair = ref[0, STATE * a : STATE * (a + 1), :]
        full[64 * a : 64 * a + 32, 128 * a : 128 * a + 128] = jnp.where(
            lane < HEADP, pair, 0.0
        ).astype(BF16)
        full[64 * a + 32 : 64 * a + 64, 128 * a : 128 * a + 128] = jnp.where(
            lane < HEADP, 0.0, pair
        ).astype(BF16)


def accumulate(ref, value):
    first = pl.program_id(0) == 0

    @pl.when(first)
    def _():
        ref[...] = value

    @pl.when(jnp.logical_not(first))
    def _():
        ref[...] += value


def front_kernel(
    feat, tk, fk, dec, dec_t, keep, w_sub, g1, w1, w2, g2, w_in,
    flat, x1, a1, r1, s1, d1, a2, r2, u, g, bs, c, ce, bt, se, ee, te, cum, cum_t, state,
    frames,
):
    steps = x1.shape[1]
    frames[...] = feat[0].astype(F32)
    parts = [
        frames[pl.ds(j, steps, stride=SUB), :] * (tk[0][:, j : j + 1] * fk[0]) for j in range(SUB)
    ]
    parts.append(jnp.zeros((steps, WIDE - SUB * parts[0].shape[1]), F32))
    stacked = jnp.concatenate(parts, axis=1).astype(BF16)
    flat[0] = stacked
    x0 = dot_t(stacked[:, : w_sub.shape[1]], w_sub[...])
    low, scale = norm(x0, g1[...])
    a1[0] = low
    r1[0] = scale
    total = jnp.zeros((steps, D), F32)
    for at in range(0, FF, D):
        hidden = dot(low, w1[:, at : at + D])
        gate = sigmoid(hidden)
        active = hidden * gate
        d1[0, :, at : at + D] = (gate * (1.0 + hidden - active)).astype(BF16)
        active = active.astype(BF16)
        s1[0, :, at : at + D] = active
        total += dot(active, w2[at : at + D, :])
    after = x0 + 0.5 * total
    x1[0] = after
    low, scale = norm(after, g2[...])
    a2[0] = low
    r2[0] = scale
    u_low = dot(low, w_in[:, :D]).astype(BF16)
    u[0] = u_low
    g[0] = dot(low, w_in[:, D : 2 * D]).astype(BF16)
    keys = dot(low, w_in[:, 2 * D : 2 * D + 256])
    reads = dot(low, w_in[:, 2 * D + 256 :])
    log_decay = jnp.log(dec_t[0])
    lower = jnp.where(iota((steps, steps), 0) >= iota((steps, steps), 1), 1.0, 0.0).astype(BF16)
    running = sum(dot(lower, part) for part in split_three(log_decay))
    running_t = sum(dot_t(part, lower) for part in split_three(jnp.log(dec[0])))
    cum[0] = running
    cum_t[0] = running_t
    spread = jnp.where(iota((HEADS, 256), 1) // STATE == iota((HEADS, 256), 0), 1.0, 0.0).astype(BF16)

    def over_columns(value):
        return sum(dot(part, spread) for part in split_two(value))

    scale_wide = over_columns(jnp.sqrt(-2.0 * log_decay))
    head = jnp.exp(running)
    head_wide = over_columns(head)
    tail_wide = over_columns(jnp.exp(running[steps - 1 :, :] - running))
    se[0] = scale_wide.astype(BF16)
    ee[0] = head_wide.astype(BF16)
    te[0] = tail_wide.astype(BF16)
    keys = keys * scale_wide
    bs[0] = keys.astype(BF16)
    c[0] = reads.astype(BF16)
    ce[0] = (reads * head_wide).astype(BF16)
    tailed = (keys * tail_wide).astype(BF16)
    bt[0] = tailed
    spread_values = jnp.where(iota((HEADS, D), 1) // HEADP == iota((HEADS, D), 0), 1.0, 0.0).astype(BF16)
    block = sum(dot(part, spread_values) for part in split_three(head[steps - 8 :, :]))
    block = block[7:8, :] * keep[0, pl.program_id(0)]
    for a, pair in enumerate(pack_state(t_dot(tailed, u_low))):
        state[0, STATE * a : STATE * (a + 1), :] = pair
    lines = [block[:, 128 * a : 128 * a + 128] for a in range(4)]
    state[0, 4 * STATE :, :] = jnp.concatenate(lines + lines, axis=0)


def mix_kernel(u, bs, c, cum, cum_t, mixed, pairs, decay_pairs):
    steps = u.shape[1]
    causal = iota((steps, steps), 0) >= iota((steps, steps), 1)
    keys = bs[0]
    reads = c[0]
    for q in range(2):
        values = u[0, :, 256 * q : 256 * q + 256]
        total = jnp.zeros((steps, 256), F32)
        for b in range(4):
            h = 4 * q + b
            weights = jnp.exp(
                jnp.where(causal, cum[0, :, h : h + 1] - cum_t[0, h : h + 1, :], -1e30)
            )
            scores = (dot_t(reads * lane_mask(256, STATE, h), keys) * weights).astype(BF16)
            decay_pairs[0, h] = weights.astype(BF16)
            pairs[0, h] = scores
            total += dot(scores, values * lane_mask(256, HEADP, b))
        mixed[0, :, 256 * q : 256 * q + 256] = total


def lift_kernel(
    mixed, ce, start, g, x1, w_out, g3, w_conv,
    z, gs, yd, x2, a3, r3, v, sq, cq, top, bottom,
    full,
):
    steps = x1.shape[1]
    unpack_state(start, full)
    y = (mixed[0] + dot(ce[0], full[...])) * READ_SCALE
    gate = g[0].astype(F32)
    sig = sigmoid(gate)
    active = gate * sig
    gs[0] = (active * READ_SCALE).astype(BF16)
    yd[0] = (y * sig * (1.0 + gate - active)).astype(BF16)
    gated = (y * active).astype(BF16)
    z[0] = gated
    after = x1[0] + dot(gated, w_out[...])
    x2[0] = after
    low, scale = norm(after, g3[...])
    a3[0] = low
    r3[0] = scale
    first = dot(low, w_conv[:, :D])
    sig = sigmoid(dot(low, w_conv[:, D:]))
    out = first * sig
    v[0] = out
    sq[0] = sig.astype(BF16)
    cq[0] = (out * (1.0 - sig)).astype(BF16)
    top[0] = out[:8, :]
    bottom[0] = out[steps - 8 :, :]


def fill_padded(padded, body, before, after, keep):
    steps = body.shape[1]
    row = pl.program_id(0)
    for i in range(D // 128):
        columns = slice(128 * i, 128 * i + 128)
        padded[i, :8, :] = before[0, :, columns] * keep[0, row]
        padded[i, 8 : 8 + steps, :] = body[0, :, columns]
        padded[i, 8 + steps :, :] = after[0, :, columns] * keep[1, row]


def depth_kernel(v, before, after, keep, taps, dc, sums, padded):
    steps = v.shape[1]
    fill_padded(padded, v, before, after, keep)
    total, square = [], []
    for at in range(0, D, 128):
        running = jnp.zeros((steps, 128), F32)
        for k in range(KERNEL):
            running += padded[at // 128, k + 1 : k + 1 + steps, :] * taps[k : k + 1, at : at + 128]
        dc[0, :, at : at + 128] = running
        total.append(jnp.sum(running, axis=0, keepdims=True))
        square.append(jnp.sum(running * running, axis=0, keepdims=True))
    accumulate(sums, jnp.concatenate([jnp.concatenate(total, axis=1), jnp.concatenate(square, axis=1)], axis=0))


def batch_stats(stats, count):
    middle = stats[0:1, :] / count
    return middle, lax.rsqrt(stats[1:2, :] / count - middle * middle + EPS)


def late_kernel(count):
    def kernel(
        dc, x2, og, stats, bn_gain, bn_shift, w_conv, g4, w3, w4, g5,
        out, e, a4, s4, gf, gh, ge, gx3, gbn, sums, ln4, ln5,
        slope,
    ):
        middle, inv = batch_stats(stats, count)
        unit = (dc[0] - middle) * inv
        batch = unit * bn_gain[...] + bn_shift[...]
        sig = sigmoid(batch)
        active = batch * sig
        conv_slope = sig * (1.0 + batch - active)
        active = active.astype(BF16)
        e[0] = active
        x3 = x2[0] + dot(active, w_conv[...])
        low, scale4 = norm(x3, g4[...])
        a4[0] = low
        total = jnp.zeros_like(x3)
        for at in range(0, FF, D):
            hidden = dot(low, w3[:, at : at + D])
            gate = sigmoid(hidden)
            active = hidden * gate
            slope[:, at : at + D] = (gate * (1.0 + hidden - active)).astype(BF16)
            active = active.astype(BF16)
            s4[0, :, at : at + D] = active
            total += dot(active, w4[at : at + D, :])
        x4 = x3 + 0.5 * total
        centred = x4 - mean(x4)
        scale = lax.rsqrt(mean(centred * centred) + EPS)
        unit5 = centred * scale
        out[0] = (unit5 * g5[...]).astype(BF16)
        grad = og[0].astype(F32)
        both = grad * unit5
        inner = grad * g5[...]
        accumulate(ln5, jnp.sum(both, axis=0, keepdims=True))
        gx4 = scale * (inner - mean(inner) - unit5 * mean(inner * unit5))
        gf_low = (0.5 * gx4).astype(BF16)
        gf[0] = gf_low
        back = jnp.zeros_like(x3)
        for at in range(0, FF, D):
            hidden = (dot_t(gf_low, w4[at : at + D, :]) * slope[:, at : at + D].astype(F32)).astype(BF16)
            gh[0, :, at : at + D] = hidden
            back += dot_t(hidden, w3[:, at : at + D])
        back, gain4 = norm_back(back, low, scale4, g4[...])
        accumulate(ln4, gain4)
        grad3 = gx4 + back
        gx3[0] = grad3
        ge_low = grad3.astype(BF16)
        ge[0] = ge_low
        batch_grad = dot_t(ge_low, w_conv[...]) * conv_slope
        gbn[0] = batch_grad
        accumulate(
            sums,
            jnp.concatenate(
                [
                    jnp.sum(batch_grad * unit, axis=0, keepdims=True),
                    jnp.sum(batch_grad, axis=0, keepdims=True),
                ],
                axis=0,
            ),
        )

    return kernel


def batch_back(gbn, dc, stats, back, bn_gain, count):
    middle, inv = batch_stats(stats, count)
    unit = (dc - middle) * inv
    return bn_gain * inv * (gbn - (back[1:2, :] + unit * back[0:1, :]) / count)


def depth_grad_kernel(count):
    def kernel(gbn, dc, stats, back, bn_gain, v, before, after, keep, _, gd, taps_grad, padded):
        steps = v.shape[1]
        fill_padded(padded, v, before, after, keep)
        grad = batch_back(gbn[0], dc[0], stats, back, bn_gain[...], count)
        gd[0] = grad
        columns = []
        for at in range(0, D, 128):
            piece = gd[0, :, at : at + 128]
            rows = [
                jnp.sum(padded[at // 128, k + 1 : k + 1 + steps, :] * piece, axis=0, keepdims=True)
                for k in range(KERNEL)
            ]
            columns.append(jnp.concatenate(rows + [jnp.zeros((1, 128), F32)], axis=0))
        accumulate(taps_grad, jnp.concatenate(columns, axis=1))

    return kernel


def conv_back_kernel(
    gd, before, after, keep, taps, sq, cq, w_conv, a3, r3, g3, gx3, w_out, gs, yd, ce, block,
    gq, gx2, gz, gy, gg, pulled, ln3,
    padded,
):
    steps = gd.shape[1]
    fill_padded(padded, gd, before, after, keep)
    for at in range(0, D, 128):
        running = jnp.zeros((steps, 128), F32)
        for k in range(KERNEL):
            running += padded[at // 128, 15 - k : 15 - k + steps, :] * taps[k : k + 1, at : at + 128]
        gq[0, :, at : at + 128] = (running * sq[0, :, at : at + 128].astype(F32)).astype(BF16)
        gq[0, :, D + at : D + at + 128] = (running * cq[0, :, at : at + 128].astype(F32)).astype(BF16)
    back, gain = norm_back(dot_t(gq[0], w_conv[...]), a3[0], r3[0], g3[...])
    accumulate(ln3, gain)
    grad = gx3[0] + back
    gx2[0] = grad
    low = grad.astype(BF16)
    gz[0] = low
    inner = dot_t(low, w_out[...])
    gg[0] = (inner * yd[0].astype(F32)).astype(BF16)
    read_grad = (inner * gs[0].astype(F32)).astype(BF16)
    gy[0] = read_grad
    row = pl.program_id(0)
    for a, pair in enumerate(pack_state(t_dot(ce[0], read_grad))):
        pulled[0, STATE * a : STATE * (a + 1), :] = pair * keep[0, row]
    pulled[0, 4 * STATE :, :] = block[0, 4 * STATE :, :]


def mix_back_kernel(u, bs, c, ee, gy, start, pairs, decay_pairs, _, __, gu, gb, gc, full):
    steps = u.shape[1]
    unpack_state(start, full)
    reads_grad = dot_t(gy[0], full[...]) * ee[0].astype(F32)
    keys_grad = jnp.zeros((steps, 256), F32)
    keys = bs[0]
    reads = c[0]
    for q in range(2):
        values = u[0, :, 256 * q : 256 * q + 256]
        grads = gy[0, :, 256 * q : 256 * q + 256]
        total = jnp.zeros((steps, 256), F32)
        for b in range(4):
            h = 4 * q + b
            masked = grads * lane_mask(256, HEADP, b)
            scores = (dot_t(masked, values) * decay_pairs[0, h].astype(F32)).astype(BF16)
            mask = lane_mask(256, STATE, h)
            reads_grad += dot(scores, keys * mask)
            keys_grad += t_dot(scores, reads * mask)
            total += t_dot(pairs[0, h], masked)
        gu[0, :, 256 * q : 256 * q + 256] = total
    gc[0] = reads_grad.astype(BF16)
    gb[0] = keys_grad


def mix_end_kernel(
    end, u, bt, te, se, gu, gb, gc, gg, w_in, a2, r2, g2, gx2, _,
    gp, gx1, gf, ln2,
    full,
):
    unpack_state(end, full)
    gp[0, :, :D] = (gu[0] + dot(bt[0], full[...])).astype(BF16)
    gp[0, :, D : 2 * D] = gg[0]
    keys_grad = gb[0] + te[0].astype(F32) * dot_t(u[0], full[...])
    gp[0, :, 2 * D : 2 * D + 256] = (keys_grad * se[0].astype(F32)).astype(BF16)
    gp[0, :, 2 * D + 256 :] = gc[0]
    back, gain = norm_back(dot_t(gp[0], w_in[...]), a2[0], r2[0], g2[...])
    accumulate(ln2, gain)
    grad = gx2[0] + back
    gx1[0] = grad
    gf[0] = (0.5 * grad).astype(BF16)


def front_back_kernel(
    gx1, gf, w2, d1, w1, a1, r1, g1, w_sub, tk, fk, _,
    gh, gxr, fg, ln1,
):
    steps = gx1.shape[1]
    low = gf[0]
    back = jnp.zeros((steps, D), F32)
    for at in range(0, FF, D):
        hidden = (dot_t(low, w2[at : at + D, :]) * d1[0, :, at : at + D].astype(F32)).astype(BF16)
        gh[0, :, at : at + D] = hidden
        back += dot_t(hidden, w1[:, at : at + D])
    back, gain = norm_back(back, a1[0], r1[0], g1[...])
    accumulate(ln1, gain)
    low = (gx1[0] + back).astype(BF16)
    gxr[0] = low
    frames = dot(low, w_sub[...])
    mels = fk.shape[2]
    for j in range(SUB):
        fg[0, pl.ds(j, steps, stride=SUB), :] = frames[:, mels * j : mels * (j + 1)] * (
            tk[0][:, j : j + 1] * fk[0]
        )


def by_share_store(out, at, share, start, block):
    for piece in range(block.shape[0] // share):
        row = start + share * piece
        place = row // (4 * share) * share
        k = row % (4 * share) // share
        out[place : place + share, at + D * k : at + D * (k + 1)] = block[
            share * piece : share * (piece + 1), :
        ]


def late_weights_kernel(share):
    def kernel(a4, e, s4, gh, ge, gf, out):
        left = a4[...].T
        for at in range(0, FF, D):
            out[:, at : at + D] = dot(left, gh[:, at : at + D])
        for at in range(0, 1024, 256):
            by_share_store(out, FF, share, at, dot(s4[:, at : at + 256].T, gf[...]))
        out[:, 2 * FF :] = dot(e[...].T, ge[...])

    return kernel


def turned(place, share, core, block):
    rows = block.T
    half = rows.shape[0] // 2
    for s in range(rows.shape[0] // share):
        side = core if s % 2 == 0 else 1 - core
        at = pl.multiple_of(side * half + s // 2 * share, 16)
        place[pl.ds(at, share), :] = rows[s * share : (s + 1) * share, :]


def turned_by_share(place, share, core, block):
    for at in range(0, block.shape[1], 256):
        rows = block[:, at : at + 256].T
        for piece in range(256 // share):
            row = at + share * piece
            s, k = row // (4 * share), row % (4 * share) // share
            side = core if s % 2 == 0 else 1 - core
            to = pl.multiple_of(side * (D // 2) + D * k + s // 2 * share, 16)
            place[pl.ds(to, share), :] = rows[share * piece : share * (piece + 1), :]


def weights_kernel(pairs, share, waits, cuts):
    has_small = pairs[-1] == (1, 0)

    def kernel(core_ref, *refs):
        count = len(pairs)
        lefts, rights = refs[:count], refs[count : 2 * count]
        lines = refs[2 * count : 2 * count + 6 * has_small]
        kept, *sents = refs[2 * count + 6 * has_small + waits :][: len(cuts)]
        places = refs[2 * count + 6 * has_small + waits + len(cuts) :]

        def send(change):
            for sent, low, high in zip(sents, cuts, cuts[1:]):
                pl.when((step >= low) & (step < high))(lambda sent=sent: change(sent))

        step = pl.program_id(0)
        core = core_ref[0]
        start = 0
        for (wide, long), left, right, place in zip(pairs, lefts, rights, places[:count]):
            steps = max(wide, long)

            @pl.when(step == start)
            def _(left=left, place=place, wide=wide):
                if wide == 1:
                    turned(place, share, core, left[...])
                else:
                    turned_by_share(place, share, core, left)

            @pl.when((step >= start) & (step < start + steps))
            def _(right=right, place=place, wide=wide, start=start):
                if wide == 1:
                    rows = place[...]
                else:
                    rows = place[pl.ds(pl.multiple_of((step - start) * D, D), D), :]
                block = dot(rows, right[...])
                kept[...] = block[: D // 2, :]

                def put(sent):
                    sent[...] = block[D // 2 :, :]

                send(put)

            start += steps
        if has_small:

            @pl.when(step == start - 1)
            def _():
                stacked = jnp.concatenate([line[...] for line in lines] + [jnp.zeros((107, D), F32)], axis=0)
                places[-1][...] = stacked.T
                for s in range(D // share // 2):
                    for out, side in ((kept, core), (sents[-1], 1 - core)):
                        at = pl.multiple_of((2 * s + side) * share, 8)
                        out[s * share : (s + 1) * share, D - 128 :] = places[-1][pl.ds(at, share), :]

    return kernel


def weight_sums(pairs, share, core, small=None, after=(), pieces=1):
    tokens = pairs[0][0].shape[0]
    sizes = [(l.shape[1] // D, r.shape[1] // D) for l, r in pairs]
    if small is not None:
        sizes[-1] = (1, 0)
    lefts, rights, start = [], [], 0
    for (left, right), (wide, long) in zip(pairs, sizes):
        steps = max(wide, long)
        lefts.append((left, "all"))
        if wide == 1 and long > 1:
            index = lambda j, start=start, last=steps - 1: (0, jnp.clip(j - start, 0, last))
            rights.append((right, pl.BlockSpec((tokens, D), index)))
        else:
            rights.append((right, "all"))
        start += steps
    columns = start * D
    extra = [] if small is None else [(line, "all") for line in small]
    cuts = [start * i // pieces for i in range(pieces + 1)]

    def half(low, high):
        index = lambda j: (0, jnp.clip(j - low, 0, high - low - 1))
        return ((D // 2, D * (high - low)), F32, pl.BlockSpec((D // 2, D), index))

    kept, *sent, token = call(
        weights_kernel(sizes, share, len(after), cuts),
        (start,),
        [(core, scalars())] + lefts + rights + extra + [(a, anywhere()) for a in after],
        [half(0, start)] + [half(low, high) for low, high in zip(cuts, cuts[1:])],
        [pltpu.VMEM((D * wide, tokens), BF16) for wide, _ in sizes]
        + [pltpu.VMEM((D, 128), F32)] * (small is not None),
        2 * tokens * D * columns,
        "weights",
    )
    return kept, sent, token


def row_spec(shape):
    rest = len(shape) - 1
    return pl.BlockSpec((1,) + tuple(shape[1:]), lambda r: (r,) + (0,) * rest)


def whole_spec(shape):
    return pl.BlockSpec(tuple(shape), lambda r: (0,) * len(shape))


def held_spec(shape):
    return pl.BlockSpec(tuple(shape), lambda r: (0,) * len(shape), pipeline_mode=pl.Buffered(1))


def scalars():
    return pl.BlockSpec(memory_space=pltpu.SMEM)


def anywhere():
    return pl.BlockSpec(memory_space=pl.ANY)


ROOM = {'front': 44, 'mix': 24, 'lift': 28, 'depth': 20, 'late': 44, 'late_weights': 36, 'depth_grad': 20, 'conv_back': 28, 'mix_back': 28, 'mix_end': 24, 'front_back': 32, 'weights': 28}
TIMES = {'front': 60.0, 'mix': 21.0, 'lift': 27.0, 'depth': 18.0, 'late': 69.0, 'late_weights': 33.0, 'depth_grad': 21.0, 'conv_back': 33.0, 'mix_back': 36.0, 'mix_end': 30.0, 'front_back': 42.0, 'weights': 30.0}


def call(kernel, grid, ins, outs, scratch=(), flops=0, name=None):
    def placed(array, kind):
        if kind not in ("row", "all") and kind.memory_space is not None:
            return array
        return pltpu.with_memory_space_constraint(array, pltpu.HBM)

    def made(kind, shape):
        if kind == "row":
            return row_spec(shape)
        return whole_spec(shape) if kind == "all" else kind

    moved = sum(a.size * a.dtype.itemsize for a, _ in ins)
    inner = len(ins) + len(outs)

    def with_token(*refs):
        kernel(*refs[:inner], *refs[inner + 1 :])
        refs[inner][...] = jnp.zeros((8, 128), F32)

    *made_arrays, token = pl.pallas_call(
        with_token,
        grid=grid,
        in_specs=[held_spec(a.shape) if kind == "all" else made(kind, a.shape) for a, kind in ins],
        out_specs=[made(kind, shape) for shape, _, kind in outs] + [whole_spec((8, 128))],
        out_shape=[pltpu.HBM(shape, kind) for shape, kind, _ in outs] + [pltpu.HBM((8, 128), F32)],
        scratch_shapes=list(scratch),
        compiler_params=pltpu.CompilerParams(
            dimension_semantics=("arbitrary",), vmem_limit_bytes=ROOM[name] * 2**20
        ),
        cost_estimate=pl.CostEstimate(
            flops=int(TIMES[name] * 1.15e9), bytes_accessed=0, transcendentals=0
        ),
        name=name,
    )(*[placed(a, kind) for a, kind in ins])
    return (*made_arrays, token)


def flip_pairs(count, mask):
    return [(i, i ^ mask) for i in range(count)]


def hop_kernel(backward, first, keep_state):
    def kernel(keep, second_ref, value, other, *refs):
        before, (out, out_before, token) = (None, refs) if first else (refs[0], refs[1:])
        token[...] = jnp.zeros((8, 128), F32)
        second = (second_ref[0] != 0) != backward
        rows = value.shape[0]
        decay_rows = slice(4 * STATE, 4 * STATE + 8)
        for r in range(rows):
            here, there = value[r, decay_rows, :], other[r, decay_rows, :]
            out[r, decay_rows, :] = here * there
            if first:
                entered = jnp.where(second, there, 1.0)
            else:
                entered = before[r, decay_rows, :]
                entered = jnp.where(second, entered * there, entered)
            out_before[r, decay_rows, :] = entered
            for a in range(4):
                at = slice(STATE * a, STATE * (a + 1))
                mine, others = value[r, at, :], other[r, at, :]
                mine_decay, other_decay = here[a : a + 1, :], there[a : a + 1, :]
                out[r, at, :] = jnp.where(
                    second, mine_decay * others + mine, other_decay * mine + others
                )
                if first:
                    entered = jnp.where(second, others, 0.0)
                else:
                    entered = before[r, at, :]
                    own = before[r, 4 * STATE + a : 4 * STATE + a + 1, :]
                    entered = jnp.where(second, own * others + entered, entered)
                out_before[r, at, :] = entered * keep[0, r] if keep_state else entered

    return kernel


def entering(value, backward, keep):
    count, place = lax.axis_size("seq"), lax.axis_index("seq")
    vmem = pl.BlockSpec(memory_space=pltpu.VMEM)
    shape = jax.ShapeDtypeStruct(value.shape, F32)
    before, tokens = [], []
    for bit in range(count.bit_length() - 1):
        other = lax.ppermute(value, "seq", flip_pairs(count, 1 << bit))
        last = (2 << bit) == count
        value, entered, token = pl.pallas_call(
            hop_kernel(backward, bit == 0, last and not backward),
            in_specs=[scalars(), scalars()] + [vmem] * (2 + len(before)),
            out_specs=[vmem] * 3,
            out_shape=[shape, shape, jax.ShapeDtypeStruct((8, 128), F32)],
            compiler_params=pltpu.CompilerParams(vmem_limit_bytes=8 * 2**20),
            cost_estimate=pl.CostEstimate(flops=0, bytes_accessed=0, transcendentals=0),
            name="hop",
        )(keep, ((place >> bit) & 1).reshape(1), value, other, *before)
        before = [entered]
        tokens.append(token)
    return before[0], tokens


def halos(top, bottom):
    count = lax.axis_size("seq")
    ends = range(count - 1)
    return (
        lax.ppermute(bottom, "seq", [(i, i + 1) for i in ends]),
        lax.ppermute(top, "seq", [(i + 1, i) for i in ends]),
    )


def sum_over_all(value):
    count = lax.axis_size("seq") * lax.axis_size("rec")
    copies = jnp.broadcast_to(value[None], (count,) + value.shape)
    return jnp.sum(lax.all_to_all(copies, ("rec", "seq"), 0, 0), axis=0)


def scatter_sum(value):
    return lax.psum_scatter(value, "seq", scatter_dimension=0, tiled=True)


def in_vmem(kernel, scalars_in, ins, outs, after, name, cost=0):
    vmem = pl.BlockSpec(memory_space=pltpu.VMEM)
    return pl.pallas_call(
        kernel,
        in_specs=[scalars()] + [vmem] * len(ins) + [anywhere()] * len(after),
        out_specs=[vmem] * len(outs) + [vmem],
        out_shape=[jax.ShapeDtypeStruct(shape, F32) for shape in outs + [(8, 128)]],
        compiler_params=pltpu.CompilerParams(vmem_limit_bytes=8 * 2**20),
        cost_estimate=pl.CostEstimate(
            flops=int(cost * 1.15e9), bytes_accessed=0, transcendentals=0
        ),
        name=name,
    )(scalars_in, *ins, *after)


def part_rows(ref, group, chunk, side, columns):
    if chunk % 8:
        low = ref[2 * group * chunk : (2 * group + 1) * chunk, columns]
        high = ref[(2 * group + 1) * chunk : (2 * group + 2) * chunk, columns]
        return jnp.where(side == 0, low, high)
    return ref[pl.ds(pl.multiple_of((2 * group + side) * chunk, 8), chunk), columns]


def split_task(groups):
    arrays, outs, plan = [], [], []

    def known(array):
        for i, other in enumerate(arrays):
            if other is array:
                return i
        arrays.append(array)
        return len(arrays) - 1

    for items, chunk, bit in groups:
        rows = items[0][0].shape[0]
        placed, at = [], 0
        for kept, first, received, other_first, columns in items:
            there = None if received is None else known(received)
            placed.append((known(kept), first, there, other_first, columns, at))
            at += columns
        plan.append((placed, rows, chunk, bit, len(outs)))
        outs += [(rows // 2, at)] * 2

    def body(bit_ref, ins, made):
        for placed, rows, chunk, bit, out in plan:
            mine = bit_ref[bit]
            for kept, first, received, other_first, columns, at in placed:
                mine_at = slice(first, first + columns)
                other_at = slice(other_first, other_first + columns)
                for target, side in ((made[out], mine), (made[out + 1], 1 - mine)):
                    for group in range(rows // chunk // 2):
                        value = part_rows(ins[kept], group, chunk, side, mine_at)
                        if received is not None:
                            value = value + part_rows(ins[received], group, chunk, side, other_at)
                        target[group * chunk : (group + 1) * chunk, at : at + columns] = value

    return arrays, outs, body


def add_task(kept, received):
    def body(_, ins, made):
        made[0][...] = ins[0][...] + ins[1][...]

    return [kept, received], [kept.shape], body


def join_task(mine, other, bit, pieces=None):
    rows, columns = mine.shape
    cuts = [(0, columns, False)] if pieces is None else pieces
    outs = [(8 * rows, D) if spread else (2 * rows, wide) for _, wide, spread in cuts]

    def body(bit_ref, ins, made):
        first = bit_ref[bit] == 0
        for target, (at, wide, spread) in zip(made, cuts):
            for k in range(4 if spread else 1):
                width = D if spread else wide
                left = ins[0][:, at + D * k : at + D * k + width]
                right = ins[1][:, at + D * k : at + D * k + width]
                start = 2 * rows * k
                target[start : start + rows, :] = jnp.where(first, left, right)
                target[start + rows : start + 2 * rows, :] = jnp.where(first, right, left)

    return [mine, other], outs, body


def together(bits, sums, after, cost=0):
    tasks = [one.step() for one in sums]
    arrays = [array for ins, _, _, _ in tasks for array in ins]
    outs = [shape for _, shapes, _, _ in tasks for shape in shapes]
    count = len(arrays) + len(after)

    def kernel(bit_ref, *refs):
        at, out = 0, count
        for ins, shapes, body, _ in tasks:
            body(bit_ref, refs[at : at + len(ins)], refs[out : out + len(shapes)])
            at, out = at + len(ins), out + len(shapes)
        refs[-1][...] = jnp.zeros((8, 128), F32)

    *made, token = in_vmem(kernel, bits, arrays, outs, after, "together", cost)
    for _, shapes, _, commit in tasks:
        commit(made[: len(shapes)])
        made = made[len(shapes) :]
    return token


class Sum:
    def __init__(self, pieces):
        self.pieces = pieces
        self.chip_bits = lax.axis_size("seq").bit_length() - 2
        self.rec_bits = lax.axis_size("rec").bit_length() - 1
        self.parts, self.left, self.steps, self.beside = [], [], [], []
        self.done = None

    def swap(self, value, axis, bit):
        return lax.ppermute(value, axis, flip_pairs(lax.axis_size(axis), 1 << bit))

    def begin(self, kept, sent, first):
        self.parts = [[], []]
        at = 0
        for piece in sent:
            received = self.swap(piece, "seq", 0)
            end = at + piece.shape[1]
            for part, low, high in ((0, at, min(end, first)), (1, max(at, first), end)):
                if low < high:
                    self.parts[part].append((kept, low, received, low - at, high - low))
            at = end
        turn = 1 + self.chip_bits // 2
        orders = (
            list(range(1, self.chip_bits + 1)),
            list(range(turn, self.chip_bits + 1)) + list(range(1, turn)),
        )
        self.left = [list(range(self.chip_bits, 0, -1)) for _ in orders]
        self.steps += [("chips", now) for now in zip(*orders)]
        self.steps += [("rec", bit) for bit in range(self.rec_bits)] + [("turn", self.rec_bits - 1)]
        self.steps += [("join", bit) for bit in reversed(range(self.rec_bits))]

    def step(self):
        kind, now = self.steps.pop(0)
        if kind == "chips":
            groups = []
            for items, bit, left in zip(self.parts, now, self.left):
                chunk = items[0][0].shape[0] >> (left.index(bit) + 1)
                left.remove(bit)
                groups.append((items, chunk, bit))

            def commit(made):
                self.parts = [
                    [(made[2 * i], 0, self.swap(made[2 * i + 1], "seq", bit), 0, made[2 * i].shape[1])]
                    for i, bit in enumerate(now)
                ]

            return *split_task(groups), commit
        if kind == "rec":
            items = [item for part in self.beside + self.parts for item in part]
            self.beside = []

            def commit(made):
                kept, sent = made
                self.parts = [[(kept, 0, self.swap(sent, "rec", now), 0, kept.shape[1])]]

            chunk = items[0][0].shape[0] // 2
            return *split_task([(items, chunk, self.chip_bits + 1 + now)]), commit
        if kind == "turn":
            [[(kept, _, received, _, _)]] = self.parts

            def commit(made):
                [self.mine] = made
                self.other = self.swap(self.mine, "rec", now)

            return *add_task(kept, received), commit

        def commit(made):
            if now == 0:
                self.done = made
                return
            [self.mine] = made
            self.other = self.swap(self.mine, "rec", now - 1)

        pieces = self.pieces if now == 0 else None
        return *join_task(self.mine, self.other, self.chip_bits + 1 + now, pieces), commit


def local(
    features, time_keep, freq_keep, block_flags, decays, w_sub, ln1_gain, ffn1_in, ffn1_out, ln2_gain,
    ssm_in, ssm_out, ln3_gain, conv_in, conv_depth, bn_gain, bn_shift, conv_out, ln4_gain, ffn2_in,
    ffn2_out, ln5_gain, out_grad,
):
    rows, frame_count, mels = features.shape
    steps = frame_count // SUB
    tokens = rows * steps
    blocks = lax.axis_size("seq")
    place = lax.axis_index("seq")
    count = float(tokens * blocks * lax.axis_size("rec"))
    share = D // blocks
    here = lax.dynamic_index_in_dim(block_flags, place, 1, keepdims=False)
    after = lax.dynamic_index_in_dim(
        block_flags, jnp.minimum(place + 1, blocks - 1), 1, keepdims=False
    )
    keep_here = (1 - here).astype(F32)
    keep_next = jnp.where(place + 1 < blocks, 1 - after, 0).astype(F32)
    keep = (jnp.stack([keep_here, keep_next]), scalars())
    tk = (time_keep.reshape(rows, steps, SUB).astype(F32), "row")
    fk = (freq_keep[:, None, :].astype(F32), "row")
    g1, g2, g3, g4, g5, bg, bb = (
        (gain.reshape(1, D), "all")
        for gain in (ln1_gain, ln2_gain, ln3_gain, ln4_gain, ln5_gain, bn_gain, bn_shift)
    )
    taps = (jnp.pad(conv_depth.T, ((0, 1), (0, 0))), "all")

    def rows_of(width, kind=F32):
        return ((rows, steps, width), kind, "row")


    per_state = ((rows, 4 * STATE + 8, 128), F32, "row")
    edge = ((rows, 8, D), F32, "row")
    line = ((1, D), F32, "all")
    two_lines = ((2, D), F32, "all")
    padded = pltpu.VMEM((D // 128, steps + 16, 128), F32)
    full = pltpu.VMEM((256, D), BF16)

    def row(value):
        return (value, "row")

    def every(value):
        return (value, "all")

    (flat, x1, a1, r1, s1, d1, a2, r2, u, g, bs, c, ce, bt, se, ee, te, cum, cum_t, state, _) = call(
        front_kernel,
        (rows,),
        [
            row(features), tk, fk, row(decays), row(decays.transpose(0, 2, 1)), keep,
            every(w_sub), g1, every(ffn1_in), every(ffn1_out), g2, every(ssm_in),
        ],
        [
            rows_of(WIDE, BF16), rows_of(D), rows_of(D, BF16), rows_of(1), rows_of(FF, BF16),
            rows_of(FF, BF16), rows_of(D, BF16), rows_of(1), rows_of(D, BF16), rows_of(D, BF16),
            rows_of(256, BF16), rows_of(256, BF16), rows_of(256, BF16), rows_of(256, BF16),
            rows_of(256, BF16), rows_of(256, BF16), rows_of(256, BF16), rows_of(HEADS),
            ((rows, HEADS, steps), F32, "row"), per_state,
        ],
        [pltpu.VMEM((frame_count, mels), F32)],
        2 * tokens * D * (WIDE + 2 * FF + PROJ),
        "front",
    )
    start, _ = entering(state, False, keep[0])
    pair_shape = ((rows, HEADS, steps, steps), BF16, "row")
    mixed, pairs, decay_pairs, _ = call(
        mix_kernel,
        (rows,),
        [row(u), row(bs), row(c), row(cum), row(cum_t)],
        [rows_of(D), pair_shape, pair_shape],
        (),
        2 * tokens * 256 * 256 * 16,
        "mix",
    )
    z, gs, yd, x2, a3, r3, v, sq, cq, top, bottom, _ = call(
        lift_kernel,
        (rows,),
        [row(mixed), row(ce), row(start), row(g), row(x1), every(ssm_out), g3, every(conv_in)],
        [
            rows_of(D, BF16), rows_of(D, BF16), rows_of(D, BF16), rows_of(D), rows_of(D, BF16),
            rows_of(1), rows_of(D), rows_of(D, BF16), rows_of(D, BF16), edge, edge,
        ],
        [full],
        2 * tokens * D * 4 * D,
        "lift",
    )
    v_before, v_after = halos(top, bottom)
    dc, sums, _ = call(
        depth_kernel,
        (rows,),
        [row(v), row(v_before), row(v_after), keep, taps],
        [rows_of(D), two_lines],
        [padded],
        2 * tokens * D * 64,
        "depth",
    )
    stats = sum_over_all(sums)
    out, e, a4, s4, gf4, gh4, ge, gx3, gbn, back_sums, ln4, ln5, _ = call(
        late_kernel(count),
        (rows,),
        [
            row(dc), row(x2), row(out_grad), every(stats), bg, bb, every(conv_out), g4,
            every(ffn2_in), every(ffn2_out), g5,
        ],
        [
            rows_of(D, BF16), rows_of(D, BF16), rows_of(D, BF16), rows_of(FF, BF16), rows_of(D, BF16),
            rows_of(FF, BF16), rows_of(D, BF16), rows_of(D), rows_of(D), two_lines, line, line,
        ],
        [pltpu.VMEM((steps, FF), BF16)],
        2 * tokens * D * (4 * FF + 2 * D),
        "late",
    )
    back = sum_over_all(back_sums)

    def flatten(value):
        return value.reshape(tokens, value.shape[-1])

    def column_block(value, width):
        return (flatten(value), pl.BlockSpec((tokens, width), lambda i: (0, i)))

    def row_block(columns):
        return ((D, columns), F32, pl.BlockSpec((256, columns), lambda i: (i, 0)))

    late_grads, late_token = call(
        late_weights_kernel(share),
        (2,),
        [
            column_block(a4, 256), column_block(e, 256), column_block(s4, 1024),
            every(flatten(gh4)), every(flatten(ge)), every(flatten(gf4)),
        ],
        [row_block(2 * FF + D)],
        (),
        2 * tokens * D * (2 * FF + D),
        "late_weights",
    )
    scattered_a = scatter_sum(late_grads)

    def edge_grad(at):
        return batch_back(
            lax.slice_in_dim(gbn, at, at + 8, axis=1),
            lax.slice_in_dim(dc, at, at + 8, axis=1),
            stats, back, bn_gain, count,
        )

    gd_before, gd_after = halos(edge_grad(0), edge_grad(steps - 8))
    gd, taps_grad, _ = call(
        depth_grad_kernel(count),
        (rows,),
        [
            row(gbn), row(dc), every(stats), every(back), bg, row(v), row(v_before), row(v_after), keep,
            (late_token, anywhere()),
        ],
        [rows_of(D), ((16, D), F32, "all")],
        [padded],
        2 * tokens * D * 64,
        "depth_grad",
    )
    gq, gx2, gz, gy, gg, pulled, ln3, _ = call(
        conv_back_kernel,
        (rows,),
        [
            row(gd), row(gd_before), row(gd_after), keep, taps, row(sq), row(cq), every(conv_in),
            row(a3), row(r3), g3, row(gx3), every(ssm_out), row(gs), row(yd), row(ce), row(state),
        ],
        [
            rows_of(2 * D, BF16), rows_of(D), rows_of(D, BF16), rows_of(D, BF16), rows_of(D, BF16),
            per_state, line,
        ],
        [padded],
        2 * tokens * D * 4 * D,
        "conv_back",
    )
    end, hops = entering(pulled, True, keep[0])
    core = (place % 2).reshape(1)
    kept, sent, weights_token = weight_sums(
        [(flatten(a3), flatten(gq)), (flatten(z), flatten(gz))], share, core, None, hops[:-2]
    )
    bits = jnp.stack(
        [(place >> k) & 1 for k in range(blocks.bit_length() - 1)]
        + [(lax.axis_index("rec") >> k) & 1 for k in range(lax.axis_size("rec").bit_length() - 1)]
    )
    early = Sum(
        [
            (0, FF, False), (FF, FF, True), (2 * FF, D, False), (2 * FF + D, 2 * D, False),
            (2 * FF + 3 * D, D, False),
        ],
    )
    early.begin(kept, sent, D)
    gu, gb, gc, mixed_token = call(
        mix_back_kernel,
        (rows,),
        [
            row(u), row(bs), row(c), row(ee), row(gy), row(start), row(pairs), row(decay_pairs),
            (weights_token, anywhere()), (hops[-2], anywhere()),
        ],
        [rows_of(D), rows_of(256), rows_of(256, BF16)],
        [full],
        2 * tokens * 256 * 256 * 32,
        "mix_back",
    )
    token = together(bits, [early], [mixed_token])
    gp, gx1, gf1, ln2, end_token = call(
        mix_end_kernel,
        (rows,),
        [
            row(end), row(u), row(bt), row(te), row(se), row(gu), row(gb), row(gc), row(gg),
            every(ssm_in), row(a2), row(r2), g2, row(gx2), (token, anywhere()),
        ],
        [rows_of(PROJ, BF16), rows_of(D), rows_of(D, BF16), line],
        [full],
        2 * tokens * D * PROJ,
        "mix_end",
    )
    token = together(bits, [early], [end_token])
    kept, sent, weights_token = weight_sums(
        [(flatten(a2), flatten(gp)), (flatten(s1), flatten(gf1))], share, core, None, [token]
    )
    middle = Sum([(0, PROJ, False), (PROJ, FF, True)])
    middle.begin(kept, sent, PROJ)
    token = weights_token
    while early.steps[0][0] == "chips":
        token = together(bits, [early], [token])
    early.parts = [[(scattered_a, 0, None, 0, scattered_a.shape[1])]] + early.parts
    token = together(bits, [early], [token])
    gh1, gxr, features_grad, ln1, back_token = call(
        front_back_kernel,
        (rows,),
        [
            row(gx1), row(gf1), every(ffn1_out), row(d1), every(ffn1_in), row(a1), row(r1), g1,
            every(w_sub), tk, fk, (token, anywhere()),
        ],
        [rows_of(FF, BF16), rows_of(D, BF16), ((rows, frame_count, mels), F32, "row"), line],
        (),
        2 * tokens * D * (WIDE + 2 * FF),
        "front_back",
    )
    small = [taps_grad, ln1, ln2, ln3, ln4, ln5]
    token = together(bits, [early, middle], [back_token])
    last = Sum([(0, FF, False), (FF, SUB * mels, False), (FF + D - 128, 128, False)])
    kept, sent, weights_token = weight_sums(
        [(flatten(a1), flatten(gh1)), (flatten(gxr), flatten(flat))], share, core, small, [token], 1
    )
    last.begin(kept, sent, 2 * D)
    token = weights_token
    token = together(bits, [early, middle], [token], 60.0)
    rounds = [(last,), (early, middle, last), (middle, last)]
    while early.steps or middle.steps or last.steps:
        now = rounds.pop(0) if rounds else (early, middle, last)
        now = [one for one in now if one.steps]
        if now:
            token = together(bits, now, [token])
    ffn2_in_grad, ffn2_out_grad, conv_out_grad, conv_in_grad, ssm_out_grad = early.done
    ssm_in_grad, ffn1_out_grad = middle.done
    ffn1_in_grad, w_sub_grad, gains = last.done

    start_row = place * share
    return (
        out,
        features_grad,
        w_sub_grad,
        gains[:, 16],
        ffn1_in_grad,
        ffn1_out_grad,
        gains[:, 17],
        ssm_in_grad,
        ssm_out_grad,
        gains[:, 18],
        conv_in_grad,
        gains[:, :KERNEL],
        lax.dynamic_slice_in_dim(back[0], start_row, share),
        lax.dynamic_slice_in_dim(back[1], start_row, share),
        conv_out_grad,
        gains[:, 19],
        ffn2_in_grad,
        ffn2_out_grad,
        gains[:, 20],
    )


def solution(mesh):
    block = P("rec", "seq", None)
    rows_of_seq, line = P("seq", None), P("seq")
    return jax.shard_map(
        local,
        mesh=mesh,
        in_specs=(block, P("rec", "seq"), P("rec", None), P("rec", None), P("rec", None, "seq"))
        + (P(),) * 17
        + (block,),
        out_specs=(
            block, block, rows_of_seq, line, rows_of_seq, rows_of_seq, line, rows_of_seq, rows_of_seq,
            line, rows_of_seq, rows_of_seq, line, line, rows_of_seq, line, rows_of_seq, rows_of_seq, line,
        ),
        check_vma=False,
    )
```

```python
import jax
import jax.numpy as jnp
from jax import lax
from jax.experimental import pallas as pl
from jax.experimental.pallas import tpu as pltpu
from jax.sharding import PartitionSpec as P

D = 512
FF = 2048
HEADS = 8
STATE = 32
SUB = 4
KERNEL = 15
HEADP = 64
PROJ = 1536
WIDE = 512
EPS = 1e-05
F32 = jnp.float32
BF16 = jnp.bfloat16
LIMIT = 32
READ_SCALE = STATE ** (-0.5)


def dot(a, b):
    return lax.dot_general(a, b, (((1,), (0,)), ((), ())), preferred_element_type=F32)


def dot_t(a, b):
    return lax.dot_general(a, b, (((1,), (1,)), ((), ())), preferred_element_type=F32)


def t_dot(a, b):
    return lax.dot_general(a, b, (((0,), (0,)), ((), ())), preferred_element_type=F32)


def sigmoid(x):
    return 0.5 * jnp.tanh(0.5 * x) + 0.5


def mean(x):
    return jnp.mean(x, axis=-1, keepdims=True)


def norm(x, gain):
    centred = x - mean(x)
    scale = lax.rsqrt(mean(centred * centred) + EPS)
    return (centred * scale * gain).astype(BF16), scale


def norm_back(grad, normed, scale, gain):
    wide = normed.astype(F32)
    inverse = 1.0 / gain
    both = grad * wide
    inner = grad * gain
    back = scale * (inner - mean(inner) - wide * inverse * mean(both))
    return back, jnp.sum(both, axis=0, keepdims=True) * inverse


def split_two(x):
    high = x.astype(BF16)
    return high, (x - high.astype(F32)).astype(BF16)


def split_three(x):
    high, rest = split_two(x)
    return high, rest, (x - high.astype(F32) - rest.astype(F32)).astype(BF16)


def iota(shape, dim):
    return lax.broadcasted_iota(jnp.int32, shape, dim)


def lane_mask(columns, width, index):
    lane = iota((16, columns), 1)
    inside = (lane >= width * index) & (lane < width * (index + 1))
    return jnp.where(inside, 1.0, 0.0).astype(BF16)[:1]


def pack_state(full):
    lane = iota((STATE, 128), 1)
    return [
        jnp.where(
            lane < HEADP,
            full[64 * a : 64 * a + 32, 128 * a : 128 * a + 128],
            full[64 * a + 32 : 64 * a + 64, 128 * a : 128 * a + 128],
        )
        for a in range(4)
    ]


def unpack_state(ref, full):
    lane = iota((STATE, 128), 1)
    full[...] = jnp.zeros_like(full)
    for a in range(4):
        pair = ref[0, STATE * a : STATE * (a + 1), :]
        full[64 * a : 64 * a + 32, 128 * a : 128 * a + 128] = jnp.where(
            lane < HEADP, pair, 0.0
        ).astype(BF16)
        full[64 * a + 32 : 64 * a + 64, 128 * a : 128 * a + 128] = jnp.where(
            lane < HEADP, 0.0, pair
        ).astype(BF16)


def accumulate(ref, value):
    first = pl.program_id(0) == 0

    @pl.when(first)
    def _():
        ref[...] = value

    @pl.when(jnp.logical_not(first))
    def _():
        ref[...] += value


def front_kernel(
    feat, tk, fk, dec, keep, w_sub, g1, w1, w2, g2, w_in,
    flat, x1, a1, r1, s1, d1, a2, r2, u, g, bs, c, ce, bt, se, ee, te, cum, cum_t, state,
    frames,
):
    steps = x1.shape[1]
    here = pl.ds(pl.program_id(0), 1)
    kept = feat[0].astype(F32) * tk[here, :].astype(F32)
    frames[...] = kept.T * fk[here, :].astype(F32)
    parts = [frames[pl.ds(j, steps, stride=SUB), :] for j in range(SUB)]
    parts.append(jnp.zeros((steps, WIDE - SUB * parts[0].shape[1]), F32))
    stacked = jnp.concatenate(parts, axis=1).astype(BF16)
    flat[0] = stacked
    x0 = dot(stacked[:, : w_sub.shape[0]], w_sub[...])
    low, scale = norm(x0, g1[...])
    a1[0] = low
    r1[0] = scale
    total = jnp.zeros((steps, D), F32)
    for at in range(0, FF, D):
        hidden = dot(low, w1[:, at : at + D])
        gate = sigmoid(hidden)
        active = hidden * gate
        d1[0, :, at : at + D] = (gate * (1.0 + hidden - active)).astype(BF16)
        active = active.astype(BF16)
        s1[0, :, at : at + D] = active
        total += dot(active, w2[at : at + D, :])
    after = x0 + 0.5 * total
    x1[0] = after
    low, scale = norm(after, g2[...])
    a2[0] = low
    r2[0] = scale
    u_low = dot(low, w_in[:, :D]).astype(BF16)
    u[0] = u_low
    g[0] = dot(low, w_in[:, D : 2 * D]).astype(BF16)
    keys = dot(low, w_in[:, 2 * D : 2 * D + 256])
    reads = dot(low, w_in[:, 2 * D + 256 :])
    log_rows = jnp.log(dec[0])
    log_decay = log_rows.T
    lower = jnp.where(iota((steps, steps), 0) >= iota((steps, steps), 1), 1.0, 0.0).astype(BF16)
    running = sum(dot(lower, part) for part in split_three(log_decay))
    running_t = sum(dot_t(part, lower) for part in split_three(log_rows))
    cum[0] = running
    cum_t[0] = running_t
    spread = jnp.where(iota((HEADS, 256), 1) // STATE == iota((HEADS, 256), 0), 1.0, 0.0).astype(BF16)

    def over_columns(value):
        return sum(dot(part, spread) for part in split_two(value))

    scale_wide = over_columns(jnp.sqrt(-2.0 * log_decay))
    head = jnp.exp(running)
    head_wide = over_columns(head)
    tail_wide = over_columns(jnp.exp(running[steps - 1 :, :] - running))
    se[0] = scale_wide.astype(BF16)
    ee[0] = head_wide.astype(BF16)
    te[0] = tail_wide.astype(BF16)
    keys = keys * scale_wide
    bs[0] = keys.astype(BF16)
    c[0] = reads.astype(BF16)
    ce[0] = (reads * head_wide).astype(BF16)
    tailed = (keys * tail_wide).astype(BF16)
    bt[0] = tailed
    spread_values = jnp.where(iota((HEADS, D), 1) // HEADP == iota((HEADS, D), 0), 1.0, 0.0).astype(BF16)
    block = sum(dot(part, spread_values) for part in split_three(head[steps - 8 :, :]))
    block = block[7:8, :] * keep[0, pl.program_id(0)]
    for a, pair in enumerate(pack_state(t_dot(tailed, u_low))):
        state[0, STATE * a : STATE * (a + 1), :] = pair
    lines = [block[:, 128 * a : 128 * a + 128] for a in range(4)]
    state[0, 4 * STATE :, :] = jnp.concatenate(lines + lines, axis=0)


def mix_kernel(u, bs, c, cum, cum_t, mixed, pairs, decay_pairs):
    steps = u.shape[1]
    causal = iota((steps, steps), 0) >= iota((steps, steps), 1)
    keys = bs[0]
    reads = c[0]
    for q in range(2):
        values = u[0, :, 256 * q : 256 * q + 256]
        total = jnp.zeros((steps, 256), F32)
        for b in range(4):
            h = 4 * q + b
            weights = jnp.exp(
                jnp.where(causal, cum[0, :, h : h + 1] - cum_t[0, h : h + 1, :], -1e30)
            )
            scores = (dot_t(reads * lane_mask(256, STATE, h), keys) * weights).astype(BF16)
            decay_pairs[0, h] = weights.astype(BF16)
            pairs[0, h] = scores
            total += dot(scores, values * lane_mask(256, HEADP, b))
        mixed[0, :, 256 * q : 256 * q + 256] = total


def lift_kernel(
    mixed, ce, start, g, x1, w_out, g3, w_conv,
    z, gs, yd, x2, a3, r3, v, sq, cq, top, bottom,
    full,
):
    steps = x1.shape[1]
    unpack_state(start, full)
    y = (mixed[0] + dot(ce[0], full[...])) * READ_SCALE
    gate = g[0].astype(F32)
    sig = sigmoid(gate)
    active = gate * sig
    gs[0] = (active * READ_SCALE).astype(BF16)
    yd[0] = (y * sig * (1.0 + gate - active)).astype(BF16)
    gated = (y * active).astype(BF16)
    z[0] = gated
    after = x1[0] + dot(gated, w_out[...])
    x2[0] = after
    low, scale = norm(after, g3[...])
    a3[0] = low
    r3[0] = scale
    first = dot(low, w_conv[:, :D])
    sig = sigmoid(dot(low, w_conv[:, D:]))
    out = first * sig
    v[0] = out
    sq[0] = sig.astype(BF16)
    cq[0] = (out * (1.0 - sig)).astype(BF16)
    top[0] = out[:8, :]
    bottom[0] = out[steps - 8 :, :]


def fill_padded(padded, body, before, after, keep):
    steps = body.shape[1]
    row = pl.program_id(0)
    for i in range(D // 128):
        columns = slice(128 * i, 128 * i + 128)
        padded[i, :8, :] = before[0, :, columns] * keep[0, row]
        padded[i, 8 : 8 + steps, :] = body[0, :, columns]
        padded[i, 8 + steps :, :] = after[0, :, columns] * keep[1, row]


def depth_kernel(v, before, after, keep, taps, dc, sums, padded):
    steps = v.shape[1]
    fill_padded(padded, v, before, after, keep)
    total, square = [], []
    for at in range(0, D, 128):
        running = jnp.zeros((steps, 128), F32)
        for k in range(KERNEL):
            running += padded[at // 128, k + 1 : k + 1 + steps, :] * taps[k : k + 1, at : at + 128]
        dc[0, :, at : at + 128] = running
        total.append(jnp.sum(running, axis=0, keepdims=True))
        square.append(jnp.sum(running * running, axis=0, keepdims=True))
    accumulate(sums, jnp.concatenate([jnp.concatenate(total, axis=1), jnp.concatenate(square, axis=1)], axis=0))


def batch_stats(stats, count):
    middle = stats[0:1, :] / count
    return middle, lax.rsqrt(stats[1:2, :] / count - middle * middle + EPS)


def late_kernel(count):
    def kernel(
        dc, x2, og, stats, bn_gain, bn_shift, w_conv, g4, w3, w4, g5,
        out, e, a4, s4, gf, gh, ge, gx3, gbn, sums, ln4, ln5,
        slope,
    ):
        middle, inv = batch_stats(stats, count)
        unit = (dc[0] - middle) * inv
        batch = unit * bn_gain[...] + bn_shift[...]
        sig = sigmoid(batch)
        active = batch * sig
        conv_slope = sig * (1.0 + batch - active)
        active = active.astype(BF16)
        e[0] = active
        x3 = x2[0] + dot(active, w_conv[...])
        low, scale4 = norm(x3, g4[...])
        a4[0] = low
        total = jnp.zeros_like(x3)
        for at in range(0, FF, D):
            hidden = dot(low, w3[:, at : at + D])
            gate = sigmoid(hidden)
            active = hidden * gate
            slope[:, at : at + D] = (gate * (1.0 + hidden - active)).astype(BF16)
            active = active.astype(BF16)
            s4[0, :, at : at + D] = active
            total += dot(active, w4[at : at + D, :])
        x4 = x3 + 0.5 * total
        centred = x4 - mean(x4)
        scale = lax.rsqrt(mean(centred * centred) + EPS)
        unit5 = centred * scale
        out[0] = (unit5 * g5[...]).astype(BF16)
        grad = og[0].astype(F32)
        both = grad * unit5
        inner = grad * g5[...]
        accumulate(ln5, jnp.sum(both, axis=0, keepdims=True))
        gx4 = scale * (inner - mean(inner) - unit5 * mean(inner * unit5))
        gf_low = (0.5 * gx4).astype(BF16)
        gf[0] = gf_low
        back = jnp.zeros_like(x3)
        for at in range(0, FF, D):
            hidden = (dot_t(gf_low, w4[at : at + D, :]) * slope[:, at : at + D].astype(F32)).astype(BF16)
            gh[0, :, at : at + D] = hidden
            back += dot_t(hidden, w3[:, at : at + D])
        back, gain4 = norm_back(back, low, scale4, g4[...])
        accumulate(ln4, gain4)
        grad3 = gx4 + back
        gx3[0] = grad3
        ge_low = grad3.astype(BF16)
        ge[0] = ge_low
        batch_grad = dot_t(ge_low, w_conv[...]) * conv_slope
        gbn[0] = batch_grad
        accumulate(
            sums,
            jnp.concatenate(
                [
                    jnp.sum(batch_grad * unit, axis=0, keepdims=True),
                    jnp.sum(batch_grad, axis=0, keepdims=True),
                ],
                axis=0,
            ),
        )

    return kernel


def batch_back(gbn, dc, stats, back, bn_gain, count):
    middle, inv = batch_stats(stats, count)
    unit = (dc - middle) * inv
    return bn_gain * inv * (gbn - (back[1:2, :] + unit * back[0:1, :]) / count)


def depth_grad_kernel(count):
    def kernel(gbn, dc, stats, back, bn_gain, v, before, after, keep, _, gd, taps_grad, padded):
        steps = v.shape[1]
        fill_padded(padded, v, before, after, keep)
        grad = batch_back(gbn[0], dc[0], stats, back, bn_gain[...], count)
        gd[0] = grad
        columns = []
        for at in range(0, D, 128):
            piece = gd[0, :, at : at + 128]
            rows = [
                jnp.sum(padded[at // 128, k + 1 : k + 1 + steps, :] * piece, axis=0, keepdims=True)
                for k in range(KERNEL)
            ]
            columns.append(jnp.concatenate(rows + [jnp.zeros((1, 128), F32)], axis=0))
        accumulate(taps_grad, jnp.concatenate(columns, axis=1))

    return kernel


def conv_back_kernel(
    gd, before, after, keep, taps, sq, cq, w_conv, a3, r3, g3, gx3, w_out, gs, yd, ce, block,
    gq, gx2, gz, gy, gg, pulled, ln3,
    padded,
):
    steps = gd.shape[1]
    fill_padded(padded, gd, before, after, keep)
    for at in range(0, D, 128):
        running = jnp.zeros((steps, 128), F32)
        for k in range(KERNEL):
            running += padded[at // 128, 15 - k : 15 - k + steps, :] * taps[k : k + 1, at : at + 128]
        gq[0, :, at : at + 128] = (running * sq[0, :, at : at + 128].astype(F32)).astype(BF16)
        gq[0, :, D + at : D + at + 128] = (running * cq[0, :, at : at + 128].astype(F32)).astype(BF16)
    back, gain = norm_back(dot_t(gq[0], w_conv[...]), a3[0], r3[0], g3[...])
    accumulate(ln3, gain)
    grad = gx3[0] + back
    gx2[0] = grad
    low = grad.astype(BF16)
    gz[0] = low
    inner = dot_t(low, w_out[...])
    gg[0] = (inner * yd[0].astype(F32)).astype(BF16)
    read_grad = (inner * gs[0].astype(F32)).astype(BF16)
    gy[0] = read_grad
    row = pl.program_id(0)
    for a, pair in enumerate(pack_state(t_dot(ce[0], read_grad))):
        pulled[0, STATE * a : STATE * (a + 1), :] = pair * keep[0, row]
    pulled[0, 4 * STATE :, :] = block[0, 4 * STATE :, :]


def mix_back_kernel(u, bs, c, ee, gy, start, pairs, decay_pairs, _, gu, gb, gc, full):
    steps = u.shape[1]
    unpack_state(start, full)
    reads_grad = dot_t(gy[0], full[...]) * ee[0].astype(F32)
    keys_grad = jnp.zeros((steps, 256), F32)
    keys = bs[0]
    reads = c[0]
    for q in range(2):
        values = u[0, :, 256 * q : 256 * q + 256]
        grads = gy[0, :, 256 * q : 256 * q + 256]
        total = jnp.zeros((steps, 256), F32)
        for b in range(4):
            h = 4 * q + b
            masked = grads * lane_mask(256, HEADP, b)
            scores = (dot_t(masked, values) * decay_pairs[0, h].astype(F32)).astype(BF16)
            mask = lane_mask(256, STATE, h)
            reads_grad += dot(scores, keys * mask)
            keys_grad += t_dot(scores, reads * mask)
            total += t_dot(pairs[0, h], masked)
        gu[0, :, 256 * q : 256 * q + 256] = total
    gc[0] = reads_grad.astype(BF16)
    gb[0] = keys_grad


def mix_end_kernel(
    end, u, bt, te, se, gu, gb, gc, gg, w_in, a2, r2, g2, gx2, _,
    gp, gx1, gf, ln2,
    full,
):
    unpack_state(end, full)
    gp[0, :, :D] = (gu[0] + dot(bt[0], full[...])).astype(BF16)
    gp[0, :, D : 2 * D] = gg[0]
    keys_grad = gb[0] + te[0].astype(F32) * dot_t(u[0], full[...])
    gp[0, :, 2 * D : 2 * D + 256] = (keys_grad * se[0].astype(F32)).astype(BF16)
    gp[0, :, 2 * D + 256 :] = gc[0]
    back, gain = norm_back(dot_t(gp[0], w_in[...]), a2[0], r2[0], g2[...])
    accumulate(ln2, gain)
    grad = gx2[0] + back
    gx1[0] = grad
    gf[0] = (0.5 * grad).astype(BF16)


def front_back_kernel(
    gx1, gf, w2, d1, w1, a1, r1, g1, w_sub, tk, fk, _,
    gh, gxr, fg, ln1,
    mel_rows,
):
    steps = gx1.shape[1]
    low = gf[0]
    back = jnp.zeros((steps, D), F32)
    for at in range(0, FF, D):
        hidden = (dot_t(low, w2[at : at + D, :]) * d1[0, :, at : at + D].astype(F32)).astype(BF16)
        gh[0, :, at : at + D] = hidden
        back += dot_t(hidden, w1[:, at : at + D])
    back, gain = norm_back(back, a1[0], r1[0], g1[...])
    accumulate(ln1, gain)
    low = (gx1[0] + back).astype(BF16)
    gxr[0] = low
    frames = dot_t(low, w_sub[...])
    mels = fk.shape[1]
    here = pl.ds(pl.program_id(0), 1)
    keep_mels = fk[here, :].astype(F32)
    for j in range(SUB):
        mel_rows[pl.ds(j, steps, stride=SUB), :] = frames[:, mels * j : mels * (j + 1)] * keep_mels
    fg[0] = mel_rows[...].T * tk[here, :].astype(F32)


def by_share_store(out, at, share, start, block):
    for piece in range(block.shape[0] // share):
        row = start + share * piece
        place = row // (4 * share) * share
        k = row % (4 * share) // share
        out[place : place + share, at + D * k : at + D * (k + 1)] = block[
            share * piece : share * (piece + 1), :
        ]


def late_weights_kernel(share):
    def kernel(a4, e, s4, gh, ge, gf, out):
        left = a4[...].T
        for at in range(0, FF, D):
            out[:, at : at + D] = dot(left, gh[:, at : at + D])
        for at in range(0, 1024, 256):
            by_share_store(out, FF, share, at, dot(s4[:, at : at + 256].T, gf[...]))
        out[:, 2 * FF :] = dot(e[...].T, ge[...])

    return kernel


def turned(place, share, core, block):
    rows = block.T
    half = rows.shape[0] // 2
    for s in range(rows.shape[0] // share):
        side = core if s % 2 == 0 else 1 - core
        at = pl.multiple_of(side * half + s // 2 * share, 16)
        place[pl.ds(at, share), :] = rows[s * share : (s + 1) * share, :]


def turned_by_share(place, share, core, block, at_block):
    for at in range(0, D, 256):
        rows = block[:, at : at + 256].T
        for piece in range(256 // share):
            here = at + share * piece
            first, k = here // (4 * share), here % (4 * share) // share
            side = core if first % 2 == 0 else 1 - core
            to = side * (D // 2) + D * k + (at_block * (D // (8 * share)) + first // 2) * share
            place[pl.ds(pl.multiple_of(to, 16), share), :] = rows[share * piece : share * (piece + 1), :]


def weights_kernel(pairs, share, waits, cuts):
    has_small = pairs[-1] == (1, 0)

    def kernel(core_ref, *refs):
        count = len(pairs)
        lefts, rights = refs[:count], refs[count : 2 * count]
        lines = refs[2 * count : 2 * count + 6 * has_small]
        kept, *sents = refs[2 * count + 6 * has_small + waits :][: len(cuts)]
        places = refs[2 * count + 6 * has_small + waits + len(cuts) :]

        def send(change):
            for sent, low, high in zip(sents, cuts, cuts[1:]):
                pl.when((step >= low) & (step < high))(lambda sent=sent: change(sent))

        step = pl.program_id(0)
        core = core_ref[0]
        start = 0
        for (wide, long), left, right, place in zip(pairs, lefts, rights, places[:count]):
            steps = max(wide, long)

            if wide == 1:

                @pl.when(step == start)
                def _(left=left, place=place):
                    turned(place, share, core, left[...])

            else:

                @pl.when((step > start - wide) & (step <= start))
                def _(left=left, place=place, before=start - wide + 1):
                    turned_by_share(place, share, core, left, step - before)

            @pl.when((step >= start) & (step < start + steps))
            def _(right=right, place=place, wide=wide, start=start):
                if wide == 1:
                    rows = place[...]
                else:
                    rows = place[pl.ds(pl.multiple_of((step - start) * D, D), D), :]
                block = dot(rows, right[...])
                kept[...] = block[: D // 2, :]

                def put(sent):
                    sent[...] = block[D // 2 :, :]

                send(put)

            start += steps
        if has_small:

            @pl.when(step == start - 1)
            def _():
                stacked = jnp.concatenate([line[...] for line in lines] + [jnp.zeros((107, D), F32)], axis=0)
                places[-1][...] = stacked.T
                for s in range(D // share // 2):
                    for out, side in ((kept, core), (sents[-1], 1 - core)):
                        at = pl.multiple_of((2 * s + side) * share, 8)
                        out[s * share : (s + 1) * share, D - 128 :] = places[-1][pl.ds(at, share), :]

    return kernel


def weight_sums(pairs, share, core, small=None, after=(), pieces=1):
    tokens = pairs[0][0].shape[0]
    sizes = [(l.shape[1] // D, r.shape[1] // D) for l, r in pairs]
    if small is not None:
        sizes[-1] = (1, 0)
    lefts, rights, start = [], [], 0
    for (left, right), (wide, long) in zip(pairs, sizes):
        steps = max(wide, long)
        if wide == 1:
            lefts.append((left, "all"))
        else:
            index = lambda j, first=start - wide + 1, last=wide - 1: (0, jnp.clip(j - first, 0, last))
            lefts.append((left, pl.BlockSpec((tokens, D), index)))
        if wide == 1 and long > 1:
            index = lambda j, start=start, last=steps - 1: (0, jnp.clip(j - start, 0, last))
            rights.append((right, pl.BlockSpec((tokens, D), index)))
        else:
            rights.append((right, "all"))
        start += steps
    columns = start * D
    extra = [] if small is None else [(line, "all") for line in small]
    cuts = [start * i // pieces for i in range(pieces + 1)]

    def half(low, high):
        index = lambda j: (0, jnp.clip(j - low, 0, high - low - 1))
        return ((D // 2, D * (high - low)), F32, pl.BlockSpec((D // 2, D), index))

    kept, *sent, token = call(
        weights_kernel(sizes, share, len(after), cuts),
        (start,),
        [(core, scalars())] + lefts + rights + extra + [(a, anywhere()) for a in after],
        [half(0, start)] + [half(low, high) for low, high in zip(cuts, cuts[1:])],
        [pltpu.VMEM((D * wide, tokens), BF16) for wide, _ in sizes]
        + [pltpu.VMEM((D, 128), F32)] * (small is not None),
        2 * tokens * D * columns,
        "weights",
    )
    return kept, sent, token


def row_spec(shape):
    rest = len(shape) - 1
    return pl.BlockSpec((1,) + tuple(shape[1:]), lambda r: (r,) + (0,) * rest)


def whole_spec(shape):
    return pl.BlockSpec(tuple(shape), lambda r: (0,) * len(shape))


def held_spec(shape):
    return pl.BlockSpec(tuple(shape), lambda r: (0,) * len(shape), pipeline_mode=pl.Buffered(1))


def scalars():
    return pl.BlockSpec(memory_space=pltpu.SMEM)


def anywhere():
    return pl.BlockSpec(memory_space=pl.ANY)


ROOM = {'front': 44, 'mix': 24, 'lift': 28, 'depth': 20, 'late': 44, 'late_weights': 36, 'depth_grad': 20, 'conv_back': 28, 'mix_back': 28, 'mix_end': 24, 'front_back': 32, 'weights': 28}
HOP_COST = 30e9
TIMES = {'front': 40.0, 'mix': 14.0, 'lift': 18.0, 'depth': 12.0, 'late': 46.0, 'late_weights': 22.0, 'depth_grad': 10.0, 'conv_back': 4, 'mix_back': 24.0, 'mix_end': 20.0, 'front_back': 60, 'weights': 20.0}


def call(kernel, grid, ins, outs, scratch=(), flops=0, name=None):
    def placed(array, kind):
        if kind not in ("row", "all") and kind.memory_space is not None:
            return array
        return pltpu.with_memory_space_constraint(array, pltpu.HBM)

    def made(kind, shape):
        if kind == "row":
            return row_spec(shape)
        return whole_spec(shape) if kind == "all" else kind

    moved = sum(a.size * a.dtype.itemsize for a, _ in ins)
    inner = len(ins) + len(outs)

    def with_token(*refs):
        kernel(*refs[:inner], *refs[inner + 1 :])
        refs[inner][...] = jnp.zeros((8, 128), F32)

    *made_arrays, token = pl.pallas_call(
        with_token,
        grid=grid,
        in_specs=[held_spec(a.shape) if kind == "all" else made(kind, a.shape) for a, kind in ins],
        out_specs=[made(kind, shape) for shape, _, kind in outs] + [whole_spec((8, 128))],
        out_shape=[pltpu.HBM(shape, kind) for shape, kind, _ in outs] + [pltpu.HBM((8, 128), F32)],
        scratch_shapes=list(scratch),
        compiler_params=pltpu.CompilerParams(
            dimension_semantics=("arbitrary",), vmem_limit_bytes=ROOM[name] * 2**20
        ),
        cost_estimate=pl.CostEstimate(
            flops=int(TIMES[name] * 1.15e9), bytes_accessed=0, transcendentals=0
        ),
        name=name,
    )(*[placed(a, kind) for a, kind in ins])
    return (*made_arrays, token)


def flip_pairs(count, mask):
    return [(i, i ^ mask) for i in range(count)]


def hop_kernel(backward, first, keep_state, waits):
    def kernel(keep, second_ref, value, other, *refs):
        refs = refs[waits:]
        before, (out, out_before, token) = (None, refs) if first else (refs[0], refs[1:])
        token[...] = jnp.zeros((8, 128), F32)
        second = (second_ref[0] != 0) != backward
        rows = value.shape[0]
        decay_rows = slice(4 * STATE, 4 * STATE + 8)
        for r in range(rows):
            here, there = value[r, decay_rows, :], other[r, decay_rows, :]
            out[r, decay_rows, :] = here * there
            if first:
                entered = jnp.where(second, there, 1.0)
            else:
                entered = before[r, decay_rows, :]
                entered = jnp.where(second, entered * there, entered)
            out_before[r, decay_rows, :] = entered
            for a in range(4):
                at = slice(STATE * a, STATE * (a + 1))
                mine, others = value[r, at, :], other[r, at, :]
                mine_decay, other_decay = here[a : a + 1, :], there[a : a + 1, :]
                out[r, at, :] = jnp.where(
                    second, mine_decay * others + mine, other_decay * mine + others
                )
                if first:
                    entered = jnp.where(second, others, 0.0)
                else:
                    entered = before[r, at, :]
                    own = before[r, 4 * STATE + a : 4 * STATE + a + 1, :]
                    entered = jnp.where(second, own * others + entered, entered)
                out_before[r, at, :] = entered * keep[0, r] if keep_state else entered

    return kernel


def entering(value, backward, keep, meanwhile=lambda tokens: []):
    count, place = lax.axis_size("seq"), lax.axis_index("seq")
    vmem = pl.BlockSpec(memory_space=pltpu.VMEM)
    shape = jax.ShapeDtypeStruct(value.shape, F32)
    before, tokens = [], []
    for bit in range(count.bit_length() - 1):
        other = lax.ppermute(value, "seq", flip_pairs(count, 1 << bit))
        last = (2 << bit) == count
        after = meanwhile(tokens) if last else []
        value, entered, token = pl.pallas_call(
            hop_kernel(backward, bit == 0, last and not backward, len(after)),
            in_specs=[scalars()] * 2 + [vmem] * 2 + [anywhere()] * len(after) + [vmem] * len(before),
            out_specs=[vmem] * 3,
            out_shape=[shape, shape, jax.ShapeDtypeStruct((8, 128), F32)],
            compiler_params=pltpu.CompilerParams(vmem_limit_bytes=8 * 2**20),
            cost_estimate=pl.CostEstimate(
                flops=int(HOP_COST) if backward and bit == 1 else 0, bytes_accessed=0, transcendentals=0
            ),
            name="hop",
        )(keep, ((place >> bit) & 1).reshape(1), value, other, *after, *before)
        before = [entered]
        tokens.append(token)
    return before[0]


def halos(top, bottom):
    count = lax.axis_size("seq")
    ends = range(count - 1)
    return (
        lax.ppermute(bottom, "seq", [(i, i + 1) for i in ends]),
        lax.ppermute(top, "seq", [(i + 1, i) for i in ends]),
    )


def sum_over_all(value):
    count = lax.axis_size("seq") * lax.axis_size("rec")
    copies = jnp.broadcast_to(value[None], (count,) + value.shape)
    return jnp.sum(lax.all_to_all(copies, ("rec", "seq"), 0, 0), axis=0)


def scatter_sum(value):
    return lax.psum_scatter(value, "seq", scatter_dimension=0, tiled=True)


def in_vmem(kernel, scalars_in, ins, outs, after, name, cost=0):
    vmem = pl.BlockSpec(memory_space=pltpu.VMEM)
    return pl.pallas_call(
        kernel,
        in_specs=[scalars()] + [vmem] * len(ins) + [anywhere()] * len(after),
        out_specs=[vmem] * len(outs) + [vmem],
        out_shape=[jax.ShapeDtypeStruct(shape, F32) for shape in outs + [(8, 128)]],
        compiler_params=pltpu.CompilerParams(vmem_limit_bytes=8 * 2**20),
        cost_estimate=pl.CostEstimate(
            flops=int(cost * 1.15e9), bytes_accessed=0, transcendentals=0
        ),
        name=name,
    )(scalars_in, *ins, *after)


def part_rows(ref, group, chunk, side, columns):
    if chunk % 8:
        low = ref[2 * group * chunk : (2 * group + 1) * chunk, columns]
        high = ref[(2 * group + 1) * chunk : (2 * group + 2) * chunk, columns]
        return jnp.where(side == 0, low, high)
    return ref[pl.ds(pl.multiple_of((2 * group + side) * chunk, 8), chunk), columns]


def split_task(groups):
    arrays, outs, plan = [], [], []

    def known(array):
        for i, other in enumerate(arrays):
            if other is array:
                return i
        arrays.append(array)
        return len(arrays) - 1

    for items, chunk, bit in groups:
        rows = items[0][0].shape[0]
        placed, at = [], 0
        for kept, first, received, other_first, columns in items:
            there = None if received is None else known(received)
            placed.append((known(kept), first, there, other_first, columns, at))
            at += columns
        plan.append((placed, rows, chunk, bit, len(outs)))
        outs += [(rows // 2, at)] * 2

    def body(bit_ref, ins, made):
        for placed, rows, chunk, bit, out in plan:
            mine = bit_ref[bit]
            for kept, first, received, other_first, columns, at in placed:
                mine_at = slice(first, first + columns)
                other_at = slice(other_first, other_first + columns)
                for target, side in ((made[out], mine), (made[out + 1], 1 - mine)):
                    for group in range(rows // chunk // 2):
                        value = part_rows(ins[kept], group, chunk, side, mine_at)
                        if received is not None:
                            value = value + part_rows(ins[received], group, chunk, side, other_at)
                        target[group * chunk : (group + 1) * chunk, at : at + columns] = value

    return arrays, outs, body


def add_task(kept, received):
    def body(_, ins, made):
        made[0][...] = ins[0][...] + ins[1][...]

    return [kept, received], [kept.shape], body


def join_task(mine, other, bit, pieces=None):
    rows, columns = mine.shape
    cuts = [(0, columns, False)] if pieces is None else pieces
    outs = [(8 * rows, D) if spread else (2 * rows, wide) for _, wide, spread in cuts]

    def body(bit_ref, ins, made):
        first = bit_ref[bit] == 0
        for target, (at, wide, spread) in zip(made, cuts):
            for k in range(4 if spread else 1):
                width = D if spread else wide
                left = ins[0][:, at + D * k : at + D * k + width]
                right = ins[1][:, at + D * k : at + D * k + width]
                start = 2 * rows * k
                target[start : start + rows, :] = jnp.where(first, left, right)
                target[start + rows : start + 2 * rows, :] = jnp.where(first, right, left)

    return [mine, other], outs, body


def together(bits, sums, after, cost=0):
    tasks = [one.step() for one in sums]
    arrays = [array for ins, _, _, _ in tasks for array in ins]
    outs = [shape for _, shapes, _, _ in tasks for shape in shapes]
    count = len(arrays) + len(after)

    def kernel(bit_ref, *refs):
        at, out = 0, count
        for ins, shapes, body, _ in tasks:
            body(bit_ref, refs[at : at + len(ins)], refs[out : out + len(shapes)])
            at, out = at + len(ins), out + len(shapes)
        refs[-1][...] = jnp.zeros((8, 128), F32)

    *made, token = in_vmem(kernel, bits, arrays, outs, after, "together", cost)
    for _, shapes, _, commit in tasks:
        commit(made[: len(shapes)])
        made = made[len(shapes) :]
    return token


class Sum:
    def __init__(self, pieces):
        self.pieces = pieces
        self.chip_bits = lax.axis_size("seq").bit_length() - 2
        self.rec_bits = lax.axis_size("rec").bit_length() - 1
        self.parts, self.left, self.steps, self.beside = [], [], [], []
        self.done = None

    def swap(self, value, axis, bit):
        return lax.ppermute(value, axis, flip_pairs(lax.axis_size(axis), 1 << bit))

    def begin(self, kept, sent, first):
        self.parts = [[], []]
        at = 0
        for piece in sent:
            received = self.swap(piece, "seq", 0)
            end = at + piece.shape[1]
            for part, low, high in ((0, at, min(end, first)), (1, max(at, first), end)):
                if low < high:
                    self.parts[part].append((kept, low, received, low - at, high - low))
            at = end
        turn = 1 + self.chip_bits // 2
        orders = (
            list(range(1, self.chip_bits + 1)),
            list(range(turn, self.chip_bits + 1)) + list(range(1, turn)),
        )
        self.left = [list(range(self.chip_bits, 0, -1)) for _ in orders]
        self.steps += [("chips", now) for now in zip(*orders)]
        self.steps += [("rec", bit) for bit in range(self.rec_bits)] + [("turn", self.rec_bits - 1)]
        self.steps += [("join", bit) for bit in reversed(range(self.rec_bits))]

    def step(self):
        kind, now = self.steps.pop(0)
        if kind == "chips":
            groups = []
            for items, bit, left in zip(self.parts, now, self.left):
                chunk = items[0][0].shape[0] >> (left.index(bit) + 1)
                left.remove(bit)
                groups.append((items, chunk, bit))

            def commit(made):
                self.parts = [
                    [(made[2 * i], 0, self.swap(made[2 * i + 1], "seq", bit), 0, made[2 * i].shape[1])]
                    for i, bit in enumerate(now)
                ]

            return *split_task(groups), commit
        if kind == "rec":
            items = [item for part in self.beside + self.parts for item in part]
            self.beside = []

            def commit(made):
                kept, sent = made
                self.parts = [[(kept, 0, self.swap(sent, "rec", now), 0, kept.shape[1])]]

            chunk = items[0][0].shape[0] // 2
            return *split_task([(items, chunk, self.chip_bits + 1 + now)]), commit
        if kind == "turn":
            [[(kept, _, received, _, _)]] = self.parts

            def commit(made):
                [self.mine] = made
                self.other = self.swap(self.mine, "rec", now)

            return *add_task(kept, received), commit

        def commit(made):
            if now == 0:
                self.done = made
                return
            [self.mine] = made
            self.other = self.swap(self.mine, "rec", now - 1)

        pieces = self.pieces if now == 0 else None
        return *join_task(self.mine, self.other, self.chip_bits + 1 + now, pieces), commit


def local(
    features, time_keep, freq_keep, block_flags, decays, w_sub, ln1_gain, ffn1_in, ffn1_out, ln2_gain,
    ssm_in, ssm_out, ln3_gain, conv_in, conv_depth, bn_gain, bn_shift, conv_out, ln4_gain, ffn2_in,
    ffn2_out, ln5_gain, out_grad,
):
    rows, frame_count, mels = features.shape
    steps = frame_count // SUB
    tokens = rows * steps
    blocks = lax.axis_size("seq")
    place = lax.axis_index("seq")
    count = float(tokens * blocks * lax.axis_size("rec"))
    share = D // blocks
    here = lax.dynamic_index_in_dim(block_flags, place, 1, keepdims=False)
    after = lax.dynamic_index_in_dim(
        block_flags, jnp.minimum(place + 1, blocks - 1), 1, keepdims=False
    )
    keep_here = (1 - here).astype(F32)
    keep_next = jnp.where(place + 1 < blocks, 1 - after, 0).astype(F32)
    keep = (jnp.stack([keep_here, keep_next]), scalars())
    tk = (time_keep, "all")
    fk = (freq_keep, "all")
    g1, g2, g3, g4, g5, bg, bb = (
        (gain.reshape(1, D), "all")
        for gain in (ln1_gain, ln2_gain, ln3_gain, ln4_gain, ln5_gain, bn_gain, bn_shift)
    )
    taps = (jnp.pad(conv_depth.T, ((0, 1), (0, 0))), "all")

    def rows_of(width, kind=F32):
        return ((rows, steps, width), kind, "row")


    per_state = ((rows, 4 * STATE + 8, 128), F32, "row")
    edge = ((rows, 8, D), F32, "row")
    line = ((1, D), F32, "all")
    two_lines = ((2, D), F32, "all")
    padded = pltpu.VMEM((D // 128, steps + 16, 128), F32)
    full = pltpu.VMEM((256, D), BF16)

    def row(value):
        return (value, "row")

    def every(value):
        return (value, "all")

    (flat, x1, a1, r1, s1, d1, a2, r2, u, g, bs, c, ce, bt, se, ee, te, cum, cum_t, state, _) = call(
        front_kernel,
        (rows,),
        [
            row(features.transpose(0, 2, 1)), tk, fk, row(decays), keep,
            every(w_sub.T), g1, every(ffn1_in), every(ffn1_out), g2, every(ssm_in),
        ],
        [
            rows_of(WIDE, BF16), rows_of(D), rows_of(D, BF16), rows_of(1), rows_of(FF, BF16),
            rows_of(FF, BF16), rows_of(D, BF16), rows_of(1), rows_of(D, BF16), rows_of(D, BF16),
            rows_of(256, BF16), rows_of(256, BF16), rows_of(256, BF16), rows_of(256, BF16),
            rows_of(256, BF16), rows_of(256, BF16), rows_of(256, BF16), rows_of(HEADS),
            ((rows, HEADS, steps), F32, "row"), per_state,
        ],
        [pltpu.VMEM((frame_count, mels), F32)],
        2 * tokens * D * (WIDE + 2 * FF + PROJ),
        "front",
    )
    start = entering(state, False, keep[0])
    pair_shape = ((rows, HEADS, steps, steps), BF16, "row")
    mixed, pairs, decay_pairs, _ = call(
        mix_kernel,
        (rows,),
        [row(u), row(bs), row(c), row(cum), row(cum_t)],
        [rows_of(D), pair_shape, pair_shape],
        (),
        2 * tokens * 256 * 256 * 16,
        "mix",
    )
    z, gs, yd, x2, a3, r3, v, sq, cq, top, bottom, _ = call(
        lift_kernel,
        (rows,),
        [row(mixed), row(ce), row(start), row(g), row(x1), every(ssm_out), g3, every(conv_in)],
        [
            rows_of(D, BF16), rows_of(D, BF16), rows_of(D, BF16), rows_of(D), rows_of(D, BF16),
            rows_of(1), rows_of(D), rows_of(D, BF16), rows_of(D, BF16), edge, edge,
        ],
        [full],
        2 * tokens * D * 4 * D,
        "lift",
    )
    v_before, v_after = halos(top, bottom)
    dc, sums, _ = call(
        depth_kernel,
        (rows,),
        [row(v), row(v_before), row(v_after), keep, taps],
        [rows_of(D), two_lines],
        [padded],
        2 * tokens * D * 64,
        "depth",
    )
    stats = sum_over_all(sums)
    out, e, a4, s4, gf4, gh4, ge, gx3, gbn, back_sums, ln4, ln5, _ = call(
        late_kernel(count),
        (rows,),
        [
            row(dc), row(x2), row(out_grad), every(stats), bg, bb, every(conv_out), g4,
            every(ffn2_in), every(ffn2_out), g5,
        ],
        [
            rows_of(D, BF16), rows_of(D, BF16), rows_of(D, BF16), rows_of(FF, BF16), rows_of(D, BF16),
            rows_of(FF, BF16), rows_of(D, BF16), rows_of(D), rows_of(D), two_lines, line, line,
        ],
        [pltpu.VMEM((steps, FF), BF16)],
        2 * tokens * D * (4 * FF + 2 * D),
        "late",
    )
    back = sum_over_all(back_sums)

    def flatten(value):
        return value.reshape(tokens, value.shape[-1])

    def column_block(value, width):
        return (flatten(value), pl.BlockSpec((tokens, width), lambda i: (0, i)))

    def row_block(columns):
        return ((D, columns), F32, pl.BlockSpec((256, columns), lambda i: (i, 0)))

    late_grads, late_token = call(
        late_weights_kernel(share),
        (2,),
        [
            column_block(a4, 256), column_block(e, 256), column_block(s4, 1024),
            every(flatten(gh4)), every(flatten(ge)), every(flatten(gf4)),
        ],
        [row_block(2 * FF + D)],
        (),
        2 * tokens * D * (2 * FF + D),
        "late_weights",
    )
    scattered_a = scatter_sum(late_grads)

    def edge_grad(at):
        return batch_back(
            lax.slice_in_dim(gbn, at, at + 8, axis=1),
            lax.slice_in_dim(dc, at, at + 8, axis=1),
            stats, back, bn_gain, count,
        )

    gd_before, gd_after = halos(edge_grad(0), edge_grad(steps - 8))
    gd, taps_grad, _ = call(
        depth_grad_kernel(count),
        (rows,),
        [
            row(gbn), row(dc), every(stats), every(back), bg, row(v), row(v_before), row(v_after), keep,
            (late_token, anywhere()),
        ],
        [rows_of(D), ((16, D), F32, "all")],
        [padded],
        2 * tokens * D * 64,
        "depth_grad",
    )
    gq, gx2, gz, gy, gg, pulled, ln3, _ = call(
        conv_back_kernel,
        (rows,),
        [
            row(gd), row(gd_before), row(gd_after), keep, taps, row(sq), row(cq), every(conv_in),
            row(a3), row(r3), g3, row(gx3), every(ssm_out), row(gs), row(yd), row(ce), row(state),
        ],
        [
            rows_of(2 * D, BF16), rows_of(D), rows_of(D, BF16), rows_of(D, BF16), rows_of(D, BF16),
            per_state, line,
        ],
        [padded],
        2 * tokens * D * 4 * D,
        "conv_back",
    )
    core = (place % 2).reshape(1)
    bits = jnp.stack(
        [(place >> k) & 1 for k in range(blocks.bit_length() - 1)]
        + [(lax.axis_index("rec") >> k) & 1 for k in range(lax.axis_size("rec").bit_length() - 1)]
    )
    early = Sum(
        [
            (0, FF, False), (FF, FF, True), (2 * FF, D, False), (2 * FF + D, 2 * D, False),
            (2 * FF + 3 * D, D, False),
        ],
    )
    found = {}

    def beside(hops):
        kept, sent, weights_token = weight_sums(
            [(flatten(a3), flatten(gq)), (flatten(z), flatten(gz))], share, core, None, hops[-2:-1]
        )
        early.begin(kept, sent, D)
        token = together(bits, [early], [weights_token, hops[-1]])
        gu, gb, gc, mixed_token = call(
            mix_back_kernel,
            (rows,),
            [
                row(u), row(bs), row(c), row(ee), row(gy), row(start), row(pairs), row(decay_pairs),
                (token, anywhere()),
            ],
            [rows_of(D), rows_of(256), rows_of(256, BF16)],
            [full],
            2 * tokens * 256 * 256 * 32,
            "mix_back",
        )
        found["mixed"] = (gu, gb, gc, mixed_token)
        return [mixed_token]

    end = entering(pulled, True, keep[0], beside)
    gu, gb, gc, mixed_token = found["mixed"]
    token = together(bits, [early], [mixed_token])
    gp, gx1, gf1, ln2, end_token = call(
        mix_end_kernel,
        (rows,),
        [
            row(end), row(u), row(bt), row(te), row(se), row(gu), row(gb), row(gc), row(gg),
            every(ssm_in), row(a2), row(r2), g2, row(gx2), (token, anywhere()),
        ],
        [rows_of(PROJ, BF16), rows_of(D), rows_of(D, BF16), line],
        [full],
        2 * tokens * D * PROJ,
        "mix_end",
    )
    kept, sent, weights_token = weight_sums(
        [(flatten(a2), flatten(gp)), (flatten(s1), flatten(gf1))], share, core, None, [end_token]
    )
    middle = Sum([(0, PROJ, False), (PROJ, FF, True)])
    middle.begin(kept, sent, PROJ)
    token = weights_token
    while early.steps[0][0] == "chips":
        token = together(bits, [early], [token])
    early.parts = [[(scattered_a, 0, None, 0, scattered_a.shape[1])]] + early.parts
    token = together(bits, [early], [token])
    gh1, gxr, features_grad, ln1, back_token = call(
        front_back_kernel,
        (rows,),
        [
            row(gx1), row(gf1), every(ffn1_out), row(d1), every(ffn1_in), row(a1), row(r1), g1,
            every(w_sub.T), tk, fk, (token, anywhere()),
        ],
        [rows_of(FF, BF16), rows_of(D, BF16), ((rows, mels, frame_count), F32, "row"), line],
        [pltpu.VMEM((frame_count, mels), F32)],
        2 * tokens * D * (WIDE + 2 * FF),
        "front_back",
    )
    small = [taps_grad, ln1, ln2, ln3, ln4, ln5]
    token = together(bits, [early, middle], [back_token])
    last = Sum([(0, FF, False), (FF, SUB * mels, False), (FF + D - 128, 128, False)])
    kept, sent, weights_token = weight_sums(
        [(flatten(a1), flatten(gh1)), (flatten(gxr), flatten(flat))], share, core, small, [token], 1
    )
    last.begin(kept, sent, 2 * D)
    token = weights_token
    token = together(bits, [early, middle], [token], 60.0)
    rounds = [(last,), (early, middle, last), (middle, last)]
    while early.steps or middle.steps or last.steps:
        now = rounds.pop(0) if rounds else (early, middle, last)
        now = [one for one in now if one.steps]
        if now:
            token = together(bits, now, [token])
    ffn2_in_grad, ffn2_out_grad, conv_out_grad, conv_in_grad, ssm_out_grad = early.done
    ssm_in_grad, ffn1_out_grad = middle.done
    ffn1_in_grad, w_sub_grad, gains = last.done

    start_row = place * share
    return (
        out,
        features_grad.transpose(0, 2, 1),
        w_sub_grad,
        gains[:, 16],
        ffn1_in_grad,
        ffn1_out_grad,
        gains[:, 17],
        ssm_in_grad,
        ssm_out_grad,
        gains[:, 18],
        conv_in_grad,
        gains[:, :KERNEL],
        lax.dynamic_slice_in_dim(back[0], start_row, share),
        lax.dynamic_slice_in_dim(back[1], start_row, share),
        conv_out_grad,
        gains[:, 19],
        ffn2_in_grad,
        ffn2_out_grad,
        gains[:, 20],
    )


def solution(mesh):
    block = P("rec", "seq", None)
    rows_of_seq, line = P("seq", None), P("seq")
    return jax.shard_map(
        local,
        mesh=mesh,
        in_specs=(block, P("rec", "seq"), P("rec", None), P("rec", None), P("rec", None, "seq"))
        + (P(),) * 17
        + (block,),
        out_specs=(
            block, block, rows_of_seq, line, rows_of_seq, rows_of_seq, line, rows_of_seq, rows_of_seq,
            line, rows_of_seq, rows_of_seq, line, line, rows_of_seq, line, rows_of_seq, rows_of_seq, line,
        ),
        check_vma=False,
    )
```

```python
import jax
import jax.numpy as jnp
from jax import lax
from jax.experimental import pallas as pl
from jax.experimental.pallas import tpu as pltpu
from jax.sharding import PartitionSpec as P

D = 512
FF = 2048
HEADS = 8
STATE = 32
SUB = 4
KERNEL = 15
HEADP = 64
PROJ = 1536
WIDE = 512
EPS = 1e-05
F32 = jnp.float32
BF16 = jnp.bfloat16
LIMIT = 32
READ_SCALE = STATE ** (-0.5)


def dot(a, b):
    return lax.dot_general(a, b, (((1,), (0,)), ((), ())), preferred_element_type=F32)


def dot_t(a, b):
    return lax.dot_general(a, b, (((1,), (1,)), ((), ())), preferred_element_type=F32)


def t_dot(a, b):
    return lax.dot_general(a, b, (((0,), (0,)), ((), ())), preferred_element_type=F32)


def sigmoid(x):
    return 0.5 * jnp.tanh(0.5 * x) + 0.5


def mean(x):
    return jnp.mean(x, axis=-1, keepdims=True)


def norm(x, gain):
    centred = x - mean(x)
    scale = lax.rsqrt(mean(centred * centred) + EPS)
    return (centred * scale * gain).astype(BF16), scale


def norm_back(grad, normed, scale, gain):
    wide = normed.astype(F32)
    inverse = 1.0 / gain
    both = grad * wide
    inner = grad * gain
    back = scale * (inner - mean(inner) - wide * inverse * mean(both))
    return back, jnp.sum(both, axis=0, keepdims=True) * inverse


def split_two(x):
    high = x.astype(BF16)
    return high, (x - high.astype(F32)).astype(BF16)


def split_three(x):
    high, rest = split_two(x)
    return high, rest, (x - high.astype(F32) - rest.astype(F32)).astype(BF16)


def iota(shape, dim):
    return lax.broadcasted_iota(jnp.int32, shape, dim)


def lane_mask(columns, width, index):
    lane = iota((16, columns), 1)
    inside = (lane >= width * index) & (lane < width * (index + 1))
    return jnp.where(inside, 1.0, 0.0).astype(BF16)[:1]


def pack_state(full):
    lane = iota((STATE, 128), 1)
    return [
        jnp.where(
            lane < HEADP,
            full[64 * a : 64 * a + 32, 128 * a : 128 * a + 128],
            full[64 * a + 32 : 64 * a + 64, 128 * a : 128 * a + 128],
        )
        for a in range(4)
    ]


def unpack_state(ref, full):
    lane = iota((STATE, 128), 1)
    full[...] = jnp.zeros_like(full)
    for a in range(4):
        pair = ref[0, STATE * a : STATE * (a + 1), :]
        full[64 * a : 64 * a + 32, 128 * a : 128 * a + 128] = jnp.where(
            lane < HEADP, pair, 0.0
        ).astype(BF16)
        full[64 * a + 32 : 64 * a + 64, 128 * a : 128 * a + 128] = jnp.where(
            lane < HEADP, 0.0, pair
        ).astype(BF16)


def accumulate(ref, value):
    first = pl.program_id(0) == 0

    @pl.when(first)
    def _():
        ref[...] = value

    @pl.when(jnp.logical_not(first))
    def _():
        ref[...] += value


def front_kernel(
    feat, tk, fk, dec, keep, w_sub, g1, w1, w2, g2, w_in,
    flat, x1, a1, r1, s1, d1, a2, r2, u, g, bs, c, ce, bt, se, ee, te, cum, cum_t, state,
    frames,
):
    steps = x1.shape[1]
    here = pl.ds(pl.program_id(0), 1)
    kept = feat[0].astype(F32) * tk[here, :].astype(F32)
    frames[...] = kept.T * fk[here, :].astype(F32)
    parts = [frames[pl.ds(j, steps, stride=SUB), :] for j in range(SUB)]
    parts.append(jnp.zeros((steps, WIDE - SUB * parts[0].shape[1]), F32))
    stacked = jnp.concatenate(parts, axis=1).astype(BF16)
    flat[0] = stacked
    x0 = dot(stacked[:, : w_sub.shape[0]], w_sub[...])
    low, scale = norm(x0, g1[...])
    a1[0] = low
    r1[0] = scale
    for at in range(0, FF, D):
        hidden = dot(low, w1[:, at : at + D])
        gate = sigmoid(hidden)
        active = hidden * gate
        d1[0, :, at : at + D] = (gate * (1.0 + hidden - active)).astype(BF16)
        s1[0, :, at : at + D] = active.astype(BF16)
    after = x0 + 0.5 * dot(s1[0], w2[...])
    x1[0] = after
    low, scale = norm(after, g2[...])
    a2[0] = low
    r2[0] = scale
    u_low = dot(low, w_in[:, :D]).astype(BF16)
    u[0] = u_low
    g[0] = dot(low, w_in[:, D : 2 * D]).astype(BF16)
    keys = dot(low, w_in[:, 2 * D : 2 * D + 256])
    reads = dot(low, w_in[:, 2 * D + 256 :])
    log_rows = jnp.log(dec[0])
    log_decay = log_rows.T
    lower = jnp.where(iota((steps, steps), 0) >= iota((steps, steps), 1), 1.0, 0.0).astype(BF16)
    running = sum(dot(lower, part) for part in split_three(log_decay))
    running_t = sum(dot_t(part, lower) for part in split_three(log_rows))
    cum[0] = running
    cum_t[0] = running_t
    spread = jnp.where(iota((HEADS, 256), 1) // STATE == iota((HEADS, 256), 0), 1.0, 0.0).astype(BF16)

    def over_columns(value):
        return sum(dot(part, spread) for part in split_two(value))

    scale_wide = over_columns(jnp.sqrt(-2.0 * log_decay))
    head = jnp.exp(running)
    head_wide = over_columns(head)
    tail_wide = over_columns(jnp.exp(running[steps - 1 :, :] - running))
    se[0] = scale_wide.astype(BF16)
    ee[0] = head_wide.astype(BF16)
    te[0] = tail_wide.astype(BF16)
    keys = keys * scale_wide
    bs[0] = keys.astype(BF16)
    c[0] = reads.astype(BF16)
    ce[0] = (reads * head_wide).astype(BF16)
    tailed = (keys * tail_wide).astype(BF16)
    bt[0] = tailed
    spread_values = jnp.where(iota((HEADS, D), 1) // HEADP == iota((HEADS, D), 0), 1.0, 0.0).astype(BF16)
    block = sum(dot(part, spread_values) for part in split_three(head[steps - 8 :, :]))
    block = block[7:8, :] * keep[0, pl.program_id(0)]
    for a, pair in enumerate(pack_state(t_dot(tailed, u_low))):
        state[0, STATE * a : STATE * (a + 1), :] = pair
    lines = [block[:, 128 * a : 128 * a + 128] for a in range(4)]
    state[0, 4 * STATE :, :] = jnp.concatenate(lines + lines, axis=0)


def mix_kernel(u, bs, c, cum, cum_t, mixed, pairs, decay_pairs):
    steps = u.shape[1]
    causal = iota((steps, steps), 0) >= iota((steps, steps), 1)
    keys = bs[0]
    reads = c[0]
    for q in range(2):
        values = u[0, :, 256 * q : 256 * q + 256]
        total = jnp.zeros((steps, 256), F32)
        for b in range(4):
            h = 4 * q + b
            weights = jnp.exp(
                jnp.where(causal, cum[0, :, h : h + 1] - cum_t[0, h : h + 1, :], -1e30)
            )
            scores = (dot_t(reads * lane_mask(256, STATE, h), keys) * weights).astype(BF16)
            decay_pairs[0, h] = weights.astype(BF16)
            pairs[0, h] = scores
            total += dot(scores, values * lane_mask(256, HEADP, b))
        mixed[0, :, 256 * q : 256 * q + 256] = total


def lift_kernel(
    mixed, ce, start, g, x1, w_out, g3, w_conv,
    z, gs, yd, x2, a3, r3, v, sq, cq, top, bottom,
    full,
):
    steps = x1.shape[1]
    unpack_state(start, full)
    y = (mixed[0] + dot(ce[0], full[...])) * READ_SCALE
    gate = g[0].astype(F32)
    sig = sigmoid(gate)
    active = gate * sig
    gs[0] = (active * READ_SCALE).astype(BF16)
    yd[0] = (y * sig * (1.0 + gate - active)).astype(BF16)
    gated = (y * active).astype(BF16)
    z[0] = gated
    after = x1[0] + dot(gated, w_out[...])
    x2[0] = after
    low, scale = norm(after, g3[...])
    a3[0] = low
    r3[0] = scale
    first = dot(low, w_conv[:, :D])
    sig = sigmoid(dot(low, w_conv[:, D:]))
    out = first * sig
    v[0] = out
    sq[0] = sig.astype(BF16)
    cq[0] = (out * (1.0 - sig)).astype(BF16)
    top[0] = out[:8, :]
    bottom[0] = out[steps - 8 :, :]


def fill_padded(padded, body, before, after, keep):
    steps = body.shape[1]
    row = pl.program_id(0)
    for i in range(D // 128):
        columns = slice(128 * i, 128 * i + 128)
        padded[i, :8, :] = before[0, :, columns] * keep[0, row]
        padded[i, 8 : 8 + steps, :] = body[0, :, columns]
        padded[i, 8 + steps :, :] = after[0, :, columns] * keep[1, row]


def depth_kernel(v, before, after, keep, taps, dc, sums, padded):
    steps = v.shape[1]
    fill_padded(padded, v, before, after, keep)
    total, square = [], []
    for at in range(0, D, 128):
        running = jnp.zeros((steps, 128), F32)
        for k in range(KERNEL):
            running += padded[at // 128, k + 1 : k + 1 + steps, :] * taps[k : k + 1, at : at + 128]
        dc[0, :, at : at + 128] = running
        total.append(jnp.sum(running, axis=0, keepdims=True))
        square.append(jnp.sum(running * running, axis=0, keepdims=True))
    accumulate(sums, jnp.concatenate([jnp.concatenate(total, axis=1), jnp.concatenate(square, axis=1)], axis=0))


def batch_stats(stats, count):
    middle = stats[0:1, :] / count
    return middle, lax.rsqrt(stats[1:2, :] / count - middle * middle + EPS)


def late_kernel(count):
    def kernel(
        dc, x2, og, stats, bn_gain, bn_shift, w_conv, g4, w3, w4, g5,
        out, e, a4, s4, gf, gh, ge, gx3, gbn, sums, ln4, ln5,
        slope,
    ):
        middle, inv = batch_stats(stats, count)
        unit = (dc[0] - middle) * inv
        batch = unit * bn_gain[...] + bn_shift[...]
        sig = sigmoid(batch)
        active = batch * sig
        conv_slope = sig * (1.0 + batch - active)
        active = active.astype(BF16)
        e[0] = active
        x3 = x2[0] + dot(active, w_conv[...])
        low, scale4 = norm(x3, g4[...])
        a4[0] = low
        for at in range(0, FF, D):
            hidden = dot(low, w3[:, at : at + D])
            gate = sigmoid(hidden)
            active = hidden * gate
            slope[:, at : at + D] = (gate * (1.0 + hidden - active)).astype(BF16)
            s4[0, :, at : at + D] = active.astype(BF16)
        x4 = x3 + 0.5 * dot(s4[0], w4[...])
        centred = x4 - mean(x4)
        scale = lax.rsqrt(mean(centred * centred) + EPS)
        unit5 = centred * scale
        out[0] = (unit5 * g5[...]).astype(BF16)
        grad = og[0].astype(F32)
        both = grad * unit5
        inner = grad * g5[...]
        accumulate(ln5, jnp.sum(both, axis=0, keepdims=True))
        gx4 = scale * (inner - mean(inner) - unit5 * mean(inner * unit5))
        gf_low = (0.5 * gx4).astype(BF16)
        gf[0] = gf_low
        for at in range(0, FF, D):
            hidden = (dot_t(gf_low, w4[at : at + D, :]) * slope[:, at : at + D].astype(F32)).astype(BF16)
            gh[0, :, at : at + D] = hidden
        back, gain4 = norm_back(dot_t(gh[0], w3[...]), low, scale4, g4[...])
        accumulate(ln4, gain4)
        grad3 = gx4 + back
        gx3[0] = grad3
        ge_low = grad3.astype(BF16)
        ge[0] = ge_low
        batch_grad = dot_t(ge_low, w_conv[...]) * conv_slope
        gbn[0] = batch_grad
        accumulate(
            sums,
            jnp.concatenate(
                [
                    jnp.sum(batch_grad * unit, axis=0, keepdims=True),
                    jnp.sum(batch_grad, axis=0, keepdims=True),
                ],
                axis=0,
            ),
        )

    return kernel


def batch_back(gbn, dc, stats, back, bn_gain, count):
    middle, inv = batch_stats(stats, count)
    unit = (dc - middle) * inv
    return bn_gain * inv * (gbn - (back[1:2, :] + unit * back[0:1, :]) / count)


def depth_grad_kernel(count):
    def kernel(gbn, dc, stats, back, bn_gain, v, before, after, keep, _, gd, taps_grad, padded):
        steps = v.shape[1]
        fill_padded(padded, v, before, after, keep)
        grad = batch_back(gbn[0], dc[0], stats, back, bn_gain[...], count)
        gd[0] = grad
        columns = []
        for at in range(0, D, 128):
            piece = gd[0, :, at : at + 128]
            rows = [
                jnp.sum(padded[at // 128, k + 1 : k + 1 + steps, :] * piece, axis=0, keepdims=True)
                for k in range(KERNEL)
            ]
            columns.append(jnp.concatenate(rows + [jnp.zeros((1, 128), F32)], axis=0))
        accumulate(taps_grad, jnp.concatenate(columns, axis=1))

    return kernel


def conv_back_kernel(
    gd, before, after, keep, taps, sq, cq, w_conv, a3, r3, g3, gx3, w_out, gs, yd, ce, block,
    gq, gx2, gz, gy, gg, pulled, ln3,
    padded,
):
    steps = gd.shape[1]
    fill_padded(padded, gd, before, after, keep)
    for at in range(0, D, 128):
        running = jnp.zeros((steps, 128), F32)
        for k in range(KERNEL):
            running += padded[at // 128, 15 - k : 15 - k + steps, :] * taps[k : k + 1, at : at + 128]
        gq[0, :, at : at + 128] = (running * sq[0, :, at : at + 128].astype(F32)).astype(BF16)
        gq[0, :, D + at : D + at + 128] = (running * cq[0, :, at : at + 128].astype(F32)).astype(BF16)
    back, gain = norm_back(dot_t(gq[0], w_conv[...]), a3[0], r3[0], g3[...])
    accumulate(ln3, gain)
    grad = gx3[0] + back
    gx2[0] = grad
    low = grad.astype(BF16)
    gz[0] = low
    inner = dot_t(low, w_out[...])
    gg[0] = (inner * yd[0].astype(F32)).astype(BF16)
    read_grad = (inner * gs[0].astype(F32)).astype(BF16)
    gy[0] = read_grad
    row = pl.program_id(0)
    for a, pair in enumerate(pack_state(t_dot(ce[0], read_grad))):
        pulled[0, STATE * a : STATE * (a + 1), :] = pair * keep[0, row]
    pulled[0, 4 * STATE :, :] = block[0, 4 * STATE :, :]


def mix_back_kernel(u, bs, c, ee, gy, start, pairs, decay_pairs, _, gu, gb, gc, full):
    steps = u.shape[1]
    unpack_state(start, full)
    reads_grad = dot_t(gy[0], full[...]) * ee[0].astype(F32)
    keys_grad = jnp.zeros((steps, 256), F32)
    keys = bs[0]
    reads = c[0]
    for q in range(2):
        values = u[0, :, 256 * q : 256 * q + 256]
        grads = gy[0, :, 256 * q : 256 * q + 256]
        total = jnp.zeros((steps, 256), F32)
        for b in range(4):
            h = 4 * q + b
            masked = grads * lane_mask(256, HEADP, b)
            scores = (dot_t(masked, values) * decay_pairs[0, h].astype(F32)).astype(BF16)
            mask = lane_mask(256, STATE, h)
            reads_grad += dot(scores, keys * mask)
            keys_grad += t_dot(scores, reads * mask)
            total += t_dot(pairs[0, h], masked)
        gu[0, :, 256 * q : 256 * q + 256] = total
    gc[0] = reads_grad.astype(BF16)
    gb[0] = keys_grad


def mix_end_kernel(
    end, u, bt, te, se, gu, gb, gc, gg, w_in, a2, r2, g2, gx2, _,
    gp, gx1, gf, ln2,
    full,
):
    unpack_state(end, full)
    gp[0, :, :D] = (gu[0] + dot(bt[0], full[...])).astype(BF16)
    gp[0, :, D : 2 * D] = gg[0]
    keys_grad = gb[0] + te[0].astype(F32) * dot_t(u[0], full[...])
    gp[0, :, 2 * D : 2 * D + 256] = (keys_grad * se[0].astype(F32)).astype(BF16)
    gp[0, :, 2 * D + 256 :] = gc[0]
    back, gain = norm_back(dot_t(gp[0], w_in[...]), a2[0], r2[0], g2[...])
    accumulate(ln2, gain)
    grad = gx2[0] + back
    gx1[0] = grad
    gf[0] = (0.5 * grad).astype(BF16)


def front_back_kernel(
    gx1, gf, w2, d1, w1, a1, r1, g1, w_sub, tk, fk, _,
    gh, gxr, fg, ln1,
    mel_rows,
):
    steps = gx1.shape[1]
    low = gf[0]
    for at in range(0, FF, D):
        hidden = (dot_t(low, w2[at : at + D, :]) * d1[0, :, at : at + D].astype(F32)).astype(BF16)
        gh[0, :, at : at + D] = hidden
    back, gain = norm_back(dot_t(gh[0], w1[...]), a1[0], r1[0], g1[...])
    accumulate(ln1, gain)
    low = (gx1[0] + back).astype(BF16)
    gxr[0] = low
    frames = dot_t(low, w_sub[...])
    mels = fk.shape[1]
    here = pl.ds(pl.program_id(0), 1)
    keep_mels = fk[here, :].astype(F32)
    for j in range(SUB):
        mel_rows[pl.ds(j, steps, stride=SUB), :] = frames[:, mels * j : mels * (j + 1)] * keep_mels
    fg[0] = mel_rows[...].T * tk[here, :].astype(F32)


def by_share_store(out, at, share, start, block):
    for piece in range(block.shape[0] // share):
        row = start + share * piece
        place = row // (4 * share) * share
        k = row % (4 * share) // share
        out[place : place + share, at + D * k : at + D * (k + 1)] = block[
            share * piece : share * (piece + 1), :
        ]


def late_weights_kernel(share):
    def kernel(a4, e, s4, gh, ge, gf, out):
        left = a4[...].T
        for at in range(0, FF, D):
            out[:, at : at + D] = dot(left, gh[:, at : at + D])
        for at in range(0, 1024, 256):
            by_share_store(out, FF, share, at, dot(s4[:, at : at + 256].T, gf[...]))
        out[:, 2 * FF :] = dot(e[...].T, ge[...])

    return kernel


def turned(place, share, core, block):
    rows = block.T
    half = rows.shape[0] // 2
    for s in range(rows.shape[0] // share):
        side = core if s % 2 == 0 else 1 - core
        at = pl.multiple_of(side * half + s // 2 * share, 16)
        place[pl.ds(at, share), :] = rows[s * share : (s + 1) * share, :]


def turned_by_share(place, share, core, block, at_block):
    for at in range(0, D, 256):
        rows = block[:, at : at + 256].T
        for piece in range(256 // share):
            here = at + share * piece
            first, k = here // (4 * share), here % (4 * share) // share
            side = core if first % 2 == 0 else 1 - core
            to = side * (D // 2) + D * k + (at_block * (D // (8 * share)) + first // 2) * share
            place[pl.ds(pl.multiple_of(to, 16), share), :] = rows[share * piece : share * (piece + 1), :]


def weights_kernel(pairs, share, waits, cuts):
    has_small = pairs[-1] == (1, 0)

    def kernel(core_ref, *refs):
        count = len(pairs)
        lefts, rights = refs[:count], refs[count : 2 * count]
        lines = refs[2 * count : 2 * count + 6 * has_small]
        kept, *sents = refs[2 * count + 6 * has_small + waits :][: len(cuts)]
        places = refs[2 * count + 6 * has_small + waits + len(cuts) :]

        def send(change):
            for sent, low, high in zip(sents, cuts, cuts[1:]):
                pl.when((step >= low) & (step < high))(lambda sent=sent: change(sent))

        step = pl.program_id(0)
        core = core_ref[0]
        start = 0
        for (wide, long), left, right, place in zip(pairs, lefts, rights, places[:count]):
            steps = max(wide, long)

            if wide == 1:

                @pl.when(step == start)
                def _(left=left, place=place):
                    turned(place, share, core, left[...])

            else:

                @pl.when((step > start - wide) & (step <= start))
                def _(left=left, place=place, before=start - wide + 1):
                    turned_by_share(place, share, core, left, step - before)

            @pl.when((step >= start) & (step < start + steps))
            def _(right=right, place=place, wide=wide, start=start):
                if wide == 1:
                    rows = place[...]
                else:
                    rows = place[pl.ds(pl.multiple_of((step - start) * D, D), D), :]
                block = dot(rows, right[...])
                kept[...] = block[: D // 2, :]

                def put(sent):
                    sent[...] = block[D // 2 :, :]

                send(put)

            start += steps
        if has_small:

            @pl.when(step == start - 1)
            def _():
                stacked = jnp.concatenate([line[...] for line in lines] + [jnp.zeros((107, D), F32)], axis=0)
                places[-1][...] = stacked.T
                for s in range(D // share // 2):
                    for out, side in ((kept, core), (sents[-1], 1 - core)):
                        at = pl.multiple_of((2 * s + side) * share, 8)
                        out[s * share : (s + 1) * share, D - 128 :] = places[-1][pl.ds(at, share), :]

    return kernel


def weight_sums(pairs, share, core, small=None, after=(), pieces=1):
    tokens = pairs[0][0].shape[0]
    sizes = [(l.shape[1] // D, r.shape[1] // D) for l, r in pairs]
    if small is not None:
        sizes[-1] = (1, 0)
    lefts, rights, start = [], [], 0
    for (left, right), (wide, long) in zip(pairs, sizes):
        steps = max(wide, long)
        if wide == 1:
            lefts.append((left, "all"))
        else:
            index = lambda j, first=start - wide + 1, last=wide - 1: (0, jnp.clip(j - first, 0, last))
            lefts.append((left, pl.BlockSpec((tokens, D), index)))
        if wide == 1 and long > 1:
            index = lambda j, start=start, last=steps - 1: (0, jnp.clip(j - start, 0, last))
            rights.append((right, pl.BlockSpec((tokens, D), index)))
        else:
            rights.append((right, "all"))
        start += steps
    columns = start * D
    extra = [] if small is None else [(line, "all") for line in small]
    cuts = [start * i // pieces for i in range(pieces + 1)]

    def half(low, high):
        index = lambda j: (0, jnp.clip(j - low, 0, high - low - 1))
        return ((D // 2, D * (high - low)), F32, pl.BlockSpec((D // 2, D), index))

    kept, *sent, token = call(
        weights_kernel(sizes, share, len(after), cuts),
        (start,),
        [(core, scalars())] + lefts + rights + extra + [(a, anywhere()) for a in after],
        [half(0, start)] + [half(low, high) for low, high in zip(cuts, cuts[1:])],
        [pltpu.VMEM((D * wide, tokens), BF16) for wide, _ in sizes]
        + [pltpu.VMEM((D, 128), F32)] * (small is not None),
        2 * tokens * D * columns,
        "weights",
    )
    return kept, sent, token


def row_spec(shape):
    rest = len(shape) - 1
    return pl.BlockSpec((1,) + tuple(shape[1:]), lambda r: (r,) + (0,) * rest)


def whole_spec(shape):
    return pl.BlockSpec(tuple(shape), lambda r: (0,) * len(shape))


def held_spec(shape):
    return pl.BlockSpec(tuple(shape), lambda r: (0,) * len(shape), pipeline_mode=pl.Buffered(1))


def scalars():
    return pl.BlockSpec(memory_space=pltpu.SMEM)


def anywhere():
    return pl.BlockSpec(memory_space=pl.ANY)


ROOM = {'front': 44, 'mix': 24, 'lift': 28, 'depth': 20, 'late': 44, 'late_weights': 36, 'depth_grad': 20, 'conv_back': 28, 'mix_back': 28, 'mix_end': 24, 'front_back': 32, 'weights': 28}
HOP_COST = 30e9
TIMES = {'front': 40.0, 'mix': 14.0, 'lift': 18.0, 'depth': 12.0, 'late': 46.0, 'late_weights': 22.0, 'depth_grad': 10.0, 'conv_back': 4, 'mix_back': 24.0, 'mix_end': 20.0, 'front_back': 60, 'weights': 20.0}


def call(kernel, grid, ins, outs, scratch=(), flops=0, name=None):
    def placed(array, kind):
        if kind not in ("row", "all") and kind.memory_space is not None:
            return array
        return pltpu.with_memory_space_constraint(array, pltpu.HBM)

    def made(kind, shape):
        if kind == "row":
            return row_spec(shape)
        return whole_spec(shape) if kind == "all" else kind

    moved = sum(a.size * a.dtype.itemsize for a, _ in ins)
    inner = len(ins) + len(outs)

    def with_token(*refs):
        kernel(*refs[:inner], *refs[inner + 1 :])
        refs[inner][...] = jnp.zeros((8, 128), F32)

    *made_arrays, token = pl.pallas_call(
        with_token,
        grid=grid,
        in_specs=[held_spec(a.shape) if kind == "all" else made(kind, a.shape) for a, kind in ins],
        out_specs=[made(kind, shape) for shape, _, kind in outs] + [whole_spec((8, 128))],
        out_shape=[pltpu.HBM(shape, kind) for shape, kind, _ in outs] + [pltpu.HBM((8, 128), F32)],
        scratch_shapes=list(scratch),
        compiler_params=pltpu.CompilerParams(
            dimension_semantics=("arbitrary",), vmem_limit_bytes=ROOM[name] * 2**20
        ),
        cost_estimate=pl.CostEstimate(
            flops=int(TIMES[name] * 1.15e9), bytes_accessed=0, transcendentals=0
        ),
        name=name,
    )(*[placed(a, kind) for a, kind in ins])
    return (*made_arrays, token)


def flip_pairs(count, mask):
    return [(i, i ^ mask) for i in range(count)]


def hop_kernel(backward, first, keep_state, waits):
    def kernel(keep, second_ref, value, other, *refs):
        refs = refs[waits:]
        before, (out, out_before, token) = (None, refs) if first else (refs[0], refs[1:])
        token[...] = jnp.zeros((8, 128), F32)
        second = (second_ref[0] != 0) != backward
        rows = value.shape[0]
        decay_rows = slice(4 * STATE, 4 * STATE + 8)
        for r in range(rows):
            here, there = value[r, decay_rows, :], other[r, decay_rows, :]
            out[r, decay_rows, :] = here * there
            if first:
                entered = jnp.where(second, there, 1.0)
            else:
                entered = before[r, decay_rows, :]
                entered = jnp.where(second, entered * there, entered)
            out_before[r, decay_rows, :] = entered
            for a in range(4):
                at = slice(STATE * a, STATE * (a + 1))
                mine, others = value[r, at, :], other[r, at, :]
                mine_decay, other_decay = here[a : a + 1, :], there[a : a + 1, :]
                out[r, at, :] = jnp.where(
                    second, mine_decay * others + mine, other_decay * mine + others
                )
                if first:
                    entered = jnp.where(second, others, 0.0)
                else:
                    entered = before[r, at, :]
                    own = before[r, 4 * STATE + a : 4 * STATE + a + 1, :]
                    entered = jnp.where(second, own * others + entered, entered)
                out_before[r, at, :] = entered * keep[0, r] if keep_state else entered

    return kernel


def entering(value, backward, keep, meanwhile=lambda tokens: []):
    count, place = lax.axis_size("seq"), lax.axis_index("seq")
    vmem = pl.BlockSpec(memory_space=pltpu.VMEM)
    shape = jax.ShapeDtypeStruct(value.shape, F32)
    before, tokens = [], []
    for bit in range(count.bit_length() - 1):
        other = lax.ppermute(value, "seq", flip_pairs(count, 1 << bit))
        last = (2 << bit) == count
        after = meanwhile(tokens) if last else []
        value, entered, token = pl.pallas_call(
            hop_kernel(backward, bit == 0, last and not backward, len(after)),
            in_specs=[scalars()] * 2 + [vmem] * 2 + [anywhere()] * len(after) + [vmem] * len(before),
            out_specs=[vmem] * 3,
            out_shape=[shape, shape, jax.ShapeDtypeStruct((8, 128), F32)],
            compiler_params=pltpu.CompilerParams(vmem_limit_bytes=8 * 2**20),
            cost_estimate=pl.CostEstimate(
                flops=int(HOP_COST) if backward and bit == 1 else 0, bytes_accessed=0, transcendentals=0
            ),
            name="hop",
        )(keep, ((place >> bit) & 1).reshape(1), value, other, *after, *before)
        before = [entered]
        tokens.append(token)
    return before[0]


def halos(top, bottom):
    count = lax.axis_size("seq")
    ends = range(count - 1)
    return (
        lax.ppermute(bottom, "seq", [(i, i + 1) for i in ends]),
        lax.ppermute(top, "seq", [(i + 1, i) for i in ends]),
    )


def sum_over_all(value):
    count = lax.axis_size("seq") * lax.axis_size("rec")
    copies = jnp.broadcast_to(value[None], (count,) + value.shape)
    return jnp.sum(lax.all_to_all(copies, ("rec", "seq"), 0, 0), axis=0)


def scatter_sum(value):
    return lax.psum_scatter(value, "seq", scatter_dimension=0, tiled=True)


def in_vmem(kernel, scalars_in, ins, outs, after, name, cost=0):
    vmem = pl.BlockSpec(memory_space=pltpu.VMEM)
    return pl.pallas_call(
        kernel,
        in_specs=[scalars()] + [vmem] * len(ins) + [anywhere()] * len(after),
        out_specs=[vmem] * len(outs) + [vmem],
        out_shape=[jax.ShapeDtypeStruct(shape, F32) for shape in outs + [(8, 128)]],
        compiler_params=pltpu.CompilerParams(vmem_limit_bytes=8 * 2**20),
        cost_estimate=pl.CostEstimate(
            flops=int(cost * 1.15e9), bytes_accessed=0, transcendentals=0
        ),
        name=name,
    )(scalars_in, *ins, *after)


def part_rows(ref, group, chunk, side, columns):
    if chunk % 8:
        low = ref[2 * group * chunk : (2 * group + 1) * chunk, columns]
        high = ref[(2 * group + 1) * chunk : (2 * group + 2) * chunk, columns]
        return jnp.where(side == 0, low, high)
    return ref[pl.ds(pl.multiple_of((2 * group + side) * chunk, 8), chunk), columns]


def split_task(groups):
    arrays, outs, plan = [], [], []

    def known(array):
        for i, other in enumerate(arrays):
            if other is array:
                return i
        arrays.append(array)
        return len(arrays) - 1

    for items, chunk, bit in groups:
        rows = items[0][0].shape[0]
        placed, at = [], 0
        for kept, first, received, other_first, columns in items:
            there = None if received is None else known(received)
            placed.append((known(kept), first, there, other_first, columns, at))
            at += columns
        plan.append((placed, rows, chunk, bit, len(outs)))
        outs += [(rows // 2, at)] * 2

    def body(bit_ref, ins, made):
        for placed, rows, chunk, bit, out in plan:
            mine = bit_ref[bit]
            for kept, first, received, other_first, columns, at in placed:
                mine_at = slice(first, first + columns)
                other_at = slice(other_first, other_first + columns)
                for target, side in ((made[out], mine), (made[out + 1], 1 - mine)):
                    for group in range(rows // chunk // 2):
                        value = part_rows(ins[kept], group, chunk, side, mine_at)
                        if received is not None:
                            value = value + part_rows(ins[received], group, chunk, side, other_at)
                        target[group * chunk : (group + 1) * chunk, at : at + columns] = value

    return arrays, outs, body


def add_task(kept, received):
    def body(_, ins, made):
        made[0][...] = ins[0][...] + ins[1][...]

    return [kept, received], [kept.shape], body


def join_task(mine, other, bit, pieces=None):
    rows, columns = mine.shape
    cuts = [(0, columns, False)] if pieces is None else pieces
    outs = [(8 * rows, D) if spread else (2 * rows, wide) for _, wide, spread in cuts]

    def body(bit_ref, ins, made):
        first = bit_ref[bit] == 0
        for target, (at, wide, spread) in zip(made, cuts):
            for k in range(4 if spread else 1):
                width = D if spread else wide
                left = ins[0][:, at + D * k : at + D * k + width]
                right = ins[1][:, at + D * k : at + D * k + width]
                start = 2 * rows * k
                target[start : start + rows, :] = jnp.where(first, left, right)
                target[start + rows : start + 2 * rows, :] = jnp.where(first, right, left)

    return [mine, other], outs, body


def together(bits, sums, after, cost=0):
    tasks = [one.step() for one in sums]
    arrays = [array for ins, _, _, _ in tasks for array in ins]
    outs = [shape for _, shapes, _, _ in tasks for shape in shapes]
    count = len(arrays) + len(after)

    def kernel(bit_ref, *refs):
        at, out = 0, count
        for ins, shapes, body, _ in tasks:
            body(bit_ref, refs[at : at + len(ins)], refs[out : out + len(shapes)])
            at, out = at + len(ins), out + len(shapes)
        refs[-1][...] = jnp.zeros((8, 128), F32)

    *made, token = in_vmem(kernel, bits, arrays, outs, after, "together", cost)
    for _, shapes, _, commit in tasks:
        commit(made[: len(shapes)])
        made = made[len(shapes) :]
    return token


class Sum:
    def __init__(self, pieces):
        self.pieces = pieces
        self.chip_bits = lax.axis_size("seq").bit_length() - 2
        self.rec_bits = lax.axis_size("rec").bit_length() - 1
        self.parts, self.left, self.steps, self.beside = [], [], [], []
        self.done = None

    def swap(self, value, axis, bit):
        return lax.ppermute(value, axis, flip_pairs(lax.axis_size(axis), 1 << bit))

    def begin(self, kept, sent, first):
        self.parts = [[], []]
        at = 0
        for piece in sent:
            received = self.swap(piece, "seq", 0)
            end = at + piece.shape[1]
            for part, low, high in ((0, at, min(end, first)), (1, max(at, first), end)):
                if low < high:
                    self.parts[part].append((kept, low, received, low - at, high - low))
            at = end
        turn = 1 + self.chip_bits // 2
        orders = (
            list(range(1, self.chip_bits + 1)),
            list(range(turn, self.chip_bits + 1)) + list(range(1, turn)),
        )
        self.left = [list(range(self.chip_bits, 0, -1)) for _ in orders]
        self.steps += [("chips", now) for now in zip(*orders)]
        self.steps += [("rec", bit) for bit in range(self.rec_bits)] + [("turn", self.rec_bits - 1)]
        self.steps += [("join", bit) for bit in reversed(range(self.rec_bits))]

    def step(self):
        kind, now = self.steps.pop(0)
        if kind == "chips":
            groups = []
            for items, bit, left in zip(self.parts, now, self.left):
                chunk = items[0][0].shape[0] >> (left.index(bit) + 1)
                left.remove(bit)
                groups.append((items, chunk, bit))

            def commit(made):
                self.parts = [
                    [(made[2 * i], 0, self.swap(made[2 * i + 1], "seq", bit), 0, made[2 * i].shape[1])]
                    for i, bit in enumerate(now)
                ]

            return *split_task(groups), commit
        if kind == "rec":
            items = [item for part in self.beside + self.parts for item in part]
            self.beside = []

            def commit(made):
                kept, sent = made
                self.parts = [[(kept, 0, self.swap(sent, "rec", now), 0, kept.shape[1])]]

            chunk = items[0][0].shape[0] // 2
            return *split_task([(items, chunk, self.chip_bits + 1 + now)]), commit
        if kind == "turn":
            [[(kept, _, received, _, _)]] = self.parts

            def commit(made):
                [self.mine] = made
                self.other = self.swap(self.mine, "rec", now)

            return *add_task(kept, received), commit

        def commit(made):
            if now == 0:
                self.done = made
                return
            [self.mine] = made
            self.other = self.swap(self.mine, "rec", now - 1)

        pieces = self.pieces if now == 0 else None
        return *join_task(self.mine, self.other, self.chip_bits + 1 + now, pieces), commit


def local(
    features, time_keep, freq_keep, block_flags, decays, w_sub, ln1_gain, ffn1_in, ffn1_out, ln2_gain,
    ssm_in, ssm_out, ln3_gain, conv_in, conv_depth, bn_gain, bn_shift, conv_out, ln4_gain, ffn2_in,
    ffn2_out, ln5_gain, out_grad,
):
    rows, frame_count, mels = features.shape
    steps = frame_count // SUB
    tokens = rows * steps
    blocks = lax.axis_size("seq")
    place = lax.axis_index("seq")
    count = float(tokens * blocks * lax.axis_size("rec"))
    share = D // blocks
    here = lax.dynamic_index_in_dim(block_flags, place, 1, keepdims=False)
    after = lax.dynamic_index_in_dim(
        block_flags, jnp.minimum(place + 1, blocks - 1), 1, keepdims=False
    )
    keep_here = (1 - here).astype(F32)
    keep_next = jnp.where(place + 1 < blocks, 1 - after, 0).astype(F32)
    keep = (jnp.stack([keep_here, keep_next]), scalars())
    tk = (time_keep, "all")
    fk = (freq_keep, "all")
    g1, g2, g3, g4, g5, bg, bb = (
        (gain.reshape(1, D), "all")
        for gain in (ln1_gain, ln2_gain, ln3_gain, ln4_gain, ln5_gain, bn_gain, bn_shift)
    )
    taps = (jnp.pad(conv_depth.T, ((0, 1), (0, 0))), "all")

    def rows_of(width, kind=F32):
        return ((rows, steps, width), kind, "row")


    per_state = ((rows, 4 * STATE + 8, 128), F32, "row")
    edge = ((rows, 8, D), F32, "row")
    line = ((1, D), F32, "all")
    two_lines = ((2, D), F32, "all")
    padded = pltpu.VMEM((D // 128, steps + 16, 128), F32)
    full = pltpu.VMEM((256, D), BF16)

    def row(value):
        return (value, "row")

    def every(value):
        return (value, "all")

    (flat, x1, a1, r1, s1, d1, a2, r2, u, g, bs, c, ce, bt, se, ee, te, cum, cum_t, state, _) = call(
        front_kernel,
        (rows,),
        [
            row(features.transpose(0, 2, 1)), tk, fk, row(decays), keep,
            every(w_sub.T), g1, every(ffn1_in), every(ffn1_out), g2, every(ssm_in),
        ],
        [
            rows_of(WIDE, BF16), rows_of(D), rows_of(D, BF16), rows_of(1), rows_of(FF, BF16),
            rows_of(FF, BF16), rows_of(D, BF16), rows_of(1), rows_of(D, BF16), rows_of(D, BF16),
            rows_of(256, BF16), rows_of(256, BF16), rows_of(256, BF16), rows_of(256, BF16),
            rows_of(256, BF16), rows_of(256, BF16), rows_of(256, BF16), rows_of(HEADS),
            ((rows, HEADS, steps), F32, "row"), per_state,
        ],
        [pltpu.VMEM((frame_count, mels), F32)],
        2 * tokens * D * (WIDE + 2 * FF + PROJ),
        "front",
    )
    start = entering(state, False, keep[0])
    pair_shape = ((rows, HEADS, steps, steps), BF16, "row")
    mixed, pairs, decay_pairs, _ = call(
        mix_kernel,
        (rows,),
        [row(u), row(bs), row(c), row(cum), row(cum_t)],
        [rows_of(D), pair_shape, pair_shape],
        (),
        2 * tokens * 256 * 256 * 16,
        "mix",
    )
    z, gs, yd, x2, a3, r3, v, sq, cq, top, bottom, _ = call(
        lift_kernel,
        (rows,),
        [row(mixed), row(ce), row(start), row(g), row(x1), every(ssm_out), g3, every(conv_in)],
        [
            rows_of(D, BF16), rows_of(D, BF16), rows_of(D, BF16), rows_of(D), rows_of(D, BF16),
            rows_of(1), rows_of(D), rows_of(D, BF16), rows_of(D, BF16), edge, edge,
        ],
        [full],
        2 * tokens * D * 4 * D,
        "lift",
    )
    v_before, v_after = halos(top, bottom)
    dc, sums, _ = call(
        depth_kernel,
        (rows,),
        [row(v), row(v_before), row(v_after), keep, taps],
        [rows_of(D), two_lines],
        [padded],
        2 * tokens * D * 64,
        "depth",
    )
    stats = sum_over_all(sums)
    out, e, a4, s4, gf4, gh4, ge, gx3, gbn, back_sums, ln4, ln5, _ = call(
        late_kernel(count),
        (rows,),
        [
            row(dc), row(x2), row(out_grad), every(stats), bg, bb, every(conv_out), g4,
            every(ffn2_in), every(ffn2_out), g5,
        ],
        [
            rows_of(D, BF16), rows_of(D, BF16), rows_of(D, BF16), rows_of(FF, BF16), rows_of(D, BF16),
            rows_of(FF, BF16), rows_of(D, BF16), rows_of(D), rows_of(D), two_lines, line, line,
        ],
        [pltpu.VMEM((steps, FF), BF16)],
        2 * tokens * D * (4 * FF + 2 * D),
        "late",
    )
    back = sum_over_all(back_sums)

    def flatten(value):
        return value.reshape(tokens, value.shape[-1])

    def column_block(value, width):
        return (flatten(value), pl.BlockSpec((tokens, width), lambda i: (0, i)))

    def row_block(columns):
        return ((D, columns), F32, pl.BlockSpec((256, columns), lambda i: (i, 0)))

    late_grads, late_token = call(
        late_weights_kernel(share),
        (2,),
        [
            column_block(a4, 256), column_block(e, 256), column_block(s4, 1024),
            every(flatten(gh4)), every(flatten(ge)), every(flatten(gf4)),
        ],
        [row_block(2 * FF + D)],
        (),
        2 * tokens * D * (2 * FF + D),
        "late_weights",
    )
    scattered_a = scatter_sum(late_grads)

    def edge_grad(at):
        return batch_back(
            lax.slice_in_dim(gbn, at, at + 8, axis=1),
            lax.slice_in_dim(dc, at, at + 8, axis=1),
            stats, back, bn_gain, count,
        )

    gd_before, gd_after = halos(edge_grad(0), edge_grad(steps - 8))
    gd, taps_grad, _ = call(
        depth_grad_kernel(count),
        (rows,),
        [
            row(gbn), row(dc), every(stats), every(back), bg, row(v), row(v_before), row(v_after), keep,
            (late_token, anywhere()),
        ],
        [rows_of(D), ((16, D), F32, "all")],
        [padded],
        2 * tokens * D * 64,
        "depth_grad",
    )
    gq, gx2, gz, gy, gg, pulled, ln3, _ = call(
        conv_back_kernel,
        (rows,),
        [
            row(gd), row(gd_before), row(gd_after), keep, taps, row(sq), row(cq), every(conv_in),
            row(a3), row(r3), g3, row(gx3), every(ssm_out), row(gs), row(yd), row(ce), row(state),
        ],
        [
            rows_of(2 * D, BF16), rows_of(D), rows_of(D, BF16), rows_of(D, BF16), rows_of(D, BF16),
            per_state, line,
        ],
        [padded],
        2 * tokens * D * 4 * D,
        "conv_back",
    )
    core = (place % 2).reshape(1)
    bits = jnp.stack(
        [(place >> k) & 1 for k in range(blocks.bit_length() - 1)]
        + [(lax.axis_index("rec") >> k) & 1 for k in range(lax.axis_size("rec").bit_length() - 1)]
    )
    early = Sum(
        [
            (0, FF, False), (FF, FF, True), (2 * FF, D, False), (2 * FF + D, 2 * D, False),
            (2 * FF + 3 * D, D, False),
        ],
    )
    found = {}

    def beside(hops):
        kept, sent, weights_token = weight_sums(
            [(flatten(a3), flatten(gq)), (flatten(z), flatten(gz))], share, core, None, hops[-2:-1]
        )
        early.begin(kept, sent, 3 * D // 2)
        token = together(bits, [early], [weights_token, hops[-1]])
        gu, gb, gc, mixed_token = call(
            mix_back_kernel,
            (rows,),
            [
                row(u), row(bs), row(c), row(ee), row(gy), row(start), row(pairs), row(decay_pairs),
                (token, anywhere()),
            ],
            [rows_of(D), rows_of(256), rows_of(256, BF16)],
            [full],
            2 * tokens * 256 * 256 * 32,
            "mix_back",
        )
        found["mixed"] = (gu, gb, gc, mixed_token)
        return [mixed_token]

    end = entering(pulled, True, keep[0], beside)
    gu, gb, gc, mixed_token = found["mixed"]
    token = together(bits, [early], [mixed_token])
    gp, gx1, gf1, ln2, end_token = call(
        mix_end_kernel,
        (rows,),
        [
            row(end), row(u), row(bt), row(te), row(se), row(gu), row(gb), row(gc), row(gg),
            every(ssm_in), row(a2), row(r2), g2, row(gx2), (token, anywhere()),
        ],
        [rows_of(PROJ, BF16), rows_of(D), rows_of(D, BF16), line],
        [full],
        2 * tokens * D * PROJ,
        "mix_end",
    )
    kept, sent, weights_token = weight_sums(
        [(flatten(a2), flatten(gp)), (flatten(s1), flatten(gf1))], share, core, None, [end_token]
    )
    middle = Sum([(0, PROJ, False), (PROJ, FF, True)])
    middle.begin(kept, sent, (PROJ + FF) // 2)
    token = weights_token
    while early.steps[0][0] == "chips":
        token = together(bits, [early], [token])
    early.parts = [[(scattered_a, 0, None, 0, scattered_a.shape[1])]] + early.parts
    token = together(bits, [early], [token])
    gh1, gxr, features_grad, ln1, back_token = call(
        front_back_kernel,
        (rows,),
        [
            row(gx1), row(gf1), every(ffn1_out), row(d1), every(ffn1_in), row(a1), row(r1), g1,
            every(w_sub.T), tk, fk, (token, anywhere()),
        ],
        [rows_of(FF, BF16), rows_of(D, BF16), ((rows, mels, frame_count), F32, "row"), line],
        [pltpu.VMEM((frame_count, mels), F32)],
        2 * tokens * D * (WIDE + 2 * FF),
        "front_back",
    )
    small = [taps_grad, ln1, ln2, ln3, ln4, ln5]
    token = together(bits, [middle], [back_token])
    token = together(bits, [early], [token])
    last = Sum([(0, FF, False), (FF, SUB * mels, False), (FF + D - 128, 128, False)])
    kept, sent, weights_token = weight_sums(
        [(flatten(a1), flatten(gh1)), (flatten(gxr), flatten(flat))], share, core, small, [token], 1
    )
    last.begin(kept, sent, (FF + WIDE) // 2)
    token = weights_token
    token = together(bits, [early, middle], [token], 60.0)
    rounds = [(last,), (early, middle, last), (middle, last)]
    while early.steps or middle.steps or last.steps:
        now = rounds.pop(0) if rounds else (early, middle, last)
        now = [one for one in now if one.steps]
        if now:
            token = together(bits, now, [token])
    ffn2_in_grad, ffn2_out_grad, conv_out_grad, conv_in_grad, ssm_out_grad = early.done
    ssm_in_grad, ffn1_out_grad = middle.done
    ffn1_in_grad, w_sub_grad, gains = last.done

    start_row = place * share
    return (
        out,
        features_grad.transpose(0, 2, 1),
        w_sub_grad,
        gains[:, 16],
        ffn1_in_grad,
        ffn1_out_grad,
        gains[:, 17],
        ssm_in_grad,
        ssm_out_grad,
        gains[:, 18],
        conv_in_grad,
        gains[:, :KERNEL],
        lax.dynamic_slice_in_dim(back[0], start_row, share),
        lax.dynamic_slice_in_dim(back[1], start_row, share),
        conv_out_grad,
        gains[:, 19],
        ffn2_in_grad,
        ffn2_out_grad,
        gains[:, 20],
    )


def solution(mesh):
    block = P("rec", "seq", None)
    rows_of_seq, line = P("seq", None), P("seq")
    return jax.shard_map(
        local,
        mesh=mesh,
        in_specs=(block, P("rec", "seq"), P("rec", None), P("rec", None), P("rec", None, "seq"))
        + (P(),) * 17
        + (block,),
        out_specs=(
            block, block, rows_of_seq, line, rows_of_seq, rows_of_seq, line, rows_of_seq, rows_of_seq,
            line, rows_of_seq, rows_of_seq, line, line, rows_of_seq, line, rows_of_seq, rows_of_seq, line,
        ),
        check_vma=False,
    )
```

```python
import jax
import jax.numpy as jnp
from jax import lax
from jax.experimental import pallas as pl
from jax.experimental.pallas import tpu as pltpu
from jax.sharding import PartitionSpec as P

D = 512
FF = 2048
HEADS = 8
STATE = 32
SUB = 4
KERNEL = 15
HEADP = 64
PROJ = 1536
WIDE = 512
EPS = 1e-05
F32 = jnp.float32
BF16 = jnp.bfloat16
LIMIT = 32
READ_SCALE = STATE ** (-0.5)


def dot(a, b):
    return lax.dot_general(a, b, (((1,), (0,)), ((), ())), preferred_element_type=F32)


def dot_t(a, b):
    return lax.dot_general(a, b, (((1,), (1,)), ((), ())), preferred_element_type=F32)


def t_dot(a, b):
    return lax.dot_general(a, b, (((0,), (0,)), ((), ())), preferred_element_type=F32)


def sigmoid(x):
    return 0.5 * jnp.tanh(0.5 * x) + 0.5


def mean(x):
    return jnp.mean(x, axis=-1, keepdims=True)


def norm(x, gain):
    centred = x - mean(x)
    scale = lax.rsqrt(mean(centred * centred) + EPS)
    return (centred * scale * gain).astype(BF16), scale


def norm_back(grad, normed, scale, gain):
    wide = normed.astype(F32)
    inverse = 1.0 / gain
    both = grad * wide
    inner = grad * gain
    back = scale * (inner - mean(inner) - wide * inverse * mean(both))
    return back, jnp.sum(both, axis=0, keepdims=True) * inverse


def split_two(x):
    high = x.astype(BF16)
    return high, (x - high.astype(F32)).astype(BF16)


def split_three(x):
    high, rest = split_two(x)
    return high, rest, (x - high.astype(F32) - rest.astype(F32)).astype(BF16)


def iota(shape, dim):
    return lax.broadcasted_iota(jnp.int32, shape, dim)


def lane_mask(columns, width, index):
    lane = iota((16, columns), 1)
    inside = (lane >= width * index) & (lane < width * (index + 1))
    return jnp.where(inside, 1.0, 0.0).astype(BF16)[:1]


def pack_state(full):
    lane = iota((STATE, 128), 1)
    return [
        jnp.where(
            lane < HEADP,
            full[64 * a : 64 * a + 32, 128 * a : 128 * a + 128],
            full[64 * a + 32 : 64 * a + 64, 128 * a : 128 * a + 128],
        )
        for a in range(4)
    ]


def unpack_state(ref, full):
    lane = iota((STATE, 128), 1)
    full[...] = jnp.zeros_like(full)
    for a in range(4):
        pair = ref[0, STATE * a : STATE * (a + 1), :]
        full[64 * a : 64 * a + 32, 128 * a : 128 * a + 128] = jnp.where(
            lane < HEADP, pair, 0.0
        ).astype(BF16)
        full[64 * a + 32 : 64 * a + 64, 128 * a : 128 * a + 128] = jnp.where(
            lane < HEADP, 0.0, pair
        ).astype(BF16)


def accumulate(ref, value):
    first = pl.program_id(0) == 0

    @pl.when(first)
    def _():
        ref[...] = value

    @pl.when(jnp.logical_not(first))
    def _():
        ref[...] += value


def front_kernel(
    feat, tk, fk, dec, keep, w_sub, g1, w1, w2, g2, w_in,
    flat, x1, a1, r1, s1, d1, a2, r2, u, g, bs, c, ce, bt, se, ee, te, cum, cum_t, state,
    frames,
):
    steps = x1.shape[1]
    here = pl.ds(pl.program_id(0), 1)
    kept = feat[0].astype(F32) * tk[here, :].astype(F32)
    frames[...] = kept.T * fk[here, :].astype(F32)
    parts = [frames[pl.ds(j, steps, stride=SUB), :] for j in range(SUB)]
    parts.append(jnp.zeros((steps, WIDE - SUB * parts[0].shape[1]), F32))
    stacked = jnp.concatenate(parts, axis=1).astype(BF16)
    flat[0] = stacked
    x0 = dot(stacked[:, : w_sub.shape[0]], w_sub[...])
    low, scale = norm(x0, g1[...])
    a1[0] = low
    r1[0] = scale
    for at in range(0, FF, D):
        hidden = dot(low, w1[:, at : at + D])
        gate = sigmoid(hidden)
        active = hidden * gate
        d1[0, :, at : at + D] = (gate * (1.0 + hidden - active)).astype(BF16)
        s1[0, :, at : at + D] = active.astype(BF16)
    after = x0 + 0.5 * dot(s1[0], w2[...])
    x1[0] = after
    low, scale = norm(after, g2[...])
    a2[0] = low
    r2[0] = scale
    u_low = dot(low, w_in[:, :D]).astype(BF16)
    u[0] = u_low
    g[0] = dot(low, w_in[:, D : 2 * D]).astype(BF16)
    keys = dot(low, w_in[:, 2 * D : 2 * D + 256])
    reads = dot(low, w_in[:, 2 * D + 256 :])
    log_rows = jnp.log(dec[0])
    log_decay = log_rows.T
    lower = jnp.where(iota((steps, steps), 0) >= iota((steps, steps), 1), 1.0, 0.0).astype(BF16)
    running = sum(dot(lower, part) for part in split_three(log_decay))
    running_t = sum(dot_t(part, lower) for part in split_three(log_rows))
    cum[0] = running
    cum_t[0] = running_t
    spread = jnp.where(iota((HEADS, 256), 1) // STATE == iota((HEADS, 256), 0), 1.0, 0.0).astype(BF16)

    def over_columns(value):
        return sum(dot(part, spread) for part in split_two(value))

    scale_wide = over_columns(jnp.sqrt(-2.0 * log_decay))
    head = jnp.exp(running)
    head_wide = over_columns(head)
    tail_wide = over_columns(jnp.exp(running[steps - 1 :, :] - running))
    se[0] = scale_wide.astype(BF16)
    ee[0] = head_wide.astype(BF16)
    te[0] = tail_wide.astype(BF16)
    keys = keys * scale_wide
    bs[0] = keys.astype(BF16)
    c[0] = reads.astype(BF16)
    ce[0] = (reads * head_wide).astype(BF16)
    tailed = (keys * tail_wide).astype(BF16)
    bt[0] = tailed
    spread_values = jnp.where(iota((HEADS, D), 1) // HEADP == iota((HEADS, D), 0), 1.0, 0.0).astype(BF16)
    block = sum(dot(part, spread_values) for part in split_three(head[steps - 8 :, :]))
    block = block[7:8, :] * keep[0, pl.program_id(0)]
    for a, pair in enumerate(pack_state(t_dot(tailed, u_low))):
        state[0, STATE * a : STATE * (a + 1), :] = pair
    lines = [block[:, 128 * a : 128 * a + 128] for a in range(4)]
    state[0, 4 * STATE :, :] = jnp.concatenate(lines + lines, axis=0)


def mix_kernel(u, bs, c, cum, cum_t, mixed, pairs, decay_pairs):
    steps = u.shape[1]
    causal = iota((steps, steps), 0) >= iota((steps, steps), 1)
    keys = bs[0]
    reads = c[0]
    for q in range(2):
        values = u[0, :, 256 * q : 256 * q + 256]
        total = jnp.zeros((steps, 256), F32)
        for b in range(4):
            h = 4 * q + b
            weights = jnp.exp(
                jnp.where(causal, cum[0, :, h : h + 1] - cum_t[0, h : h + 1, :], -1e30)
            )
            scores = (dot_t(reads * lane_mask(256, STATE, h), keys) * weights).astype(BF16)
            decay_pairs[0, h] = weights.astype(BF16)
            pairs[0, h] = scores
            total += dot(scores, values * lane_mask(256, HEADP, b))
        mixed[0, :, 256 * q : 256 * q + 256] = total.astype(BF16)


def lift_kernel(
    mixed, ce, start, g, x1, w_out, g3, w_conv,
    z, gs, yd, x2, a3, r3, v, sq, cq, top, bottom,
    full,
):
    steps = x1.shape[1]
    unpack_state(start, full)
    y = (mixed[0].astype(F32) + dot(ce[0], full[...])) * READ_SCALE
    gate = g[0].astype(F32)
    sig = sigmoid(gate)
    active = gate * sig
    gs[0] = (active * READ_SCALE).astype(BF16)
    yd[0] = (y * sig * (1.0 + gate - active)).astype(BF16)
    gated = (y * active).astype(BF16)
    z[0] = gated
    after = x1[0] + dot(gated, w_out[...])
    x2[0] = after
    low, scale = norm(after, g3[...])
    a3[0] = low
    r3[0] = scale
    first = dot(low, w_conv[:, :D])
    sig = sigmoid(dot(low, w_conv[:, D:]))
    out = first * sig
    v[0] = out
    sq[0] = sig.astype(BF16)
    cq[0] = (out * (1.0 - sig)).astype(BF16)
    top[0] = out[:8, :]
    bottom[0] = out[steps - 8 :, :]


def fill_padded(padded, body, before, after, keep):
    steps = body.shape[1]
    row = pl.program_id(0)
    for i in range(D // 128):
        columns = slice(128 * i, 128 * i + 128)
        padded[i, :8, :] = before[0, :, columns] * keep[0, row]
        padded[i, 8 : 8 + steps, :] = body[0, :, columns].astype(F32)
        padded[i, 8 + steps :, :] = after[0, :, columns] * keep[1, row]


def depth_kernel(v, before, after, keep, taps, dc, sums, padded):
    steps = v.shape[1]
    fill_padded(padded, v, before, after, keep)
    total, square = [], []
    for at in range(0, D, 128):
        running = jnp.zeros((steps, 128), F32)
        for k in range(KERNEL):
            running += padded[at // 128, k + 1 : k + 1 + steps, :] * taps[k : k + 1, at : at + 128]
        dc[0, :, at : at + 128] = running
        total.append(jnp.sum(running, axis=0, keepdims=True))
        square.append(jnp.sum(running * running, axis=0, keepdims=True))
    accumulate(sums, jnp.concatenate([jnp.concatenate(total, axis=1), jnp.concatenate(square, axis=1)], axis=0))


def batch_stats(stats, count):
    middle = stats[0:1, :] / count
    return middle, lax.rsqrt(stats[1:2, :] / count - middle * middle + EPS)


def late_kernel(count):
    def kernel(
        dc, x2, og, stats, bn_gain, bn_shift, w_conv, g4, w3, w4, g5,
        out, e, a4, s4, gf, gh, ge, gx3, gbn, sums, ln4, ln5,
        slope,
    ):
        middle, inv = batch_stats(stats, count)
        unit = (dc[0] - middle) * inv
        batch = unit * bn_gain[...] + bn_shift[...]
        sig = sigmoid(batch)
        active = batch * sig
        conv_slope = sig * (1.0 + batch - active)
        active = active.astype(BF16)
        e[0] = active
        x3 = x2[0] + dot(active, w_conv[...])
        low, scale4 = norm(x3, g4[...])
        a4[0] = low
        for at in range(0, FF, D):
            hidden = dot(low, w3[:, at : at + D])
            gate = sigmoid(hidden)
            active = hidden * gate
            slope[:, at : at + D] = (gate * (1.0 + hidden - active)).astype(BF16)
            s4[0, :, at : at + D] = active.astype(BF16)
        x4 = x3 + 0.5 * dot(s4[0], w4[...])
        centred = x4 - mean(x4)
        scale = lax.rsqrt(mean(centred * centred) + EPS)
        unit5 = centred * scale
        out[0] = (unit5 * g5[...]).astype(BF16)
        grad = og[0].astype(F32)
        both = grad * unit5
        inner = grad * g5[...]
        accumulate(ln5, jnp.sum(both, axis=0, keepdims=True))
        gx4 = scale * (inner - mean(inner) - unit5 * mean(inner * unit5))
        gf_low = (0.5 * gx4).astype(BF16)
        gf[0] = gf_low
        for at in range(0, FF, D):
            hidden = (dot_t(gf_low, w4[at : at + D, :]) * slope[:, at : at + D].astype(F32)).astype(BF16)
            gh[0, :, at : at + D] = hidden
        back, gain4 = norm_back(dot_t(gh[0], w3[...]), low, scale4, g4[...])
        accumulate(ln4, gain4)
        grad3 = gx4 + back
        gx3[0] = grad3
        ge_low = grad3.astype(BF16)
        ge[0] = ge_low
        batch_grad = dot_t(ge_low, w_conv[...]) * conv_slope
        gbn[0] = batch_grad.astype(BF16)
        accumulate(
            sums,
            jnp.concatenate(
                [
                    jnp.sum(batch_grad * unit, axis=0, keepdims=True),
                    jnp.sum(batch_grad, axis=0, keepdims=True),
                ],
                axis=0,
            ),
        )

    return kernel


def batch_back(gbn, dc, stats, back, bn_gain, count):
    middle, inv = batch_stats(stats, count)
    unit = (dc - middle) * inv
    return bn_gain * inv * (gbn - (back[1:2, :] + unit * back[0:1, :]) / count)


def depth_grad_kernel(count):
    def kernel(gbn, dc, stats, back, bn_gain, v, before, after, keep, _, gd, taps_grad, padded):
        steps = v.shape[1]
        fill_padded(padded, v, before, after, keep)
        grad = batch_back(gbn[0].astype(F32), dc[0], stats, back, bn_gain[...], count)
        gd[0] = grad.astype(BF16)
        columns = []
        for at in range(0, D, 128):
            piece = grad[:, at : at + 128]
            rows = [
                jnp.sum(padded[at // 128, k + 1 : k + 1 + steps, :] * piece, axis=0, keepdims=True)
                for k in range(KERNEL)
            ]
            columns.append(jnp.concatenate(rows + [jnp.zeros((1, 128), F32)], axis=0))
        accumulate(taps_grad, jnp.concatenate(columns, axis=1))

    return kernel


def conv_back_kernel(
    gd, before, after, keep, taps, sq, cq, w_conv, a3, r3, g3, gx3, w_out, gs, yd, ce, block,
    gq, gx2, gz, gy, gg, pulled, ln3,
    padded,
):
    steps = gd.shape[1]
    fill_padded(padded, gd, before, after, keep)
    for at in range(0, D, 128):
        running = jnp.zeros((steps, 128), F32)
        for k in range(KERNEL):
            running += padded[at // 128, 15 - k : 15 - k + steps, :] * taps[k : k + 1, at : at + 128]
        gq[0, :, at : at + 128] = (running * sq[0, :, at : at + 128].astype(F32)).astype(BF16)
        gq[0, :, D + at : D + at + 128] = (running * cq[0, :, at : at + 128].astype(F32)).astype(BF16)
    back, gain = norm_back(dot_t(gq[0], w_conv[...]), a3[0], r3[0], g3[...])
    accumulate(ln3, gain)
    grad = gx3[0] + back
    gx2[0] = grad
    low = grad.astype(BF16)
    gz[0] = low
    inner = dot_t(low, w_out[...])
    gg[0] = (inner * yd[0].astype(F32)).astype(BF16)
    read_grad = (inner * gs[0].astype(F32)).astype(BF16)
    gy[0] = read_grad
    row = pl.program_id(0)
    for a, pair in enumerate(pack_state(t_dot(ce[0], read_grad))):
        pulled[0, STATE * a : STATE * (a + 1), :] = pair * keep[0, row]
    pulled[0, 4 * STATE :, :] = block[0, 4 * STATE :, :]


def mix_back_kernel(
    u, bs, c, ee, gy, start, pairs, decay_pairs, _,
    gu, gb, gc,
    full, grads_by, keys_by, reads_by, scores_rows, scores_lanes,
):
    steps = u.shape[1]
    unpack_state(start, full)
    reads_grad = dot_t(gy[0], full[...]) * ee[0].astype(F32)
    keys_grad = jnp.zeros((steps, 256), F32)
    for q in range(2):
        values = u[0, :, 256 * q : 256 * q + 256]
        grads = gy[0, :, 256 * q : 256 * q + 256]
        for b in range(4):
            here = slice(steps * b, steps * (b + 1))
            mask = lane_mask(256, STATE, 4 * q + b)
            grads_by[here, :] = grads * lane_mask(256, HEADP, b)
            keys_by[here, :] = bs[0] * mask
            reads_by[here, :] = c[0] * mask
        for b in range(4):
            here = slice(steps * b, steps * (b + 1))
            scores = dot_t(grads_by[here, :], values) * decay_pairs[0, 4 * q + b].astype(F32)
            scores = scores.astype(BF16)
            scores_rows[here, :] = scores
            scores_lanes[:, here] = scores
        heads = pairs[0, 4 * q : 4 * q + 4].reshape(4 * steps, steps)
        gu[0, :, 256 * q : 256 * q + 256] = t_dot(heads, grads_by[...]).astype(BF16)
        reads_grad += dot(scores_lanes[...], keys_by[...])
        keys_grad += t_dot(scores_rows[...], reads_by[...])
    gc[0] = reads_grad.astype(BF16)
    gb[0] = keys_grad.astype(BF16)


def mix_end_kernel(
    end, u, bt, te, se, gu, gb, gc, gg, w_in, a2, r2, g2, gx2, _,
    gp, gx1, gf, ln2,
    full,
):
    unpack_state(end, full)
    gp[0, :, :D] = (gu[0].astype(F32) + dot(bt[0], full[...])).astype(BF16)
    gp[0, :, D : 2 * D] = gg[0]
    keys_grad = gb[0].astype(F32) + te[0].astype(F32) * dot_t(u[0], full[...])
    gp[0, :, 2 * D : 2 * D + 256] = (keys_grad * se[0].astype(F32)).astype(BF16)
    gp[0, :, 2 * D + 256 :] = gc[0]
    back, gain = norm_back(dot_t(gp[0], w_in[...]), a2[0], r2[0], g2[...])
    accumulate(ln2, gain)
    grad = gx2[0] + back
    gx1[0] = grad
    gf[0] = (0.5 * grad).astype(BF16)


def front_back_kernel(
    gx1, gf, w2, d1, w1, a1, r1, g1, w_sub, tk, fk, _,
    gh, gxr, fg, ln1,
    mel_rows,
):
    steps = gx1.shape[1]
    low = gf[0]
    for at in range(0, FF, D):
        hidden = (dot_t(low, w2[at : at + D, :]) * d1[0, :, at : at + D].astype(F32)).astype(BF16)
        gh[0, :, at : at + D] = hidden
    back, gain = norm_back(dot_t(gh[0], w1[...]), a1[0], r1[0], g1[...])
    accumulate(ln1, gain)
    low = (gx1[0] + back).astype(BF16)
    gxr[0] = low
    frames = dot_t(low, w_sub[...])
    mels = fk.shape[1]
    here = pl.ds(pl.program_id(0), 1)
    keep_mels = fk[here, :].astype(F32)
    for j in range(SUB):
        mel_rows[pl.ds(j, steps, stride=SUB), :] = frames[:, mels * j : mels * (j + 1)] * keep_mels
    fg[0] = mel_rows[...].T * tk[here, :].astype(F32)


def by_share_store(out, at, share, start, block):
    for piece in range(block.shape[0] // share):
        row = start + share * piece
        place = row // (4 * share) * share
        k = row % (4 * share) // share
        out[place : place + share, at + D * k : at + D * (k + 1)] = block[
            share * piece : share * (piece + 1), :
        ]


def late_weights_kernel(share):
    def kernel(a4, e, s4, gh, ge, gf, out):
        left = a4[...].T
        for at in range(0, FF, D):
            out[:, at : at + D] = dot(left, gh[:, at : at + D])
        for at in range(0, 1024, 256):
            by_share_store(out, FF, share, at, dot(s4[:, at : at + 256].T, gf[...]))
        out[:, 2 * FF :] = dot(e[...].T, ge[...])

    return kernel


def turned(place, share, core, block):
    rows = block.T
    half = rows.shape[0] // 2
    for s in range(rows.shape[0] // share):
        side = core if s % 2 == 0 else 1 - core
        at = pl.multiple_of(side * half + s // 2 * share, 16)
        place[pl.ds(at, share), :] = rows[s * share : (s + 1) * share, :]


def turned_by_share(place, share, core, block, at_block):
    for at in range(0, D, 256):
        rows = block[:, at : at + 256].T
        for piece in range(256 // share):
            here = at + share * piece
            first, k = here // (4 * share), here % (4 * share) // share
            side = core if first % 2 == 0 else 1 - core
            to = side * (D // 2) + D * k + (at_block * (D // (8 * share)) + first // 2) * share
            place[pl.ds(pl.multiple_of(to, 16), share), :] = rows[share * piece : share * (piece + 1), :]


def weights_kernel(pairs, share, waits, cuts):
    has_small = pairs[-1] == (1, 0)

    def kernel(core_ref, *refs):
        count = len(pairs)
        lefts, rights = refs[:count], refs[count : 2 * count]
        lines = refs[2 * count : 2 * count + 6 * has_small]
        kept, *sents = refs[2 * count + 6 * has_small + waits :][: len(cuts)]
        places = refs[2 * count + 6 * has_small + waits + len(cuts) :]

        def send(change):
            for sent, low, high in zip(sents, cuts, cuts[1:]):
                pl.when((step >= low) & (step < high))(lambda sent=sent: change(sent))

        step = pl.program_id(0)
        core = core_ref[0]
        start = 0
        for (wide, long), left, right, place in zip(pairs, lefts, rights, places[:count]):
            steps = max(wide, long)

            if wide == 1:

                @pl.when(step == start)
                def _(left=left, place=place):
                    turned(place, share, core, left[...])

            else:

                @pl.when((step > start - wide) & (step <= start))
                def _(left=left, place=place, before=start - wide + 1):
                    turned_by_share(place, share, core, left, step - before)

            @pl.when((step >= start) & (step < start + steps))
            def _(right=right, place=place, wide=wide, start=start):
                if wide == 1:
                    rows = place[...]
                else:
                    rows = place[pl.ds(pl.multiple_of((step - start) * D, D), D), :]
                block = dot(rows, right[...])
                kept[...] = block[: D // 2, :]

                def put(sent):
                    sent[...] = block[D // 2 :, :]

                send(put)

            start += steps
        if has_small:

            @pl.when(step == start - 1)
            def _():
                stacked = jnp.concatenate([line[...] for line in lines] + [jnp.zeros((107, D), F32)], axis=0)
                places[-1][...] = stacked.T
                for s in range(D // share // 2):
                    for out, side in ((kept, core), (sents[-1], 1 - core)):
                        at = pl.multiple_of((2 * s + side) * share, 8)
                        out[s * share : (s + 1) * share, D - 128 :] = places[-1][pl.ds(at, share), :]

    return kernel


def weight_sums(pairs, share, core, small=None, after=(), pieces=1):
    tokens = pairs[0][0].shape[0]
    sizes = [(l.shape[1] // D, r.shape[1] // D) for l, r in pairs]
    if small is not None:
        sizes[-1] = (1, 0)
    lefts, rights, start = [], [], 0
    for (left, right), (wide, long) in zip(pairs, sizes):
        steps = max(wide, long)
        if wide == 1:
            lefts.append((left, "all"))
        else:
            index = lambda j, first=start - wide + 1, last=wide - 1: (0, jnp.clip(j - first, 0, last))
            lefts.append((left, pl.BlockSpec((tokens, D), index)))
        if wide == 1 and long > 1:
            index = lambda j, start=start, last=steps - 1: (0, jnp.clip(j - start, 0, last))
            rights.append((right, pl.BlockSpec((tokens, D), index)))
        else:
            rights.append((right, "all"))
        start += steps
    columns = start * D
    extra = [] if small is None else [(line, "all") for line in small]
    cuts = [start * i // pieces for i in range(pieces + 1)]

    def half(low, high):
        index = lambda j: (0, jnp.clip(j - low, 0, high - low - 1))
        return ((D // 2, D * (high - low)), F32, pl.BlockSpec((D // 2, D), index))

    kept, *sent, token = call(
        weights_kernel(sizes, share, len(after), cuts),
        (start,),
        [(core, scalars())] + lefts + rights + extra + [(a, anywhere()) for a in after],
        [half(0, start)] + [half(low, high) for low, high in zip(cuts, cuts[1:])],
        [pltpu.VMEM((D * wide, tokens), BF16) for wide, _ in sizes]
        + [pltpu.VMEM((D, 128), F32)] * (small is not None),
        2 * tokens * D * columns,
        "weights",
    )
    return kept, sent, token


def row_spec(shape):
    rest = len(shape) - 1
    return pl.BlockSpec((1,) + tuple(shape[1:]), lambda r: (r,) + (0,) * rest)


def whole_spec(shape):
    return pl.BlockSpec(tuple(shape), lambda r: (0,) * len(shape))


def held_spec(shape):
    return pl.BlockSpec(tuple(shape), lambda r: (0,) * len(shape), pipeline_mode=pl.Buffered(1))


def scalars():
    return pl.BlockSpec(memory_space=pltpu.SMEM)


def anywhere():
    return pl.BlockSpec(memory_space=pl.ANY)


ROOM = {'front': 44, 'mix': 24, 'lift': 28, 'depth': 20, 'late': 44, 'late_weights': 36, 'depth_grad': 20, 'conv_back': 28, 'mix_back': 28, 'mix_end': 24, 'front_back': 32, 'weights': 28}
HOP_COST = 30e9
TIMES = {'front': 40.0, 'mix': 14.0, 'lift': 18.0, 'depth': 12.0, 'late': 46.0, 'late_weights': 22.0, 'depth_grad': 26.0, 'conv_back': 4, 'mix_back': 24.0, 'mix_end': 4.0, 'front_back': 60, 'weights': 20.0}


def call(kernel, grid, ins, outs, scratch=(), flops=0, name=None):
    def placed(array, kind):
        if kind not in ("row", "all") and kind.memory_space is not None:
            return array
        return pltpu.with_memory_space_constraint(array, pltpu.HBM)

    def made(kind, shape):
        if kind == "row":
            return row_spec(shape)
        return whole_spec(shape) if kind == "all" else kind

    moved = sum(a.size * a.dtype.itemsize for a, _ in ins)
    inner = len(ins) + len(outs)

    def with_token(*refs):
        kernel(*refs[:inner], *refs[inner + 1 :])
        refs[inner][...] = jnp.zeros((8, 128), F32)

    *made_arrays, token = pl.pallas_call(
        with_token,
        grid=grid,
        in_specs=[held_spec(a.shape) if kind == "all" else made(kind, a.shape) for a, kind in ins],
        out_specs=[made(kind, shape) for shape, _, kind in outs] + [whole_spec((8, 128))],
        out_shape=[pltpu.HBM(shape, kind) for shape, kind, _ in outs] + [pltpu.HBM((8, 128), F32)],
        scratch_shapes=list(scratch),
        compiler_params=pltpu.CompilerParams(
            dimension_semantics=("arbitrary",), vmem_limit_bytes=ROOM[name] * 2**20
        ),
        cost_estimate=pl.CostEstimate(
            flops=int(TIMES[name] * 1.15e9), bytes_accessed=0, transcendentals=0
        ),
        name=name,
    )(*[placed(a, kind) for a, kind in ins])
    return (*made_arrays, token)


def flip_pairs(count, mask):
    return [(i, i ^ mask) for i in range(count)]


def hop_kernel(backward, first, keep_state, waits):
    def kernel(keep, second_ref, value, other, *refs):
        refs = refs[waits:]
        before, (out, out_before, token) = (None, refs) if first else (refs[0], refs[1:])
        token[...] = jnp.zeros((8, 128), F32)
        second = (second_ref[0] != 0) != backward
        rows = value.shape[0]
        decay_rows = slice(4 * STATE, 4 * STATE + 8)
        for r in range(rows):
            here, there = value[r, decay_rows, :], other[r, decay_rows, :]
            out[r, decay_rows, :] = here * there
            if first:
                entered = jnp.where(second, there, 1.0)
            else:
                entered = before[r, decay_rows, :]
                entered = jnp.where(second, entered * there, entered)
            out_before[r, decay_rows, :] = entered
            for a in range(4):
                at = slice(STATE * a, STATE * (a + 1))
                mine, others = value[r, at, :], other[r, at, :]
                mine_decay, other_decay = here[a : a + 1, :], there[a : a + 1, :]
                out[r, at, :] = jnp.where(
                    second, mine_decay * others + mine, other_decay * mine + others
                )
                if first:
                    entered = jnp.where(second, others, 0.0)
                else:
                    entered = before[r, at, :]
                    own = before[r, 4 * STATE + a : 4 * STATE + a + 1, :]
                    entered = jnp.where(second, own * others + entered, entered)
                out_before[r, at, :] = entered * keep[0, r] if keep_state else entered

    return kernel


def entering(value, backward, keep, meanwhile=lambda tokens: []):
    count, place = lax.axis_size("seq"), lax.axis_index("seq")
    vmem = pl.BlockSpec(memory_space=pltpu.VMEM)
    shape = jax.ShapeDtypeStruct(value.shape, F32)
    before, tokens = [], []
    for bit in range(count.bit_length() - 1):
        other = lax.ppermute(value, "seq", flip_pairs(count, 1 << bit))
        last = (2 << bit) == count
        after = meanwhile(tokens) if last else []
        value, entered, token = pl.pallas_call(
            hop_kernel(backward, bit == 0, last and not backward, len(after)),
            in_specs=[scalars()] * 2 + [vmem] * 2 + [anywhere()] * len(after) + [vmem] * len(before),
            out_specs=[vmem] * 3,
            out_shape=[shape, shape, jax.ShapeDtypeStruct((8, 128), F32)],
            compiler_params=pltpu.CompilerParams(vmem_limit_bytes=8 * 2**20),
            cost_estimate=pl.CostEstimate(
                flops=int(HOP_COST) if backward and bit == 1 else 0, bytes_accessed=0, transcendentals=0
            ),
            name="hop",
        )(keep, ((place >> bit) & 1).reshape(1), value, other, *after, *before)
        before = [entered]
        tokens.append(token)
    return before[0]


def halos(top, bottom):
    count = lax.axis_size("seq")
    ends = range(count - 1)
    return (
        lax.ppermute(bottom, "seq", [(i, i + 1) for i in ends]),
        lax.ppermute(top, "seq", [(i + 1, i) for i in ends]),
    )


def sum_over_all(value):
    count = lax.axis_size("seq") * lax.axis_size("rec")
    copies = jnp.broadcast_to(value[None], (count,) + value.shape)
    return jnp.sum(lax.all_to_all(copies, ("rec", "seq"), 0, 0), axis=0)


def scatter_sum(value):
    return lax.psum_scatter(value, "seq", scatter_dimension=0, tiled=True)


def in_vmem(kernel, scalars_in, ins, outs, after, name, cost=0):
    vmem = pl.BlockSpec(memory_space=pltpu.VMEM)
    return pl.pallas_call(
        kernel,
        in_specs=[scalars()] + [vmem] * len(ins) + [anywhere()] * len(after),
        out_specs=[vmem] * len(outs) + [vmem],
        out_shape=[jax.ShapeDtypeStruct(shape, F32) for shape in outs + [(8, 128)]],
        compiler_params=pltpu.CompilerParams(vmem_limit_bytes=8 * 2**20),
        cost_estimate=pl.CostEstimate(
            flops=int(cost * 1.15e9), bytes_accessed=0, transcendentals=0
        ),
        name=name,
    )(scalars_in, *ins, *after)


def part_rows(ref, group, chunk, side, columns):
    if chunk % 8:
        low = ref[2 * group * chunk : (2 * group + 1) * chunk, columns]
        high = ref[(2 * group + 1) * chunk : (2 * group + 2) * chunk, columns]
        return jnp.where(side == 0, low, high)
    return ref[pl.ds(pl.multiple_of((2 * group + side) * chunk, 8), chunk), columns]


def split_task(groups):
    arrays, outs, plan = [], [], []

    def known(array):
        for i, other in enumerate(arrays):
            if other is array:
                return i
        arrays.append(array)
        return len(arrays) - 1

    for items, chunk, bit in groups:
        rows = items[0][0].shape[0]
        placed, at = [], 0
        for kept, first, received, other_first, columns in items:
            there = None if received is None else known(received)
            placed.append((known(kept), first, there, other_first, columns, at))
            at += columns
        plan.append((placed, rows, chunk, bit, len(outs)))
        outs += [(rows // 2, at)] * 2

    def body(bit_ref, ins, made):
        for placed, rows, chunk, bit, out in plan:
            mine = bit_ref[bit]
            for kept, first, received, other_first, columns, at in placed:
                mine_at = slice(first, first + columns)
                other_at = slice(other_first, other_first + columns)
                for target, side in ((made[out], mine), (made[out + 1], 1 - mine)):
                    for group in range(rows // chunk // 2):
                        value = part_rows(ins[kept], group, chunk, side, mine_at)
                        if received is not None:
                            value = value + part_rows(ins[received], group, chunk, side, other_at)
                        target[group * chunk : (group + 1) * chunk, at : at + columns] = value

    return arrays, outs, body


def add_task(kept, received):
    def body(_, ins, made):
        made[0][...] = ins[0][...] + ins[1][...]

    return [kept, received], [kept.shape], body


def join_task(mine, other, bit, pieces=None):
    rows, columns = mine.shape
    cuts = [(0, columns, False)] if pieces is None else pieces
    outs = [(8 * rows, D) if spread else (2 * rows, wide) for _, wide, spread in cuts]

    def body(bit_ref, ins, made):
        first = bit_ref[bit] == 0
        for target, (at, wide, spread) in zip(made, cuts):
            for k in range(4 if spread else 1):
                width = D if spread else wide
                left = ins[0][:, at + D * k : at + D * k + width]
                right = ins[1][:, at + D * k : at + D * k + width]
                start = 2 * rows * k
                target[start : start + rows, :] = jnp.where(first, left, right)
                target[start + rows : start + 2 * rows, :] = jnp.where(first, right, left)

    return [mine, other], outs, body


def together(bits, sums, after, cost=0):
    tasks = [one.step() for one in sums]
    arrays = [array for ins, _, _, _ in tasks for array in ins]
    outs = [shape for _, shapes, _, _ in tasks for shape in shapes]
    count = len(arrays) + len(after)

    def kernel(bit_ref, *refs):
        at, out = 0, count
        for ins, shapes, body, _ in tasks:
            body(bit_ref, refs[at : at + len(ins)], refs[out : out + len(shapes)])
            at, out = at + len(ins), out + len(shapes)
        refs[-1][...] = jnp.zeros((8, 128), F32)

    *made, token = in_vmem(kernel, bits, arrays, outs, after, "together", cost)
    for _, shapes, _, commit in tasks:
        commit(made[: len(shapes)])
        made = made[len(shapes) :]
    return token


class Sum:
    def __init__(self, pieces):
        self.pieces = pieces
        self.chip_bits = lax.axis_size("seq").bit_length() - 2
        self.rec_bits = lax.axis_size("rec").bit_length() - 1
        self.parts, self.left, self.steps, self.beside = [], [], [], []
        self.done = None

    def swap(self, value, axis, bit):
        return lax.ppermute(value, axis, flip_pairs(lax.axis_size(axis), 1 << bit))

    def begin(self, kept, sent, first):
        self.parts = [[], []]
        at = 0
        for piece in sent:
            received = self.swap(piece, "seq", 0)
            end = at + piece.shape[1]
            for part, low, high in ((0, at, min(end, first)), (1, max(at, first), end)):
                if low < high:
                    self.parts[part].append((kept, low, received, low - at, high - low))
            at = end
        turn = 1 + self.chip_bits // 2
        orders = (
            list(range(1, self.chip_bits + 1)),
            list(range(turn, self.chip_bits + 1)) + list(range(1, turn)),
        )
        self.left = [list(range(self.chip_bits, 0, -1)) for _ in orders]
        self.steps += [("chips", now) for now in zip(*orders)]
        self.steps += [("rec", bit) for bit in range(self.rec_bits)] + [("turn", self.rec_bits - 1)]
        self.steps += [("join", bit) for bit in reversed(range(self.rec_bits))]

    def step(self):
        kind, now = self.steps.pop(0)
        if kind == "chips":
            groups = []
            for items, bit, left in zip(self.parts, now, self.left):
                chunk = items[0][0].shape[0] >> (left.index(bit) + 1)
                left.remove(bit)
                groups.append((items, chunk, bit))

            def commit(made):
                self.parts = [
                    [(made[2 * i], 0, self.swap(made[2 * i + 1], "seq", bit), 0, made[2 * i].shape[1])]
                    for i, bit in enumerate(now)
                ]

            return *split_task(groups), commit
        if kind == "rec":
            items = [item for part in self.beside + self.parts for item in part]
            self.beside = []

            def commit(made):
                kept, sent = made
                self.parts = [[(kept, 0, self.swap(sent, "rec", now), 0, kept.shape[1])]]

            chunk = items[0][0].shape[0] // 2
            return *split_task([(items, chunk, self.chip_bits + 1 + now)]), commit
        if kind == "turn":
            [[(kept, _, received, _, _)]] = self.parts

            def commit(made):
                [self.mine] = made
                self.other = self.swap(self.mine, "rec", now)

            return *add_task(kept, received), commit

        def commit(made):
            if now == 0:
                self.done = made
                return
            [self.mine] = made
            self.other = self.swap(self.mine, "rec", now - 1)

        pieces = self.pieces if now == 0 else None
        return *join_task(self.mine, self.other, self.chip_bits + 1 + now, pieces), commit


def local(
    features, time_keep, freq_keep, block_flags, decays, w_sub, ln1_gain, ffn1_in, ffn1_out, ln2_gain,
    ssm_in, ssm_out, ln3_gain, conv_in, conv_depth, bn_gain, bn_shift, conv_out, ln4_gain, ffn2_in,
    ffn2_out, ln5_gain, out_grad,
):
    rows, frame_count, mels = features.shape
    steps = frame_count // SUB
    tokens = rows * steps
    blocks = lax.axis_size("seq")
    place = lax.axis_index("seq")
    count = float(tokens * blocks * lax.axis_size("rec"))
    share = D // blocks
    here = lax.dynamic_index_in_dim(block_flags, place, 1, keepdims=False)
    after = lax.dynamic_index_in_dim(
        block_flags, jnp.minimum(place + 1, blocks - 1), 1, keepdims=False
    )
    keep_here = (1 - here).astype(F32)
    keep_next = jnp.where(place + 1 < blocks, 1 - after, 0).astype(F32)
    keep = (jnp.stack([keep_here, keep_next]), scalars())
    tk = (time_keep, "all")
    fk = (freq_keep, "all")
    g1, g2, g3, g4, g5, bg, bb = (
        (gain.reshape(1, D), "all")
        for gain in (ln1_gain, ln2_gain, ln3_gain, ln4_gain, ln5_gain, bn_gain, bn_shift)
    )
    taps = (jnp.pad(conv_depth.T, ((0, 1), (0, 0))), "all")

    def rows_of(width, kind=F32):
        return ((rows, steps, width), kind, "row")


    per_state = ((rows, 4 * STATE + 8, 128), F32, "row")
    edge = ((rows, 8, D), F32, "row")
    line = ((1, D), F32, "all")
    two_lines = ((2, D), F32, "all")
    padded = pltpu.VMEM((D // 128, steps + 16, 128), F32)
    full = pltpu.VMEM((256, D), BF16)

    def row(value):
        return (value, "row")

    def every(value):
        return (value, "all")

    (flat, x1, a1, r1, s1, d1, a2, r2, u, g, bs, c, ce, bt, se, ee, te, cum, cum_t, state, _) = call(
        front_kernel,
        (rows,),
        [
            row(features.transpose(0, 2, 1)), tk, fk, row(decays), keep,
            every(w_sub.T), g1, every(ffn1_in), every(ffn1_out), g2, every(ssm_in),
        ],
        [
            rows_of(WIDE, BF16), rows_of(D), rows_of(D, BF16), rows_of(1), rows_of(FF, BF16),
            rows_of(FF, BF16), rows_of(D, BF16), rows_of(1), rows_of(D, BF16), rows_of(D, BF16),
            rows_of(256, BF16), rows_of(256, BF16), rows_of(256, BF16), rows_of(256, BF16),
            rows_of(256, BF16), rows_of(256, BF16), rows_of(256, BF16), rows_of(HEADS),
            ((rows, HEADS, steps), F32, "row"), per_state,
        ],
        [pltpu.VMEM((frame_count, mels), F32)],
        2 * tokens * D * (WIDE + 2 * FF + PROJ),
        "front",
    )
    start = entering(state, False, keep[0])
    pair_shape = ((rows, HEADS, steps, steps), BF16, "row")
    mixed, pairs, decay_pairs, _ = call(
        mix_kernel,
        (rows,),
        [row(u), row(bs), row(c), row(cum), row(cum_t)],
        [rows_of(D, BF16), pair_shape, pair_shape],
        (),
        2 * tokens * 256 * 256 * 16,
        "mix",
    )
    z, gs, yd, x2, a3, r3, v, sq, cq, top, bottom, _ = call(
        lift_kernel,
        (rows,),
        [row(mixed), row(ce), row(start), row(g), row(x1), every(ssm_out), g3, every(conv_in)],
        [
            rows_of(D, BF16), rows_of(D, BF16), rows_of(D, BF16), rows_of(D), rows_of(D, BF16),
            rows_of(1), rows_of(D), rows_of(D, BF16), rows_of(D, BF16), edge, edge,
        ],
        [full],
        2 * tokens * D * 4 * D,
        "lift",
    )
    v_before, v_after = halos(top, bottom)
    dc, sums, _ = call(
        depth_kernel,
        (rows,),
        [row(v), row(v_before), row(v_after), keep, taps],
        [rows_of(D), two_lines],
        [padded],
        2 * tokens * D * 64,
        "depth",
    )
    stats = sum_over_all(sums)
    out, e, a4, s4, gf4, gh4, ge, gx3, gbn, back_sums, ln4, ln5, _ = call(
        late_kernel(count),
        (rows,),
        [
            row(dc), row(x2), row(out_grad), every(stats), bg, bb, every(conv_out), g4,
            every(ffn2_in), every(ffn2_out), g5,
        ],
        [
            rows_of(D, BF16), rows_of(D, BF16), rows_of(D, BF16), rows_of(FF, BF16), rows_of(D, BF16),
            rows_of(FF, BF16), rows_of(D, BF16), rows_of(D), rows_of(D, BF16), two_lines, line, line,
        ],
        [pltpu.VMEM((steps, FF), BF16)],
        2 * tokens * D * (4 * FF + 2 * D),
        "late",
    )
    back = sum_over_all(back_sums)

    def flatten(value):
        return value.reshape(tokens, value.shape[-1])

    def column_block(value, width):
        return (flatten(value), pl.BlockSpec((tokens, width), lambda i: (0, i)))

    def row_block(columns):
        return ((D, columns), F32, pl.BlockSpec((256, columns), lambda i: (i, 0)))

    late_grads, late_token = call(
        late_weights_kernel(share),
        (2,),
        [
            column_block(a4, 256), column_block(e, 256), column_block(s4, 1024),
            every(flatten(gh4)), every(flatten(ge)), every(flatten(gf4)),
        ],
        [row_block(2 * FF + D)],
        (),
        2 * tokens * D * (2 * FF + D),
        "late_weights",
    )
    scattered_a = scatter_sum(late_grads)

    def edge_grad(at):
        return batch_back(
            lax.slice_in_dim(gbn, at, at + 8, axis=1).astype(F32),
            lax.slice_in_dim(dc, at, at + 8, axis=1),
            stats, back, bn_gain, count,
        )

    gd_before, gd_after = halos(edge_grad(0), edge_grad(steps - 8))
    gd, taps_grad, _ = call(
        depth_grad_kernel(count),
        (rows,),
        [
            row(gbn), row(dc), every(stats), every(back), bg, row(v), row(v_before), row(v_after), keep,
            (late_token, anywhere()),
        ],
        [rows_of(D, BF16), ((16, D), F32, "all")],
        [padded],
        2 * tokens * D * 64,
        "depth_grad",
    )
    gq, gx2, gz, gy, gg, pulled, ln3, _ = call(
        conv_back_kernel,
        (rows,),
        [
            row(gd), row(gd_before), row(gd_after), keep, taps, row(sq), row(cq), every(conv_in),
            row(a3), row(r3), g3, row(gx3), every(ssm_out), row(gs), row(yd), row(ce), row(state),
        ],
        [
            rows_of(2 * D, BF16), rows_of(D), rows_of(D, BF16), rows_of(D, BF16), rows_of(D, BF16),
            per_state, line,
        ],
        [padded],
        2 * tokens * D * 4 * D,
        "conv_back",
    )
    core = (place % 2).reshape(1)
    bits = jnp.stack(
        [(place >> k) & 1 for k in range(blocks.bit_length() - 1)]
        + [(lax.axis_index("rec") >> k) & 1 for k in range(lax.axis_size("rec").bit_length() - 1)]
    )
    early = Sum(
        [
            (0, FF, False), (FF, FF, True), (2 * FF, D, False), (2 * FF + D, 2 * D, False),
            (2 * FF + 3 * D, D, False),
        ],
    )
    found = {}

    def beside(hops):
        kept, sent, weights_token = weight_sums(
            [(flatten(a3), flatten(gq)), (flatten(z), flatten(gz))], share, core, None, hops[-2:-1]
        )
        early.begin(kept, sent, 3 * D // 2)
        token = together(bits, [early], [weights_token, hops[-1]])
        gu, gb, gc, mixed_token = call(
            mix_back_kernel,
            (rows,),
            [
                row(u), row(bs), row(c), row(ee), row(gy), row(start), row(pairs), row(decay_pairs),
                (token, anywhere()),
            ],
            [rows_of(D, BF16), rows_of(256, BF16), rows_of(256, BF16)],
            [full] + [pltpu.VMEM((4 * steps, 256), BF16)] * 4 + [pltpu.VMEM((steps, 4 * steps), BF16)],
            2 * tokens * 256 * 256 * 32,
            "mix_back",
        )
        found["mixed"] = (gu, gb, gc, mixed_token)
        return [mixed_token]

    end = entering(pulled, True, keep[0], beside)
    gu, gb, gc, mixed_token = found["mixed"]
    gp, gx1, gf1, ln2, end_token = call(
        mix_end_kernel,
        (rows,),
        [
            row(end), row(u), row(bt), row(te), row(se), row(gu), row(gb), row(gc), row(gg),
            every(ssm_in), row(a2), row(r2), g2, row(gx2), (mixed_token, anywhere()),
        ],
        [rows_of(PROJ, BF16), rows_of(D), rows_of(D, BF16), line],
        [full],
        2 * tokens * D * PROJ,
        "mix_end",
    )
    token = together(bits, [early], [end_token])
    kept, sent, weights_token = weight_sums(
        [(flatten(a2), flatten(gp)), (flatten(s1), flatten(gf1))], share, core, None, [token]
    )
    middle = Sum([(0, PROJ, False), (PROJ, FF, True)])
    middle.begin(kept, sent, (PROJ + FF) // 2)
    token = weights_token
    while early.steps[0][0] == "chips":
        token = together(bits, [early], [token])
    early.parts = [[(scattered_a, 0, None, 0, scattered_a.shape[1])]] + early.parts
    token = together(bits, [early], [token])
    gh1, gxr, features_grad, ln1, back_token = call(
        front_back_kernel,
        (rows,),
        [
            row(gx1), row(gf1), every(ffn1_out), row(d1), every(ffn1_in), row(a1), row(r1), g1,
            every(w_sub.T), tk, fk, (token, anywhere()),
        ],
        [rows_of(FF, BF16), rows_of(D, BF16), ((rows, mels, frame_count), F32, "row"), line],
        [pltpu.VMEM((frame_count, mels), F32)],
        2 * tokens * D * (WIDE + 2 * FF),
        "front_back",
    )
    small = [taps_grad, ln1, ln2, ln3, ln4, ln5]
    token = together(bits, [middle], [back_token])
    token = together(bits, [early], [token])
    last = Sum([(0, FF, False), (FF, SUB * mels, False), (FF + D - 128, 128, False)])
    kept, sent, weights_token = weight_sums(
        [(flatten(a1), flatten(gh1)), (flatten(gxr), flatten(flat))], share, core, small, [token], 1
    )
    last.begin(kept, sent, (FF + WIDE) // 2)
    token = weights_token
    token = together(bits, [early, middle], [token], 60.0)
    rounds = [(last,), (early, middle, last), (middle, last)]
    while early.steps or middle.steps or last.steps:
        now = rounds.pop(0) if rounds else (early, middle, last)
        now = [one for one in now if one.steps]
        if now:
            token = together(bits, now, [token])
    ffn2_in_grad, ffn2_out_grad, conv_out_grad, conv_in_grad, ssm_out_grad = early.done
    ssm_in_grad, ffn1_out_grad = middle.done
    ffn1_in_grad, w_sub_grad, gains = last.done

    start_row = place * share
    return (
        out,
        features_grad.transpose(0, 2, 1),
        w_sub_grad,
        gains[:, 16],
        ffn1_in_grad,
        ffn1_out_grad,
        gains[:, 17],
        ssm_in_grad,
        ssm_out_grad,
        gains[:, 18],
        conv_in_grad,
        gains[:, :KERNEL],
        lax.dynamic_slice_in_dim(back[0], start_row, share),
        lax.dynamic_slice_in_dim(back[1], start_row, share),
        conv_out_grad,
        gains[:, 19],
        ffn2_in_grad,
        ffn2_out_grad,
        gains[:, 20],
    )


def solution(mesh):
    block = P("rec", "seq", None)
    rows_of_seq, line = P("seq", None), P("seq")
    return jax.shard_map(
        local,
        mesh=mesh,
        in_specs=(block, P("rec", "seq"), P("rec", None), P("rec", None), P("rec", None, "seq"))
        + (P(),) * 17
        + (block,),
        out_specs=(
            block, block, rows_of_seq, line, rows_of_seq, rows_of_seq, line, rows_of_seq, rows_of_seq,
            line, rows_of_seq, rows_of_seq, line, line, rows_of_seq, line, rows_of_seq, rows_of_seq, line,
        ),
        check_vma=False,
    )
```

```python
import jax
import jax.numpy as jnp
from jax import lax
from jax.experimental import pallas as pl
from jax.experimental.pallas import tpu as pltpu
from jax.sharding import PartitionSpec as P

D = 512
FF = 2048
HEADS = 8
STATE = 32
SUB = 4
KERNEL = 15
HEADP = 64
PROJ = 1536
WIDE = 512
EPS = 1e-05
F32 = jnp.float32
BF16 = jnp.bfloat16
LIMIT = 32
READ_SCALE = STATE ** (-0.5)


def dot(a, b):
    return lax.dot_general(a, b, (((1,), (0,)), ((), ())), preferred_element_type=F32)


def dot_t(a, b):
    return lax.dot_general(a, b, (((1,), (1,)), ((), ())), preferred_element_type=F32)


def t_dot(a, b):
    return lax.dot_general(a, b, (((0,), (0,)), ((), ())), preferred_element_type=F32)


def sigmoid(x):
    return 0.5 * jnp.tanh(0.5 * x) + 0.5


def mean(x):
    return jnp.mean(x, axis=-1, keepdims=True)


def norm(x, gain):
    centred = x - mean(x)
    scale = lax.rsqrt(mean(centred * centred) + EPS)
    return (centred * scale * gain).astype(BF16), scale


def norm_back(grad, normed, scale, gain):
    wide = normed.astype(F32)
    inverse = 1.0 / gain
    both = grad * wide
    inner = grad * gain
    back = scale * (inner - mean(inner) - wide * inverse * mean(both))
    return back, jnp.sum(both, axis=0, keepdims=True) * inverse


def split_two(x):
    high = x.astype(BF16)
    return high, (x - high.astype(F32)).astype(BF16)


def split_three(x):
    high, rest = split_two(x)
    return high, rest, (x - high.astype(F32) - rest.astype(F32)).astype(BF16)


def iota(shape, dim):
    return lax.broadcasted_iota(jnp.int32, shape, dim)


def lane_mask(columns, width, index):
    lane = iota((16, columns), 1)
    inside = (lane >= width * index) & (lane < width * (index + 1))
    return jnp.where(inside, 1.0, 0.0).astype(BF16)[:1]


def pack_state(full):
    lane = iota((STATE, 128), 1)
    return [
        jnp.where(
            lane < HEADP,
            full[64 * a : 64 * a + 32, 128 * a : 128 * a + 128],
            full[64 * a + 32 : 64 * a + 64, 128 * a : 128 * a + 128],
        )
        for a in range(4)
    ]


def unpack_state(ref, full):
    lane = iota((STATE, 128), 1)
    full[...] = jnp.zeros_like(full)
    for a in range(4):
        pair = ref[0, STATE * a : STATE * (a + 1), :]
        full[64 * a : 64 * a + 32, 128 * a : 128 * a + 128] = jnp.where(
            lane < HEADP, pair, 0.0
        ).astype(BF16)
        full[64 * a + 32 : 64 * a + 64, 128 * a : 128 * a + 128] = jnp.where(
            lane < HEADP, 0.0, pair
        ).astype(BF16)


def accumulate(ref, value):
    first = pl.program_id(0) == 0

    @pl.when(first)
    def _():
        ref[...] = value

    @pl.when(jnp.logical_not(first))
    def _():
        ref[...] += value


def front_kernel(
    feat, tk, fk, dec, keep, w_sub, g1, w1, w2, g2, w_in,
    flat, x1, a1, r1, s1, d1, a2, r2, u, g, bs, c, ce, bt, se, ee, te, cum, cum_t, state,
    frames,
):
    steps = x1.shape[1]
    here = pl.ds(pl.program_id(0), 1)
    kept = feat[0].astype(F32) * tk[here, :].astype(F32)
    frames[...] = kept.T * fk[here, :].astype(F32)
    parts = [frames[pl.ds(j, steps, stride=SUB), :] for j in range(SUB)]
    parts.append(jnp.zeros((steps, WIDE - SUB * parts[0].shape[1]), F32))
    stacked = jnp.concatenate(parts, axis=1).astype(BF16)
    flat[0] = stacked
    x0 = dot(stacked[:, : w_sub.shape[0]], w_sub[...])
    low, scale = norm(x0, g1[...])
    a1[0] = low
    r1[0] = scale
    for at in range(0, FF, D):
        hidden = dot(low, w1[:, at : at + D])
        gate = sigmoid(hidden)
        active = hidden * gate
        d1[0, :, at : at + D] = (gate * (1.0 + hidden - active)).astype(BF16)
        s1[0, :, at : at + D] = active.astype(BF16)
    after = x0 + 0.5 * dot(s1[0], w2[...])
    x1[0] = after
    low, scale = norm(after, g2[...])
    a2[0] = low
    r2[0] = scale
    u_low = dot(low, w_in[:, :D]).astype(BF16)
    u[0] = u_low
    g[0] = dot(low, w_in[:, D : 2 * D]).astype(BF16)
    keys = dot(low, w_in[:, 2 * D : 2 * D + 256])
    reads = dot(low, w_in[:, 2 * D + 256 :])
    log_rows = jnp.log(dec[0])
    log_decay = log_rows.T
    lower = jnp.where(iota((steps, steps), 0) >= iota((steps, steps), 1), 1.0, 0.0).astype(BF16)
    running = sum(dot(lower, part) for part in split_three(log_decay))
    running_t = sum(dot_t(part, lower) for part in split_three(log_rows))
    cum[0] = running
    cum_t[0] = running_t
    spread = jnp.where(iota((HEADS, 256), 1) // STATE == iota((HEADS, 256), 0), 1.0, 0.0).astype(BF16)

    def over_columns(value):
        return sum(dot(part, spread) for part in split_two(value))

    scale_wide = over_columns(jnp.sqrt(-2.0 * log_decay))
    head = jnp.exp(running)
    head_wide = over_columns(head)
    tail_wide = over_columns(jnp.exp(running[steps - 1 :, :] - running))
    se[0] = scale_wide.astype(BF16)
    ee[0] = head_wide.astype(BF16)
    te[0] = tail_wide.astype(BF16)
    keys = keys * scale_wide
    bs[0] = keys.astype(BF16)
    c[0] = reads.astype(BF16)
    ce[0] = (reads * head_wide).astype(BF16)
    tailed = (keys * tail_wide).astype(BF16)
    bt[0] = tailed
    spread_values = jnp.where(iota((HEADS, D), 1) // HEADP == iota((HEADS, D), 0), 1.0, 0.0).astype(BF16)
    block = sum(dot(part, spread_values) for part in split_three(head[steps - 8 :, :]))
    block = block[7:8, :] * keep[0, pl.program_id(0)]
    for a, pair in enumerate(pack_state(t_dot(tailed, u_low))):
        state[0, STATE * a : STATE * (a + 1), :] = pair
    lines = [block[:, 128 * a : 128 * a + 128] for a in range(4)]
    state[0, 4 * STATE :, :] = jnp.concatenate(lines + lines, axis=0)


def mix_kernel(u, bs, c, cum, cum_t, mixed, pairs, decay_pairs):
    steps = u.shape[1]
    causal = iota((steps, steps), 0) >= iota((steps, steps), 1)
    keys = bs[0]
    reads = c[0]
    for q in range(2):
        values = u[0, :, 256 * q : 256 * q + 256]
        total = jnp.zeros((steps, 256), F32)
        for b in range(4):
            h = 4 * q + b
            weights = jnp.exp(
                jnp.where(causal, cum[0, :, h : h + 1] - cum_t[0, h : h + 1, :], -1e30)
            )
            scores = (dot_t(reads * lane_mask(256, STATE, h), keys) * weights).astype(BF16)
            decay_pairs[0, h] = weights.astype(BF16)
            pairs[0, h] = scores
            total += dot(scores, values * lane_mask(256, HEADP, b))
        mixed[0, :, 256 * q : 256 * q + 256] = total.astype(BF16)


def lift_kernel(
    mixed, ce, start, g, x1, w_out, g3, w_conv,
    z, gs, yd, x2, a3, r3, v, sq, cq, top, bottom,
    full,
):
    steps = x1.shape[1]
    unpack_state(start, full)
    y = (mixed[0].astype(F32) + dot(ce[0], full[...])) * READ_SCALE
    gate = g[0].astype(F32)
    sig = sigmoid(gate)
    active = gate * sig
    gs[0] = (active * READ_SCALE).astype(BF16)
    yd[0] = (y * sig * (1.0 + gate - active)).astype(BF16)
    gated = (y * active).astype(BF16)
    z[0] = gated
    after = x1[0] + dot(gated, w_out[...])
    x2[0] = after
    low, scale = norm(after, g3[...])
    a3[0] = low
    r3[0] = scale
    first = dot(low, w_conv[:, :D])
    sig = sigmoid(dot(low, w_conv[:, D:]))
    out = first * sig
    v[0] = out
    sq[0] = sig.astype(BF16)
    cq[0] = (out * (1.0 - sig)).astype(BF16)
    top[0] = out[:8, :]
    bottom[0] = out[steps - 8 :, :]


def fill_padded(padded, body, before, after, keep):
    steps = body.shape[1]
    row = pl.program_id(0)
    for i in range(D // 128):
        columns = slice(128 * i, 128 * i + 128)
        padded[i, :8, :] = before[0, :, columns] * keep[0, row]
        padded[i, 8 : 8 + steps, :] = body[0, :, columns].astype(F32)
        padded[i, 8 + steps :, :] = after[0, :, columns] * keep[1, row]


def depth_kernel(v, before, after, keep, taps, dc, sums, padded):
    steps = v.shape[1]
    fill_padded(padded, v, before, after, keep)
    total, square = [], []
    for at in range(0, D, 128):
        running = jnp.zeros((steps, 128), F32)
        for k in range(KERNEL):
            running += padded[at // 128, k + 1 : k + 1 + steps, :] * taps[k : k + 1, at : at + 128]
        dc[0, :, at : at + 128] = running
        total.append(jnp.sum(running, axis=0, keepdims=True))
        square.append(jnp.sum(running * running, axis=0, keepdims=True))
    accumulate(sums, jnp.concatenate([jnp.concatenate(total, axis=1), jnp.concatenate(square, axis=1)], axis=0))


def batch_stats(stats, count):
    middle = stats[0:1, :] / count
    return middle, lax.rsqrt(stats[1:2, :] / count - middle * middle + EPS)


def late_kernel(count):
    def kernel(
        dc, x2, og, stats, bn_gain, bn_shift, w_conv, g4, w3, w4, g5,
        out, e, a4, s4, gf, gh, ge, gx3, gbn, sums, ln4, ln5,
        slope,
    ):
        middle, inv = batch_stats(stats, count)
        unit = (dc[0] - middle) * inv
        batch = unit * bn_gain[...] + bn_shift[...]
        sig = sigmoid(batch)
        active = batch * sig
        conv_slope = sig * (1.0 + batch - active)
        active = active.astype(BF16)
        e[0] = active
        x3 = x2[0] + dot(active, w_conv[...])
        low, scale4 = norm(x3, g4[...])
        a4[0] = low
        for at in range(0, FF, D):
            hidden = dot(low, w3[:, at : at + D])
            gate = sigmoid(hidden)
            active = hidden * gate
            slope[:, at : at + D] = (gate * (1.0 + hidden - active)).astype(BF16)
            s4[0, :, at : at + D] = active.astype(BF16)
        x4 = x3 + 0.5 * dot(s4[0], w4[...])
        centred = x4 - mean(x4)
        scale = lax.rsqrt(mean(centred * centred) + EPS)
        unit5 = centred * scale
        out[0] = (unit5 * g5[...]).astype(BF16)
        grad = og[0].astype(F32)
        both = grad * unit5
        inner = grad * g5[...]
        accumulate(ln5, jnp.sum(both, axis=0, keepdims=True))
        gx4 = scale * (inner - mean(inner) - unit5 * mean(inner * unit5))
        gf_low = (0.5 * gx4).astype(BF16)
        gf[0] = gf_low
        for at in range(0, FF, D):
            hidden = (dot_t(gf_low, w4[at : at + D, :]) * slope[:, at : at + D].astype(F32)).astype(BF16)
            gh[0, :, at : at + D] = hidden
        back, gain4 = norm_back(dot_t(gh[0], w3[...]), low, scale4, g4[...])
        accumulate(ln4, gain4)
        grad3 = gx4 + back
        gx3[0] = grad3
        ge_low = grad3.astype(BF16)
        ge[0] = ge_low
        batch_grad = dot_t(ge_low, w_conv[...]) * conv_slope
        gbn[0] = batch_grad.astype(BF16)
        accumulate(
            sums,
            jnp.concatenate(
                [
                    jnp.sum(batch_grad * unit, axis=0, keepdims=True),
                    jnp.sum(batch_grad, axis=0, keepdims=True),
                ],
                axis=0,
            ),
        )

    return kernel


def batch_back(gbn, dc, stats, back, bn_gain, count):
    middle, inv = batch_stats(stats, count)
    unit = (dc - middle) * inv
    return bn_gain * inv * (gbn - (back[1:2, :] + unit * back[0:1, :]) / count)


def depth_grad_kernel(count):
    def kernel(gbn, dc, stats, back, bn_gain, v, before, after, keep, _, gd, taps_grad, padded):
        steps = v.shape[1]
        fill_padded(padded, v, before, after, keep)
        grad = batch_back(gbn[0].astype(F32), dc[0], stats, back, bn_gain[...], count)
        gd[0] = grad.astype(BF16)
        columns = []
        for at in range(0, D, 128):
            piece = grad[:, at : at + 128]
            rows = [
                jnp.sum(padded[at // 128, k + 1 : k + 1 + steps, :] * piece, axis=0, keepdims=True)
                for k in range(KERNEL)
            ]
            columns.append(jnp.concatenate(rows + [jnp.zeros((1, 128), F32)], axis=0))
        accumulate(taps_grad, jnp.concatenate(columns, axis=1))

    return kernel


def conv_back_kernel(
    gd, before, after, keep, taps, sq, cq, w_conv, a3, r3, g3, gx3, w_out, gs, yd, ce, block,
    gq, gx2, gz, gy, gg, pulled, ln3,
    padded,
):
    steps = gd.shape[1]
    fill_padded(padded, gd, before, after, keep)
    for at in range(0, D, 128):
        running = jnp.zeros((steps, 128), F32)
        for k in range(KERNEL):
            running += padded[at // 128, 15 - k : 15 - k + steps, :] * taps[k : k + 1, at : at + 128]
        gq[0, :, at : at + 128] = (running * sq[0, :, at : at + 128].astype(F32)).astype(BF16)
        gq[0, :, D + at : D + at + 128] = (running * cq[0, :, at : at + 128].astype(F32)).astype(BF16)
    back, gain = norm_back(dot_t(gq[0], w_conv[...]), a3[0], r3[0], g3[...])
    accumulate(ln3, gain)
    grad = gx3[0] + back
    gx2[0] = grad
    low = grad.astype(BF16)
    gz[0] = low
    inner = dot_t(low, w_out[...])
    gg[0] = (inner * yd[0].astype(F32)).astype(BF16)
    read_grad = (inner * gs[0].astype(F32)).astype(BF16)
    gy[0] = read_grad
    row = pl.program_id(0)
    for a, pair in enumerate(pack_state(t_dot(ce[0], read_grad))):
        pulled[0, STATE * a : STATE * (a + 1), :] = pair * keep[0, row]
    pulled[0, 4 * STATE :, :] = block[0, 4 * STATE :, :]


def mix_back_kernel(
    u, bs, c, ee, gy, start, pairs, decay_pairs, _,
    gu, gb, gc,
    full, grads_by, keys_by, reads_by, scores_rows, scores_lanes,
):
    steps = u.shape[1]
    unpack_state(start, full)
    reads_grad = dot_t(gy[0], full[...]) * ee[0].astype(F32)
    keys_grad = jnp.zeros((steps, 256), F32)
    for q in range(2):
        values = u[0, :, 256 * q : 256 * q + 256]
        grads = gy[0, :, 256 * q : 256 * q + 256]
        for b in range(4):
            here = slice(steps * b, steps * (b + 1))
            mask = lane_mask(256, STATE, 4 * q + b)
            grads_by[here, :] = grads * lane_mask(256, HEADP, b)
            keys_by[here, :] = bs[0] * mask
            reads_by[here, :] = c[0] * mask
        for b in range(4):
            here = slice(steps * b, steps * (b + 1))
            scores = dot_t(grads_by[here, :], values) * decay_pairs[0, 4 * q + b].astype(F32)
            scores = scores.astype(BF16)
            scores_rows[here, :] = scores
            scores_lanes[:, here] = scores
        heads = pairs[0, 4 * q : 4 * q + 4].reshape(4 * steps, steps)
        gu[0, :, 256 * q : 256 * q + 256] = t_dot(heads, grads_by[...]).astype(BF16)
        reads_grad += dot(scores_lanes[...], keys_by[...])
        keys_grad += t_dot(scores_rows[...], reads_by[...])
    gc[0] = reads_grad.astype(BF16)
    gb[0] = keys_grad.astype(BF16)


def mix_end_kernel(
    end, u, bt, te, se, gu, gb, gc, gg, w_in, a2, r2, g2, gx2, _,
    gp, gx1, gf, ln2,
    full,
):
    unpack_state(end, full)
    gp[0, :, :D] = (gu[0].astype(F32) + dot(bt[0], full[...])).astype(BF16)
    gp[0, :, D : 2 * D] = gg[0]
    keys_grad = gb[0].astype(F32) + te[0].astype(F32) * dot_t(u[0], full[...])
    gp[0, :, 2 * D : 2 * D + 256] = (keys_grad * se[0].astype(F32)).astype(BF16)
    gp[0, :, 2 * D + 256 :] = gc[0]
    back, gain = norm_back(dot_t(gp[0], w_in[...]), a2[0], r2[0], g2[...])
    accumulate(ln2, gain)
    grad = gx2[0] + back
    gx1[0] = grad
    gf[0] = (0.5 * grad).astype(BF16)


def front_back_kernel(
    gx1, gf, w2, d1, w1, a1, r1, g1, w_sub, tk, fk, _,
    gh, gxr, fg, ln1,
    mel_rows,
):
    steps = gx1.shape[1]
    low = gf[0]
    for at in range(0, FF, D):
        hidden = (dot_t(low, w2[at : at + D, :]) * d1[0, :, at : at + D].astype(F32)).astype(BF16)
        gh[0, :, at : at + D] = hidden
    back, gain = norm_back(dot_t(gh[0], w1[...]), a1[0], r1[0], g1[...])
    accumulate(ln1, gain)
    low = (gx1[0] + back).astype(BF16)
    gxr[0] = low
    frames = dot_t(low, w_sub[...])
    mels = fk.shape[1]
    here = pl.ds(pl.program_id(0), 1)
    keep_mels = fk[here, :].astype(F32)
    for j in range(SUB):
        mel_rows[pl.ds(j, steps, stride=SUB), :] = frames[:, mels * j : mels * (j + 1)] * keep_mels
    fg[0] = mel_rows[...].T * tk[here, :].astype(F32)


def by_share_store(out, at, share, start, block):
    for piece in range(block.shape[0] // share):
        row = start + share * piece
        place = row // (4 * share) * share
        k = row % (4 * share) // share
        out[place : place + share, at + D * k : at + D * (k + 1)] = block[
            share * piece : share * (piece + 1), :
        ]


def late_weights_kernel(share):
    def kernel(a4, s4, gh, gf, out):
        left = a4[...].T
        for at in range(0, FF, D):
            out[:, at : at + D] = dot(left, gh[:, at : at + D])
        for at in range(0, 1024, 256):
            by_share_store(out, FF, share, at, dot(s4[:, at : at + 256].T, gf[...]))

    return kernel


def turned(place, share, core, block):
    rows = block.T
    half = rows.shape[0] // 2
    for s in range(rows.shape[0] // share):
        side = core if s % 2 == 0 else 1 - core
        at = pl.multiple_of(side * half + s // 2 * share, 16)
        place[pl.ds(at, share), :] = rows[s * share : (s + 1) * share, :]


def turned_by_share(place, share, core, block, at_block):
    for at in range(0, D, 256):
        rows = block[:, at : at + 256].T
        for piece in range(256 // share):
            here = at + share * piece
            first, k = here // (4 * share), here % (4 * share) // share
            side = core if first % 2 == 0 else 1 - core
            to = side * (D // 2) + D * k + (at_block * (D // (8 * share)) + first // 2) * share
            place[pl.ds(pl.multiple_of(to, 16), share), :] = rows[share * piece : share * (piece + 1), :]


def weights_kernel(pairs, share, waits, cuts):
    has_small = pairs[-1] == (1, 0)

    def kernel(core_ref, *refs):
        count = len(pairs)
        lefts, rights = refs[:count], refs[count : 2 * count]
        lines = refs[2 * count : 2 * count + 6 * has_small]
        kept, *sents = refs[2 * count + 6 * has_small + waits :][: len(cuts)]
        places = refs[2 * count + 6 * has_small + waits + len(cuts) :]

        def send(change):
            for sent, low, high in zip(sents, cuts, cuts[1:]):
                pl.when((step >= low) & (step < high))(lambda sent=sent: change(sent))

        step = pl.program_id(0)
        core = core_ref[0]
        start = 0
        for (wide, long), left, right, place in zip(pairs, lefts, rights, places[:count]):
            steps = max(wide, long)

            if wide == 1:

                @pl.when(step == start)
                def _(left=left, place=place):
                    turned(place, share, core, left[...])

            else:

                @pl.when((step > start - wide) & (step <= start))
                def _(left=left, place=place, before=start - wide + 1):
                    turned_by_share(place, share, core, left, step - before)

            @pl.when((step >= start) & (step < start + steps))
            def _(right=right, place=place, wide=wide, start=start):
                if wide == 1:
                    rows = place[...]
                else:
                    rows = place[pl.ds(pl.multiple_of((step - start) * D, D), D), :]
                block = dot(rows, right[...])
                kept[...] = block[: D // 2, :]

                def put(sent):
                    sent[...] = block[D // 2 :, :]

                send(put)

            start += steps
        if has_small:

            @pl.when(step == start - 1)
            def _():
                stacked = jnp.concatenate([line[...] for line in lines] + [jnp.zeros((107, D), F32)], axis=0)
                places[-1][...] = stacked.T
                for s in range(D // share // 2):
                    for out, side in ((kept, core), (sents[-1], 1 - core)):
                        at = pl.multiple_of((2 * s + side) * share, 8)
                        out[s * share : (s + 1) * share, D - 128 :] = places[-1][pl.ds(at, share), :]

    return kernel


def weight_sums(pairs, share, core, small=None, after=(), pieces=1):
    tokens = pairs[0][0].shape[0]
    sizes = [(l.shape[1] // D, r.shape[1] // D) for l, r in pairs]
    if small is not None:
        sizes[-1] = (1, 0)
    lefts, rights, start = [], [], 0
    for (left, right), (wide, long) in zip(pairs, sizes):
        steps = max(wide, long)
        if wide == 1:
            lefts.append((left, "all"))
        else:
            index = lambda j, first=start - wide + 1, last=wide - 1: (0, jnp.clip(j - first, 0, last))
            lefts.append((left, pl.BlockSpec((tokens, D), index)))
        if wide == 1 and long > 1:
            index = lambda j, start=start, last=steps - 1: (0, jnp.clip(j - start, 0, last))
            rights.append((right, pl.BlockSpec((tokens, D), index)))
        else:
            rights.append((right, "all"))
        start += steps
    columns = start * D
    extra = [] if small is None else [(line, "all") for line in small]
    cuts = [start * i // pieces for i in range(pieces + 1)]

    def half(low, high):
        index = lambda j: (0, jnp.clip(j - low, 0, high - low - 1))
        return ((D // 2, D * (high - low)), F32, pl.BlockSpec((D // 2, D), index))

    kept, *sent, token = call(
        weights_kernel(sizes, share, len(after), cuts),
        (start,),
        [(core, scalars())] + lefts + rights + extra + [(a, anywhere()) for a in after],
        [half(0, start)] + [half(low, high) for low, high in zip(cuts, cuts[1:])],
        [pltpu.VMEM((D * wide, tokens), BF16) for wide, _ in sizes]
        + [pltpu.VMEM((D, 128), F32)] * (small is not None),
        2 * tokens * D * columns,
        "weights",
    )
    return kept, sent, token


def row_spec(shape):
    rest = len(shape) - 1
    return pl.BlockSpec((1,) + tuple(shape[1:]), lambda r: (r,) + (0,) * rest)


def whole_spec(shape):
    return pl.BlockSpec(tuple(shape), lambda r: (0,) * len(shape))


def held_spec(shape):
    return pl.BlockSpec(tuple(shape), lambda r: (0,) * len(shape), pipeline_mode=pl.Buffered(1))


def scalars():
    return pl.BlockSpec(memory_space=pltpu.SMEM)


def anywhere():
    return pl.BlockSpec(memory_space=pl.ANY)


ROOM = {'front': 44, 'mix': 24, 'lift': 28, 'depth': 20, 'late': 44, 'late_weights': 36, 'depth_grad': 20, 'conv_back': 28, 'mix_back': 28, 'mix_end': 24, 'front_back': 32, 'weights': 28}
HOP_COST = 30e9
TIMES = {'front': 40.0, 'mix': 14.0, 'lift': 18.0, 'depth': 12.0, 'late': 46.0, 'late_weights': 22.0, 'depth_grad': 26.0, 'conv_back': 4, 'mix_back': 24.0, 'mix_end': 4.0, 'front_back': 60, 'weights': 20.0}


def call(kernel, grid, ins, outs, scratch=(), flops=0, name=None):
    def placed(array, kind):
        if kind not in ("row", "all") and kind.memory_space is not None:
            return array
        return pltpu.with_memory_space_constraint(array, pltpu.HBM)

    def made(kind, shape):
        if kind == "row":
            return row_spec(shape)
        return whole_spec(shape) if kind == "all" else kind

    moved = sum(a.size * a.dtype.itemsize for a, _ in ins)
    inner = len(ins) + len(outs)

    def with_token(*refs):
        kernel(*refs[:inner], *refs[inner + 1 :])
        refs[inner][...] = jnp.zeros((8, 128), F32)

    *made_arrays, token = pl.pallas_call(
        with_token,
        grid=grid,
        in_specs=[held_spec(a.shape) if kind == "all" else made(kind, a.shape) for a, kind in ins],
        out_specs=[made(kind, shape) for shape, _, kind in outs] + [whole_spec((8, 128))],
        out_shape=[pltpu.HBM(shape, kind) for shape, kind, _ in outs] + [pltpu.HBM((8, 128), F32)],
        scratch_shapes=list(scratch),
        compiler_params=pltpu.CompilerParams(
            dimension_semantics=("arbitrary",), vmem_limit_bytes=ROOM[name] * 2**20
        ),
        cost_estimate=pl.CostEstimate(
            flops=int(TIMES[name] * 1.15e9), bytes_accessed=0, transcendentals=0
        ),
        name=name,
    )(*[placed(a, kind) for a, kind in ins])
    return (*made_arrays, token)


def flip_pairs(count, mask):
    return [(i, i ^ mask) for i in range(count)]


def hop_kernel(backward, first, keep_state, waits):
    def kernel(keep, second_ref, value, other, *refs):
        refs = refs[waits:]
        before, (out, out_before, token) = (None, refs) if first else (refs[0], refs[1:])
        token[...] = jnp.zeros((8, 128), F32)
        second = (second_ref[0] != 0) != backward
        rows = value.shape[0]
        decay_rows = slice(4 * STATE, 4 * STATE + 8)
        for r in range(rows):
            here, there = value[r, decay_rows, :], other[r, decay_rows, :]
            out[r, decay_rows, :] = here * there
            if first:
                entered = jnp.where(second, there, 1.0)
            else:
                entered = before[r, decay_rows, :]
                entered = jnp.where(second, entered * there, entered)
            out_before[r, decay_rows, :] = entered
            for a in range(4):
                at = slice(STATE * a, STATE * (a + 1))
                mine, others = value[r, at, :], other[r, at, :]
                mine_decay, other_decay = here[a : a + 1, :], there[a : a + 1, :]
                out[r, at, :] = jnp.where(
                    second, mine_decay * others + mine, other_decay * mine + others
                )
                if first:
                    entered = jnp.where(second, others, 0.0)
                else:
                    entered = before[r, at, :]
                    own = before[r, 4 * STATE + a : 4 * STATE + a + 1, :]
                    entered = jnp.where(second, own * others + entered, entered)
                out_before[r, at, :] = entered * keep[0, r] if keep_state else entered

    return kernel


def entering(value, backward, keep, meanwhile=lambda tokens: []):
    count, place = lax.axis_size("seq"), lax.axis_index("seq")
    vmem = pl.BlockSpec(memory_space=pltpu.VMEM)
    shape = jax.ShapeDtypeStruct(value.shape, F32)
    before, tokens = [], []
    for bit in range(count.bit_length() - 1):
        other = lax.ppermute(value, "seq", flip_pairs(count, 1 << bit))
        last = (2 << bit) == count
        after = meanwhile(tokens) if last else []
        value, entered, token = pl.pallas_call(
            hop_kernel(backward, bit == 0, last and not backward, len(after)),
            in_specs=[scalars()] * 2 + [vmem] * 2 + [anywhere()] * len(after) + [vmem] * len(before),
            out_specs=[vmem] * 3,
            out_shape=[shape, shape, jax.ShapeDtypeStruct((8, 128), F32)],
            compiler_params=pltpu.CompilerParams(vmem_limit_bytes=8 * 2**20),
            cost_estimate=pl.CostEstimate(
                flops=int(HOP_COST) if backward and bit == 1 else 0, bytes_accessed=0, transcendentals=0
            ),
            name="hop",
        )(keep, ((place >> bit) & 1).reshape(1), value, other, *after, *before)
        before = [entered]
        tokens.append(token)
    return before[0]


def halos(top, bottom):
    count = lax.axis_size("seq")
    ends = range(count - 1)
    return (
        lax.ppermute(bottom, "seq", [(i, i + 1) for i in ends]),
        lax.ppermute(top, "seq", [(i + 1, i) for i in ends]),
    )


def sum_over_all(value):
    count = lax.axis_size("seq") * lax.axis_size("rec")
    copies = jnp.broadcast_to(value[None], (count,) + value.shape)
    return jnp.sum(lax.all_to_all(copies, ("rec", "seq"), 0, 0), axis=0)


def scatter_sum(value):
    return lax.psum_scatter(value, "seq", scatter_dimension=0, tiled=True)


def in_vmem(kernel, scalars_in, ins, outs, after, name, cost=0):
    vmem = pl.BlockSpec(memory_space=pltpu.VMEM)
    return pl.pallas_call(
        kernel,
        in_specs=[scalars()] + [vmem] * len(ins) + [anywhere()] * len(after),
        out_specs=[vmem] * len(outs) + [vmem],
        out_shape=[jax.ShapeDtypeStruct(shape, F32) for shape in outs + [(8, 128)]],
        compiler_params=pltpu.CompilerParams(vmem_limit_bytes=8 * 2**20),
        cost_estimate=pl.CostEstimate(
            flops=int(cost * 1.15e9), bytes_accessed=0, transcendentals=0
        ),
        name=name,
    )(scalars_in, *ins, *after)


def part_rows(ref, group, chunk, side, columns):
    if chunk % 8:
        low = ref[2 * group * chunk : (2 * group + 1) * chunk, columns]
        high = ref[(2 * group + 1) * chunk : (2 * group + 2) * chunk, columns]
        return jnp.where(side == 0, low, high)
    return ref[pl.ds(pl.multiple_of((2 * group + side) * chunk, 8), chunk), columns]


def split_task(groups):
    arrays, outs, plan = [], [], []

    def known(array):
        for i, other in enumerate(arrays):
            if other is array:
                return i
        arrays.append(array)
        return len(arrays) - 1

    for items, chunk, bit in groups:
        rows = items[0][0].shape[0]
        placed, at = [], 0
        for kept, first, received, other_first, columns in items:
            there = None if received is None else known(received)
            placed.append((known(kept), first, there, other_first, columns, at))
            at += columns
        plan.append((placed, rows, chunk, bit, len(outs)))
        outs += [(rows // 2, at)] * 2

    def body(bit_ref, ins, made):
        for placed, rows, chunk, bit, out in plan:
            mine = bit_ref[bit]
            for kept, first, received, other_first, columns, at in placed:
                mine_at = slice(first, first + columns)
                other_at = slice(other_first, other_first + columns)
                for target, side in ((made[out], mine), (made[out + 1], 1 - mine)):
                    for group in range(rows // chunk // 2):
                        value = part_rows(ins[kept], group, chunk, side, mine_at)
                        if received is not None:
                            value = value + part_rows(ins[received], group, chunk, side, other_at)
                        target[group * chunk : (group + 1) * chunk, at : at + columns] = value

    return arrays, outs, body


def add_task(kept, received):
    def body(_, ins, made):
        made[0][...] = ins[0][...] + ins[1][...]

    return [kept, received], [kept.shape], body


def join_task(mine, other, bit, pieces=None):
    rows, columns = mine.shape
    cuts = [(0, columns, False)] if pieces is None else pieces
    outs = [(8 * rows, D) if spread else (2 * rows, wide) for _, wide, spread in cuts]

    def body(bit_ref, ins, made):
        first = bit_ref[bit] == 0
        for target, (at, wide, spread) in zip(made, cuts):
            for k in range(4 if spread else 1):
                width = D if spread else wide
                left = ins[0][:, at + D * k : at + D * k + width]
                right = ins[1][:, at + D * k : at + D * k + width]
                start = 2 * rows * k
                target[start : start + rows, :] = jnp.where(first, left, right)
                target[start + rows : start + 2 * rows, :] = jnp.where(first, right, left)

    return [mine, other], outs, body


def together(bits, sums, after, cost=0):
    tasks = [one.step() for one in sums]
    arrays = [array for ins, _, _, _ in tasks for array in ins]
    outs = [shape for _, shapes, _, _ in tasks for shape in shapes]
    count = len(arrays) + len(after)

    def kernel(bit_ref, *refs):
        at, out = 0, count
        for ins, shapes, body, _ in tasks:
            body(bit_ref, refs[at : at + len(ins)], refs[out : out + len(shapes)])
            at, out = at + len(ins), out + len(shapes)
        refs[-1][...] = jnp.zeros((8, 128), F32)

    *made, token = in_vmem(kernel, bits, arrays, outs, after, "together", cost)
    for _, shapes, _, commit in tasks:
        commit(made[: len(shapes)])
        made = made[len(shapes) :]
    return token


class Sum:
    def __init__(self, pieces):
        self.pieces = pieces
        self.chip_bits = lax.axis_size("seq").bit_length() - 2
        self.rec_bits = lax.axis_size("rec").bit_length() - 1
        self.parts, self.left, self.steps, self.beside = [], [], [], []
        self.done = None

    def swap(self, value, axis, bit):
        return lax.ppermute(value, axis, flip_pairs(lax.axis_size(axis), 1 << bit))

    def begin(self, kept, sent, first):
        self.parts = [[], []]
        at = 0
        for piece in sent:
            received = self.swap(piece, "seq", 0)
            end = at + piece.shape[1]
            for part, low, high in ((0, at, min(end, first)), (1, max(at, first), end)):
                if low < high:
                    self.parts[part].append((kept, low, received, low - at, high - low))
            at = end
        turn = 1 + self.chip_bits // 2
        orders = (
            list(range(1, self.chip_bits + 1)),
            list(range(turn, self.chip_bits + 1)) + list(range(1, turn)),
        )
        self.left = [list(range(self.chip_bits, 0, -1)) for _ in orders]
        self.steps += [("chips", now) for now in zip(*orders)]
        self.steps += [("rec", bit) for bit in range(self.rec_bits)] + [("turn", self.rec_bits - 1)]
        self.steps += [("join", bit) for bit in reversed(range(self.rec_bits))]

    def step(self):
        kind, now = self.steps.pop(0)
        if kind == "chips":
            groups = []
            for items, bit, left in zip(self.parts, now, self.left):
                chunk = items[0][0].shape[0] >> (left.index(bit) + 1)
                left.remove(bit)
                groups.append((items, chunk, bit))

            def commit(made):
                self.parts = [
                    [(made[2 * i], 0, self.swap(made[2 * i + 1], "seq", bit), 0, made[2 * i].shape[1])]
                    for i, bit in enumerate(now)
                ]

            return *split_task(groups), commit
        if kind == "rec":
            items = [item for part in self.beside + self.parts for item in part]
            self.beside = []

            def commit(made):
                kept, sent = made
                self.parts = [[(kept, 0, self.swap(sent, "rec", now), 0, kept.shape[1])]]

            chunk = items[0][0].shape[0] // 2
            return *split_task([(items, chunk, self.chip_bits + 1 + now)]), commit
        if kind == "turn":
            [[(kept, _, received, _, _)]] = self.parts

            def commit(made):
                [self.mine] = made
                self.other = self.swap(self.mine, "rec", now)

            return *add_task(kept, received), commit

        def commit(made):
            if now == 0:
                self.done = made
                return
            [self.mine] = made
            self.other = self.swap(self.mine, "rec", now - 1)

        pieces = self.pieces if now == 0 else None
        return *join_task(self.mine, self.other, self.chip_bits + 1 + now, pieces), commit


def local(
    features, time_keep, freq_keep, block_flags, decays, w_sub, ln1_gain, ffn1_in, ffn1_out, ln2_gain,
    ssm_in, ssm_out, ln3_gain, conv_in, conv_depth, bn_gain, bn_shift, conv_out, ln4_gain, ffn2_in,
    ffn2_out, ln5_gain, out_grad,
):
    rows, frame_count, mels = features.shape
    steps = frame_count // SUB
    tokens = rows * steps
    blocks = lax.axis_size("seq")
    place = lax.axis_index("seq")
    count = float(tokens * blocks * lax.axis_size("rec"))
    share = D // blocks
    here = lax.dynamic_index_in_dim(block_flags, place, 1, keepdims=False)
    after = lax.dynamic_index_in_dim(
        block_flags, jnp.minimum(place + 1, blocks - 1), 1, keepdims=False
    )
    keep_here = (1 - here).astype(F32)
    keep_next = jnp.where(place + 1 < blocks, 1 - after, 0).astype(F32)
    keep = (jnp.stack([keep_here, keep_next]), scalars())
    tk = (time_keep, "all")
    fk = (freq_keep, "all")
    g1, g2, g3, g4, g5, bg, bb = (
        (gain.reshape(1, D), "all")
        for gain in (ln1_gain, ln2_gain, ln3_gain, ln4_gain, ln5_gain, bn_gain, bn_shift)
    )
    taps = (jnp.pad(conv_depth.T, ((0, 1), (0, 0))), "all")

    def rows_of(width, kind=F32):
        return ((rows, steps, width), kind, "row")


    per_state = ((rows, 4 * STATE + 8, 128), F32, "row")
    edge = ((rows, 8, D), F32, "row")
    line = ((1, D), F32, "all")
    two_lines = ((2, D), F32, "all")
    padded = pltpu.VMEM((D // 128, steps + 16, 128), F32)
    full = pltpu.VMEM((256, D), BF16)

    def row(value):
        return (value, "row")

    def every(value):
        return (value, "all")

    (flat, x1, a1, r1, s1, d1, a2, r2, u, g, bs, c, ce, bt, se, ee, te, cum, cum_t, state, _) = call(
        front_kernel,
        (rows,),
        [
            row(features.transpose(0, 2, 1)), tk, fk, row(decays), keep,
            every(w_sub.T), g1, every(ffn1_in), every(ffn1_out), g2, every(ssm_in),
        ],
        [
            rows_of(WIDE, BF16), rows_of(D), rows_of(D, BF16), rows_of(1), rows_of(FF, BF16),
            rows_of(FF, BF16), rows_of(D, BF16), rows_of(1), rows_of(D, BF16), rows_of(D, BF16),
            rows_of(256, BF16), rows_of(256, BF16), rows_of(256, BF16), rows_of(256, BF16),
            rows_of(256, BF16), rows_of(256, BF16), rows_of(256, BF16), rows_of(HEADS),
            ((rows, HEADS, steps), F32, "row"), per_state,
        ],
        [pltpu.VMEM((frame_count, mels), F32)],
        2 * tokens * D * (WIDE + 2 * FF + PROJ),
        "front",
    )
    start = entering(state, False, keep[0])
    pair_shape = ((rows, HEADS, steps, steps), BF16, "row")
    mixed, pairs, decay_pairs, _ = call(
        mix_kernel,
        (rows,),
        [row(u), row(bs), row(c), row(cum), row(cum_t)],
        [rows_of(D, BF16), pair_shape, pair_shape],
        (),
        2 * tokens * 256 * 256 * 16,
        "mix",
    )
    z, gs, yd, x2, a3, r3, v, sq, cq, top, bottom, _ = call(
        lift_kernel,
        (rows,),
        [row(mixed), row(ce), row(start), row(g), row(x1), every(ssm_out), g3, every(conv_in)],
        [
            rows_of(D, BF16), rows_of(D, BF16), rows_of(D, BF16), rows_of(D), rows_of(D, BF16),
            rows_of(1), rows_of(D), rows_of(D, BF16), rows_of(D, BF16), edge, edge,
        ],
        [full],
        2 * tokens * D * 4 * D,
        "lift",
    )
    v_before, v_after = halos(top, bottom)
    dc, sums, _ = call(
        depth_kernel,
        (rows,),
        [row(v), row(v_before), row(v_after), keep, taps],
        [rows_of(D), two_lines],
        [padded],
        2 * tokens * D * 64,
        "depth",
    )
    stats = sum_over_all(sums)
    out, e, a4, s4, gf4, gh4, ge, gx3, gbn, back_sums, ln4, ln5, _ = call(
        late_kernel(count),
        (rows,),
        [
            row(dc), row(x2), row(out_grad), every(stats), bg, bb, every(conv_out), g4,
            every(ffn2_in), every(ffn2_out), g5,
        ],
        [
            rows_of(D, BF16), rows_of(D, BF16), rows_of(D, BF16), rows_of(FF, BF16), rows_of(D, BF16),
            rows_of(FF, BF16), rows_of(D, BF16), rows_of(D), rows_of(D, BF16), two_lines, line, line,
        ],
        [pltpu.VMEM((steps, FF), BF16)],
        2 * tokens * D * (4 * FF + 2 * D),
        "late",
    )
    back = sum_over_all(back_sums)

    def flatten(value):
        return value.reshape(tokens, value.shape[-1])

    def column_block(value, width):
        return (flatten(value), pl.BlockSpec((tokens, width), lambda i: (0, i)))

    def row_block(columns):
        return ((D, columns), F32, pl.BlockSpec((256, columns), lambda i: (i, 0)))

    late_grads, late_token = call(
        late_weights_kernel(share),
        (2,),
        [
            column_block(a4, 256), column_block(s4, 1024), every(flatten(gh4)), every(flatten(gf4)),
        ],
        [row_block(2 * FF)],
        (),
        2 * tokens * D * 2 * FF,
        "late_weights",
    )
    scattered_a = scatter_sum(late_grads)

    def edge_grad(at):
        return batch_back(
            lax.slice_in_dim(gbn, at, at + 8, axis=1).astype(F32),
            lax.slice_in_dim(dc, at, at + 8, axis=1),
            stats, back, bn_gain, count,
        )

    gd_before, gd_after = halos(edge_grad(0), edge_grad(steps - 8))
    gd, taps_grad, _ = call(
        depth_grad_kernel(count),
        (rows,),
        [
            row(gbn), row(dc), every(stats), every(back), bg, row(v), row(v_before), row(v_after), keep,
            (late_token, anywhere()),
        ],
        [rows_of(D, BF16), ((16, D), F32, "all")],
        [padded],
        2 * tokens * D * 64,
        "depth_grad",
    )
    gq, gx2, gz, gy, gg, pulled, ln3, _ = call(
        conv_back_kernel,
        (rows,),
        [
            row(gd), row(gd_before), row(gd_after), keep, taps, row(sq), row(cq), every(conv_in),
            row(a3), row(r3), g3, row(gx3), every(ssm_out), row(gs), row(yd), row(ce), row(state),
        ],
        [
            rows_of(2 * D, BF16), rows_of(D), rows_of(D, BF16), rows_of(D, BF16), rows_of(D, BF16),
            per_state, line,
        ],
        [padded],
        2 * tokens * D * 4 * D,
        "conv_back",
    )
    core = (place % 2).reshape(1)
    bits = jnp.stack(
        [(place >> k) & 1 for k in range(blocks.bit_length() - 1)]
        + [(lax.axis_index("rec") >> k) & 1 for k in range(lax.axis_size("rec").bit_length() - 1)]
    )
    early = Sum(
        [
            (0, FF, False), (FF, FF, True), (2 * FF, 2 * D, False), (2 * FF + 2 * D, D, False),
            (2 * FF + 3 * D, D, False),
        ],
    )
    found = {}

    def beside(hops):
        kept, sent, weights_token = weight_sums(
            [(flatten(a3), flatten(gq)), (flatten(z), flatten(gz)), (flatten(e), flatten(ge))], share, core, None, hops[-2:-1]
        )
        early.begin(kept, sent, 2 * D)
        token = together(bits, [early], [weights_token, hops[-1]])
        gu, gb, gc, mixed_token = call(
            mix_back_kernel,
            (rows,),
            [
                row(u), row(bs), row(c), row(ee), row(gy), row(start), row(pairs), row(decay_pairs),
                (token, anywhere()),
            ],
            [rows_of(D, BF16), rows_of(256, BF16), rows_of(256, BF16)],
            [full] + [pltpu.VMEM((4 * steps, 256), BF16)] * 4 + [pltpu.VMEM((steps, 4 * steps), BF16)],
            2 * tokens * 256 * 256 * 32,
            "mix_back",
        )
        found["mixed"] = (gu, gb, gc, mixed_token)
        return [mixed_token]

    end = entering(pulled, True, keep[0], beside)
    gu, gb, gc, mixed_token = found["mixed"]
    gp, gx1, gf1, ln2, end_token = call(
        mix_end_kernel,
        (rows,),
        [
            row(end), row(u), row(bt), row(te), row(se), row(gu), row(gb), row(gc), row(gg),
            every(ssm_in), row(a2), row(r2), g2, row(gx2), (mixed_token, anywhere()),
        ],
        [rows_of(PROJ, BF16), rows_of(D), rows_of(D, BF16), line],
        [full],
        2 * tokens * D * PROJ,
        "mix_end",
    )
    token = together(bits, [early], [end_token])
    kept, sent, weights_token = weight_sums(
        [(flatten(a2), flatten(gp)), (flatten(s1), flatten(gf1))], share, core, None, [token]
    )
    middle = Sum([(0, PROJ, False), (PROJ, FF, True)])
    middle.begin(kept, sent, (PROJ + FF) // 2)
    token = weights_token
    while early.steps[0][0] == "chips":
        token = together(bits, [early], [token])
    early.parts = [[(scattered_a, 0, None, 0, scattered_a.shape[1])]] + early.parts
    token = together(bits, [early], [token])
    gh1, gxr, features_grad, ln1, back_token = call(
        front_back_kernel,
        (rows,),
        [
            row(gx1), row(gf1), every(ffn1_out), row(d1), every(ffn1_in), row(a1), row(r1), g1,
            every(w_sub.T), tk, fk, (token, anywhere()),
        ],
        [rows_of(FF, BF16), rows_of(D, BF16), ((rows, mels, frame_count), F32, "row"), line],
        [pltpu.VMEM((frame_count, mels), F32)],
        2 * tokens * D * (WIDE + 2 * FF),
        "front_back",
    )
    small = [taps_grad, ln1, ln2, ln3, ln4, ln5]
    token = together(bits, [middle], [back_token])
    token = together(bits, [early], [token])
    last = Sum([(0, FF, False), (FF, SUB * mels, False), (FF + D - 128, 128, False)])
    kept, sent, weights_token = weight_sums(
        [(flatten(a1), flatten(gh1)), (flatten(gxr), flatten(flat))], share, core, small, [token], 1
    )
    last.begin(kept, sent, (FF + WIDE) // 2)
    token = weights_token
    token = together(bits, [early, middle], [token], 60.0)
    rounds = [(last,), (early, middle, last), (middle, last)]
    while early.steps or middle.steps or last.steps:
        now = rounds.pop(0) if rounds else (early, middle, last)
        now = [one for one in now if one.steps]
        if now:
            token = together(bits, now, [token])
    ffn2_in_grad, ffn2_out_grad, conv_in_grad, ssm_out_grad, conv_out_grad = early.done
    ssm_in_grad, ffn1_out_grad = middle.done
    ffn1_in_grad, w_sub_grad, gains = last.done

    start_row = place * share
    return (
        out,
        features_grad.transpose(0, 2, 1),
        w_sub_grad,
        gains[:, 16],
        ffn1_in_grad,
        ffn1_out_grad,
        gains[:, 17],
        ssm_in_grad,
        ssm_out_grad,
        gains[:, 18],
        conv_in_grad,
        gains[:, :KERNEL],
        lax.dynamic_slice_in_dim(back[0], start_row, share),
        lax.dynamic_slice_in_dim(back[1], start_row, share),
        conv_out_grad,
        gains[:, 19],
        ffn2_in_grad,
        ffn2_out_grad,
        gains[:, 20],
    )


def solution(mesh):
    block = P("rec", "seq", None)
    rows_of_seq, line = P("seq", None), P("seq")
    return jax.shard_map(
        local,
        mesh=mesh,
        in_specs=(block, P("rec", "seq"), P("rec", None), P("rec", None), P("rec", None, "seq"))
        + (P(),) * 17
        + (block,),
        out_specs=(
            block, block, rows_of_seq, line, rows_of_seq, rows_of_seq, line, rows_of_seq, rows_of_seq,
            line, rows_of_seq, rows_of_seq, line, line, rows_of_seq, line, rows_of_seq, rows_of_seq, line,
        ),
        check_vma=False,
    )
```
